32 devices in a mesh: dp: 8 (over z, core), tensor: 4 (over y, x).
Axes of the slice: x: 2, y: 2, z: 4, core: 2. Of those that a mesh axis runs over, the one named last changes fastest.
Arguments:
- tokens_in: bfloat16 [8192, 1024], P('dp'), may hold values from -6 to 6
- norm_params: float32 [4, 1024], replicated, may hold values from -1.2 to 3.6
- query_key_value_weight: bfloat16 [3, 1024, 1024], P(None, None, 'tensor'), may hold values from -0.09375 to 0.09375
- out_weight: bfloat16 [1024, 1024], P('tensor'), may hold values from -1.5 to 1.5
- fc_weight: bfloat16 [1024, 4096], P(None, 'tensor'), may hold values from -0.1875 to 0.1875
- proj_weight: bfloat16 [4096, 1024], P('tensor'), may hold values from -0.09375 to 0.09375
- factors: float32 [4, 4, 1024], replicated, may hold values from -0.12 to 0.12
- first_moment: float32 [4, 4, 1024], replicated, may hold values from -0.375 to 0.375
- second_moment: float32 [4, 4, 1024], replicated, may hold values from 0.015625 to 0.0625
- grad_out: bfloat16 [8192, 1024], P('dp'), may hold values from -6 to 6
Outputs:
- block_out: bfloat16 [8192, 1024], P(('dp', 'tensor'))
- input_grad: float32 [8192, 1024], P(('dp', 'tensor'))
- clipped_grad: float32 [4, 4, 1024], replicated
- grad_norm: float32 [], replicated
- factors_new: float32 [4, 4, 1024], replicated
- first_new: float32 [4, 4, 1024], replicated
- second_new: float32 [4, 4, 1024], replicated
The draws below stay inside these ranges and needn't reach their ends.
All inputs are finite; a program needn't handle non-finite values.
Results may differ from the reference program's by a relative error of at most 0.015.
Values may be sent and summed in bfloat16 or wider, within the bound.
A program may use at most 128 MiB of HBM per device.

```python
import math
import jax
import jax.numpy as jnp
from jax import lax

D = 1024
HEADS = 16
HD = 64
FF = 4096
R = 4
SEQ = 1024
STEP = 5
DOCS = 8
TOKENS = 8192


CLIP_NORM = 16.0


def draw_norm_params(key, part):
    key = jax.random.fold_in(key, 11)
    subkeys = jax.random.split(key, 4)
    rising = 1.0 + 2.0 * jnp.arange(D, dtype=jnp.float32) / (D - 1)
    gain_first = rising * jax.random.uniform(subkeys[0], (D,), jnp.float32, 0.8, 1.2)
    bias_first = 0.3 * jnp.clip(jax.random.normal(subkeys[1], (D,), jnp.float32), -4.0, 4.0)
    gain_second = jax.random.uniform(subkeys[2], (D,), jnp.float32, 0.7, 1.3)
    bias_second = 0.3 * jnp.clip(jax.random.normal(subkeys[3], (D,), jnp.float32), -4.0, 4.0)
    return jnp.stack((gain_first, bias_first, gain_second, bias_second))


def draw_factors(key, part):
    key = jax.random.fold_in(key, 12)
    sample = jnp.clip(jax.random.normal(key, (4, R, D), jnp.float32), -4.0, 4.0)
    down_scale = 0.5 * D ** (-0.5)
    scales = jnp.array([down_scale, 0.03, down_scale, 0.03], jnp.float32)
    return sample * scales[:, None, None]


def draw_first_moment(key, part):
    key = jax.random.fold_in(key, 13)
    typical = CLIP_NORM * (4 * R * D) ** (-0.5)
    sample = jnp.clip(jax.random.normal(key, (4, R, D), jnp.float32), -3.0, 3.0)
    return sample * typical


def draw_second_moment(key, part):
    key = jax.random.fold_in(key, 14)
    typical = CLIP_NORM * CLIP_NORM / (4 * R * D)
    factor = jnp.exp(jax.random.uniform(key, (4, R, D), jnp.float32, math.log(0.5), math.log(2.0)))
    return 2.0 * typical * factor


def levels(rng, dims, pieces, low, high):
    factor_of, own = 1.0, jax.random.fold_in(rng, 6)
    for position, parts in pieces:
        draws = jnp.exp(jax.random.uniform(jax.random.fold_in(own, position), (parts,), jnp.float32, low / len(pieces), high / len(pieces)))
        factor_of = factor_of * jnp.repeat(draws, dims[position] // parts).reshape([-1 if axis == position else 1 for axis in range(len(dims))])
    return factor_of


def normal_values(rng, extent, deviation, limit, cuts=(), kind=jnp.bfloat16):
    gain = levels(rng, extent, cuts, -0.22, 0.18) if cuts else 1.0
    drawn = jax.random.normal(rng, extent, jnp.float32) * deviation * gain
    return jnp.minimum(jnp.maximum(drawn, -limit), limit).astype(kind)


def setup_inputs(seed: int = 0) -> dict:
    arg_keys = jax.random.split(jax.random.key(seed), 11)
    tokens_in = normal_values(arg_keys[0], (TOKENS, D), 1.0, 6.0, ((0, 8),))
    norm_params = draw_norm_params(jax.random.fold_in(arg_keys[10], 71), 0)
    query_key_value_weight = normal_values(arg_keys[2], (3, D, D), (4 * D) ** -0.5, 0.09375, ((2, 4),))
    out_weight = normal_values(arg_keys[3], (D, D), (D // 64) ** -0.5, 1.5, ((0, 4),))
    fc_weight = normal_values(arg_keys[4], (D, FF), D ** -0.5, 0.1875, ((1, 4),))
    proj_weight = normal_values(arg_keys[5], (FF, D), FF ** -0.5, 0.09375, ((0, 4),))
    factors = draw_factors(jax.random.fold_in(arg_keys[10], 71), 0)
    first_moment = draw_first_moment(jax.random.fold_in(arg_keys[10], 71), 0)
    second_moment = draw_second_moment(jax.random.fold_in(arg_keys[10], 71), 0)
    grad_out = normal_values(arg_keys[9], (TOKENS, D), 1.0, 6.0, ((0, 8),))
    return dict(tokens_in=tokens_in, norm_params=norm_params, query_key_value_weight=query_key_value_weight, out_weight=out_weight, fc_weight=fc_weight, proj_weight=proj_weight, factors=factors, first_moment=first_moment, second_moment=second_moment, grad_out=grad_out)


EPSILON = 1e-05
ADAPTER_SCALING = 8.0
CLIP_NORM = 16.0
LEARN_RATE = 0.03
BETA_ONE = 0.5
BETA_TWO = 0.5
WEIGHT_DECAY = 0.01
ADAM_EPSILON = 1e-08
NEG_LARGE = -1e+30

@jax.custom_vjp
def lowered_precision(v):
    return lax.optimization_barrier(v.astype(jnp.bfloat16)).astype(jnp.float32)

@jax.custom_vjp
def lowered_backward(v):
    return v

def low_keep(v):
    return (lowered_precision(v), None)

def low_pass(kept, grad):
    return (grad,)

def back_keep(v):
    return (v, None)

def back_low(kept, grad):
    return (lowered_precision(grad),)
lowered_precision.defvjp(low_keep, low_pass)
lowered_backward.defvjp(back_keep, back_low)

def precise_product(left, right):
    return jnp.dot(left, right, precision=lax.Precision.HIGHEST)

def layer_norm(value_rows_local, gain_vec, bias_vec):
    centered = value_rows_local - lax.optimization_barrier(jnp.mean(value_rows_local, -1, keepdims=True))
    variance = lax.optimization_barrier(jnp.mean(centered * centered, -1, keepdims=True))
    return centered * lax.rsqrt(variance + EPSILON) * gain_vec + bias_vec

def attend(inputs):
    query_doc, key_doc, value_doc = inputs
    raw_scores = lowered_backward(jnp.einsum('qhd,khd->hqk', query_doc, key_doc, precision=lax.Precision.HIGHEST))
    scores = raw_scores * 0.125
    positions = jnp.arange(SEQ)
    scores = jnp.where(positions[None, :, None] >= positions[None, None, :], scores, NEG_LARGE)
    probability = jax.nn.softmax(scores, axis=-1)
    mixture = jnp.einsum('hqk,khd->qhd', lowered_precision(probability), value_doc, precision=lax.Precision.HIGHEST)
    return lowered_backward(lowered_precision(mixture))

def forward(inputs, adapters, norm_params, query_key_value_gathered, out_full, fc_full, proj_full):
    factors_reduced_precision = lowered_precision(adapters)
    first_normalized = lowered_precision(layer_norm(inputs, norm_params[0], norm_params[1]))
    query_down_factor = lowered_precision(precise_product(first_normalized, factors_reduced_precision[0].T))
    value_down_factor = lowered_precision(precise_product(first_normalized, factors_reduced_precision[2].T))
    query_rows_local = lowered_backward(lowered_precision(precise_product(first_normalized, query_key_value_gathered[0]) + ADAPTER_SCALING * precise_product(query_down_factor, factors_reduced_precision[1])))
    keys = lowered_backward(lowered_precision(precise_product(first_normalized, query_key_value_gathered[1])))
    value_rows_local = lowered_backward(lowered_precision(precise_product(first_normalized, query_key_value_gathered[2]) + ADAPTER_SCALING * precise_product(value_down_factor, factors_reduced_precision[3])))
    head_shape = (DOCS, SEQ, HEADS, HD)
    mixture = lax.map(jax.checkpoint(attend), (query_rows_local.reshape(head_shape), keys.reshape(head_shape), value_rows_local.reshape(head_shape)))
    attn_out = lowered_backward(precise_product(mixture.reshape(TOKENS, D), out_full))
    residual = inputs + attn_out
    normed_two = lowered_precision(layer_norm(residual, norm_params[2], norm_params[3]))
    hidden_pre = lowered_backward(precise_product(normed_two, fc_full))
    hidden_act = lowered_precision(jax.nn.gelu(hidden_pre, approximate=True))
    mlp_out = lowered_backward(precise_product(hidden_act, proj_full))
    return residual + mlp_out

def reference(tokens_in, norm_params, query_key_value_weight, out_weight, fc_weight, proj_weight, factors, first_moment, second_moment, grad_out):
    inputs_f = tokens_in.astype(jnp.float32)
    query_key_value_gathered = query_key_value_weight.astype(jnp.float32)
    out_full = out_weight.astype(jnp.float32)
    fc_full = fc_weight.astype(jnp.float32)
    proj_full = proj_weight.astype(jnp.float32)

    def layer(inputs, adapters):
        return forward(inputs, adapters, norm_params, query_key_value_gathered, out_full, fc_full, proj_full)
    block_out, pullback = jax.vjp(layer, inputs_f, factors)
    input_grad, factor_grad = pullback(grad_out.astype(jnp.float32))
    grad_norm = jnp.sqrt(jnp.sum(factor_grad * factor_grad))
    clipped = factor_grad * (CLIP_NORM / jnp.maximum(grad_norm, CLIP_NORM))
    first_new = BETA_ONE * first_moment + (1.0 - BETA_ONE) * clipped
    second_new = BETA_TWO * second_moment + (1.0 - BETA_TWO) * clipped * clipped
    first_hat = first_new / (1.0 - BETA_ONE ** STEP)
    second_hat = second_new / (1.0 - BETA_TWO ** STEP)
    factors_new = factors - LEARN_RATE * (first_hat / (jnp.sqrt(second_hat) + ADAM_EPSILON) + WEIGHT_DECAY * factors)
    return (block_out.astype(jnp.bfloat16), input_grad, clipped, grad_norm, factors_new, first_new, second_new)
```

```python
import functools

import jax
import jax.numpy as jnp
from jax import lax
from jax.experimental import pallas as pl
from jax.experimental.pallas import tpu as pltpu
from jax.sharding import PartitionSpec as P

HD = 64
SEQ = 1024
STEP = 5


EPSILON = 1e-05
ADAPTER_SCALING = 8.0
CLIP_NORM = 16.0
LEARN_RATE = 0.03
BETA_ONE = 0.5
BETA_TWO = 0.5
WEIGHT_DECAY = 0.01
ADAM_EPSILON = 1e-08
NEG_LARGE = -1e30
GELU_SCALE = 0.7978845608028654
GELU_CUBE = 0.044715


def matrix_product(left, right):
    return jnp.dot(left, right, preferred_element_type=jnp.float32)


def product_with_transpose(left, right):
    return lax.dot_general(
        left, right, (((1,), (1,)), ((), ())), preferred_element_type=jnp.float32
    )


def transpose_then_product(left, right):
    return lax.dot_general(
        left, right, (((0,), (0,)), ((), ())), preferred_element_type=jnp.float32
    )


def normalize(value_rows_local, gain_vec, bias_vec):
    centered = value_rows_local - jnp.mean(value_rows_local, -1, keepdims=True)
    inverse = lax.rsqrt(jnp.mean(centered * centered, -1, keepdims=True) + EPSILON)
    unit_rows = centered * inverse
    return (unit_rows * gain_vec + bias_vec, unit_rows, inverse)


def normalize_back(incoming, unit_rows, inverse, gain_vec):
    scaled = incoming * gain_vec
    return inverse * (
        scaled
        - jnp.mean(scaled, -1, keepdims=True)
        - unit_rows * jnp.mean(scaled * unit_rows, -1, keepdims=True)
    )


def causal_scores(query_block, key_all, block_index, block_len):
    scores = (
        jnp.einsum("bqhd,bkhd->bhqk", query_block, key_all, preferred_element_type=jnp.float32)
        * 0.125
    )
    query_pos = block_index * block_len + jnp.arange(block_len)
    allowed = jnp.arange(SEQ)[None, :] <= query_pos[:, None]
    return jnp.where(allowed, scores, NEG_LARGE)


def attention_forward(query_rows_local, key_all, value_all):
    block_len = min(512, SEQ)
    outputs = []
    logsums = []
    for block_index in range(SEQ // block_len):
        query_block = query_rows_local[:, block_index * block_len : (block_index + 1) * block_len]
        scores = causal_scores(query_block, key_all, block_index, block_len)
        row_max = jnp.max(scores, -1, keepdims=True)
        exponent = jnp.exp(scores - row_max)
        row_total = jnp.sum(exponent, -1, keepdims=True)
        probability = (exponent / row_total).astype(jnp.bfloat16)
        mixture = jnp.einsum(
            "bhqk,bkhd->bqhd", probability, value_all, preferred_element_type=jnp.float32
        )
        outputs.append(mixture.astype(jnp.bfloat16))
        logsums.append(row_max[..., 0] + jnp.log(row_total[..., 0]))
    return (jnp.concatenate(outputs, 1), jnp.concatenate(logsums, 2))


def attention_backward(query_rows_local, key_all, value_all, grad_mixture, logsums):
    block_len = min(512, SEQ)
    grad_queries = []
    grad_keys = jnp.zeros(key_all.shape, jnp.float32)
    value_gradient_rows = jnp.zeros(value_all.shape, jnp.float32)
    for block_index in range(SEQ // block_len):
        lower = block_index * block_len
        query_block = query_rows_local[:, lower : lower + block_len]
        grad_block = grad_mixture[:, lower : lower + block_len]
        scores = causal_scores(query_block, key_all, block_index, block_len)
        probability = jnp.exp(scores - logsums[:, :, lower : lower + block_len, None])
        grad_prob = jnp.einsum(
            "bqhd,bkhd->bhqk", grad_block, value_all, preferred_element_type=jnp.float32
        )
        row_delta = jnp.sum(grad_prob * probability, -1, keepdims=True)
        dscore = (0.125 * (probability * (grad_prob - row_delta))).astype(jnp.bfloat16)
        grad_queries.append(
            jnp.einsum(
                "bhqk,bkhd->bqhd", dscore, key_all, preferred_element_type=jnp.float32
            ).astype(jnp.bfloat16)
        )
        grad_keys = grad_keys + jnp.einsum(
            "bhqk,bqhd->bkhd", dscore, query_block, preferred_element_type=jnp.float32
        )
        value_gradient_rows = value_gradient_rows + jnp.einsum(
            "bhqk,bqhd->bkhd",
            probability.astype(jnp.bfloat16),
            grad_block,
            preferred_element_type=jnp.float32,
        )
    return (
        jnp.concatenate(grad_queries, 1),
        grad_keys.astype(jnp.bfloat16),
        value_gradient_rows.astype(jnp.bfloat16),
    )


def adam_step(factor_grad, weights, first_old, second_old, grad_norm):
    clipped = factor_grad * (CLIP_NORM / jnp.maximum(grad_norm, CLIP_NORM))
    first_new = BETA_ONE * first_old + (1.0 - BETA_ONE) * clipped
    second_new = BETA_TWO * second_old + (1.0 - BETA_TWO) * clipped * clipped
    first_hat = first_new / (1.0 - BETA_ONE**STEP)
    second_hat = second_new / (1.0 - BETA_TWO**STEP)
    weights_new = weights - LEARN_RATE * (
        first_hat / (jnp.sqrt(second_hat) + ADAM_EPSILON) + WEIGHT_DECAY * weights
    )
    return (clipped, weights_new, first_new, second_new)


def body(
    tokens_in,
    norm_params,
    query_key_value_weight,
    out_weight,
    fc_weight,
    proj_weight,
    factors,
    first_moment,
    second_moment,
    grad_out,
):
    tensor_size = lax.axis_size("tensor")
    tensor_rank = lax.axis_index("tensor")
    token_count = tokens_in.shape[0]
    doc_count = token_count // SEQ
    local_width = query_key_value_weight.shape[2]
    heads_here = local_width // HD
    row_count = token_count // tensor_size
    row_start = tensor_rank * row_count
    rank_count = factors.shape[1]
    full_width = factors.shape[2]
    inputs = tokens_in.astype(jnp.float32)
    first_normalized, unit_one, inverse_one = normalize(inputs, norm_params[0], norm_params[1])
    first_normalized_reduced = first_normalized.astype(jnp.bfloat16)
    factor_reduced_precision = factors.astype(jnp.bfloat16)
    column_offset = tensor_rank * local_width
    query_adapter_output = lax.dynamic_slice_in_dim(
        factor_reduced_precision[1], column_offset, local_width, 1
    )
    value_adapter_output = lax.dynamic_slice_in_dim(
        factor_reduced_precision[3], column_offset, local_width, 1
    )
    query_down_factor = product_with_transpose(
        first_normalized_reduced, factor_reduced_precision[0]
    ).astype(jnp.bfloat16)
    value_down_factor = product_with_transpose(
        first_normalized_reduced, factor_reduced_precision[2]
    ).astype(jnp.bfloat16)
    query_rows_local = (
        matrix_product(first_normalized_reduced, query_key_value_weight[0])
        + ADAPTER_SCALING * matrix_product(query_down_factor, query_adapter_output)
    ).astype(jnp.bfloat16)
    keys_low = matrix_product(first_normalized_reduced, query_key_value_weight[1]).astype(
        jnp.bfloat16
    )
    values_low = (
        matrix_product(first_normalized_reduced, query_key_value_weight[2])
        + ADAPTER_SCALING * matrix_product(value_down_factor, value_adapter_output)
    ).astype(jnp.bfloat16)
    head_shape = (doc_count, SEQ, heads_here, HD)
    query_heads = query_rows_local.reshape(head_shape)
    keys_heads = keys_low.reshape(head_shape)
    values_heads = values_low.reshape(head_shape)
    mixture, logsums = attention_forward(query_heads, keys_heads, values_heads)
    attn_part = matrix_product(mixture.reshape(token_count, local_width), out_weight)
    grad_full = grad_out.astype(jnp.float32)
    attn_rows = lax.psum_scatter(
        attn_part.astype(jnp.bfloat16), "tensor", scatter_dimension=0, tiled=True
    ).astype(jnp.float32)
    resid_rows = lax.dynamic_slice_in_dim(inputs, row_start, row_count, 0) + attn_rows
    normed_two_rows, unit_two, inverse_two = normalize(resid_rows, norm_params[2], norm_params[3])
    normed_two_low = lax.all_gather(
        normed_two_rows.astype(jnp.bfloat16), "tensor", axis=0, tiled=True
    )
    hidden_pre = matrix_product(normed_two_low, fc_weight)
    hidden_act, gelu_pull = jax.vjp(
        lambda argument: jax.nn.gelu(argument, approximate=True), hidden_pre
    )
    mlp_part = matrix_product(hidden_act.astype(jnp.bfloat16), proj_weight)
    grad_hidden = product_with_transpose(grad_out, proj_weight)
    grad_pre = gelu_pull(grad_hidden)[0].astype(jnp.bfloat16)
    second_part = product_with_transpose(grad_pre, fc_weight)
    out_rows = resid_rows + lax.psum_scatter(
        mlp_part.astype(jnp.bfloat16), "tensor", scatter_dimension=0, tiled=True
    ).astype(jnp.float32)
    second_rows = lax.psum_scatter(
        second_part.astype(jnp.bfloat16), "tensor", scatter_dimension=0, tiled=True
    ).astype(jnp.float32)
    resid_grad_rows = lax.dynamic_slice_in_dim(grad_full, row_start, row_count, 0) + normalize_back(
        second_rows, unit_two, inverse_two, norm_params[2]
    )
    resid_grad_low = lax.all_gather(
        resid_grad_rows.astype(jnp.bfloat16), "tensor", axis=0, tiled=True
    )
    grad_mixture = product_with_transpose(resid_grad_low, out_weight).astype(jnp.bfloat16)
    query_gradient, grad_keys, value_gradient_rows = attention_backward(
        query_heads, keys_heads, values_heads, grad_mixture.reshape(head_shape), logsums
    )
    query_gradient = query_gradient.reshape(token_count, local_width)
    grad_keys = grad_keys.reshape(token_count, local_width)
    value_gradient_rows = value_gradient_rows.reshape(token_count, local_width)
    stacked = jnp.stack((query_gradient, grad_keys, value_gradient_rows))
    first_part = jnp.einsum(
        "stc,sdc->td", stacked, query_key_value_weight, preferred_element_type=jnp.float32
    )
    query_up_factor = ADAPTER_SCALING * product_with_transpose(query_gradient, query_adapter_output)
    value_up_factor = ADAPTER_SCALING * product_with_transpose(
        value_gradient_rows, value_adapter_output
    )
    first_part = first_part + jnp.dot(
        query_up_factor,
        factor_reduced_precision[0].astype(jnp.float32),
        precision=lax.Precision.HIGHEST,
    )
    first_part = first_part + jnp.dot(
        value_up_factor,
        factor_reduced_precision[2].astype(jnp.float32),
        precision=lax.Precision.HIGHEST,
    )
    first_rows = lax.psum_scatter(
        first_part.astype(jnp.bfloat16), "tensor", scatter_dimension=0, tiled=True
    ).astype(jnp.float32)
    unit_rows = lax.dynamic_slice_in_dim(unit_one, row_start, row_count, 0)
    inverse_rows = lax.dynamic_slice_in_dim(inverse_one, row_start, row_count, 0)
    input_rows = resid_grad_rows + normalize_back(
        first_rows, unit_rows, inverse_rows, norm_params[0]
    )
    query_cross_term = transpose_then_product(query_gradient, first_normalized_reduced)
    value_cross_term = transpose_then_product(value_gradient_rows, first_normalized_reduced)
    query_down_gradient = ADAPTER_SCALING * jnp.dot(
        query_adapter_output.astype(jnp.float32), query_cross_term, precision=lax.Precision.HIGHEST
    )
    value_down_gradient = ADAPTER_SCALING * jnp.dot(
        value_adapter_output.astype(jnp.float32), value_cross_term, precision=lax.Precision.HIGHEST
    )
    empty_slot = jnp.zeros((rank_count, full_width), jnp.float32)
    up_grad_query = lax.dynamic_update_slice_in_dim(
        empty_slot,
        ADAPTER_SCALING * transpose_then_product(query_down_factor, query_gradient),
        column_offset,
        1,
    )
    up_grad_value = lax.dynamic_update_slice_in_dim(
        empty_slot,
        ADAPTER_SCALING * transpose_then_product(value_down_factor, value_gradient_rows),
        column_offset,
        1,
    )
    partial_grad = jnp.stack(
        (query_down_gradient, up_grad_query, value_down_gradient, up_grad_value)
    )
    reduced = lax.psum(partial_grad, ("dp", "tensor"))
    grad_norm = jnp.sqrt(jnp.sum(reduced * reduced))
    clipped, weights_new, first_new, second_new = adam_step(
        reduced, factors, first_moment, second_moment, grad_norm
    )
    return (
        out_rows.astype(jnp.bfloat16),
        input_rows,
        clipped,
        grad_norm,
        weights_new,
        first_new,
        second_new,
    )


MESH = pl.DeviceIdType.MESH
BF = jnp.bfloat16
F32 = jnp.float32
GROUPS = 24
ATTN_GROUPS = 8


def mm(left, right):
    return jnp.dot(left, right, preferred_element_type=F32)


def mm_nt(left, right):
    return lax.dot_general(left, right, (((1,), (1,)), ((), ())), preferred_element_type=F32)


def mm_tn(left, right):
    return lax.dot_general(left, right, (((0,), (0,)), ((), ())), preferred_element_type=F32)


def flip(value, bit):
    return value + bit - 2 * bit * ((value // bit) % 2)


def unit_of(rows):
    centered = rows - jnp.mean(rows, -1, keepdims=True)
    inverse = lax.rsqrt(jnp.mean(centered * centered, -1, keepdims=True) + EPSILON)
    return centered * inverse, inverse


def fused_kernel(
    planes,
    tokens, norm_params, wqkv, w_out, w_fc, w_proj, factors, first_moment, second_moment, grad_out,
    block_out, input_grad, clipped, grad_norm, factors_new, first_new, second_new,
    tok, n1, go, wa, wo, fcw, pw, k_all, v_all, qs, p0, p1, p2, p3, mix, attn, attn_s, attn_r,
    res, n2, mlp_acc, gnt_acc, mlp_s, mlp_r, gnt_s, gnt_r, gr_b, bo_s, bo_r, grf,
    dk_acc, dv_acc, gq_scr, dos, gno_scr, gno_s, gno_r, chip_s, fin_r, tokr,
    fpad, f02, f1p, f3p, down, gd_scr, fg_a, fg_b, ps, ps_r, plane_buf, z_buf, fin,
    chain_send, chain_recv, load_sem, ssem, rsem,
):
    d = lax.axis_index("dp")
    t = lax.axis_index("tensor")
    z, c, x, y = d // 2, d % 2, t % 2, t // 2
    odd = z % 2
    nbr = (flip(d, 1), t)
    prim = (d, flip(t, 1 + odd))
    sec = (d, flip(t, 2 - odd))
    zn = (flip(d, 2), t)
    plane = [(d, flip(t, 1)), (d, flip(t, 2)), (d, 3 - t)]
    zs = [(2 * ((z + k) % planes) + c, t) for k in range(1, planes)]
    cross = [(flip(d, 1), flip(t, 2)), (flip(d, 1), 3 - t)]
    dests = [(2 * z + y, 2 * c + j) for j in range(2)]
    same = [jnp.logical_and(c == y, x == j) for j in range(2)]
    quarter = [t, flip(t, 1 + odd), flip(t, 2 - odd), 3 - t]
    column = [pl.multiple_of(q * 256 + c * 128, 128) for q in quarter]
    block = [2 * i + (i + x) % 2 for i in range(4)]
    block_row = [pl.multiple_of(b * 128, 128) for b in block]
    own = pl.multiple_of(c * 256, 256)
    other = pl.multiple_of(256 - c * 256, 256)
    p_refs = (p0, p1, p2, p3)

    def remote(src, dst, send, recv, device):
        return pltpu.make_async_remote_copy(
            src_ref=src, dst_ref=dst, send_sem=send, recv_sem=recv, device_id=device, device_id_type=MESH
        )

    def to_nbr(src, dst, index):
        return remote(src, dst, ssem.at[index], rsem.at[index], nbr)

    lane = pl.ds(pl.multiple_of(c * 128, 128), 128)
    loads = [
        pltpu.make_async_copy(wqkv.at[m, :, lane], wa.at[m, :, pl.ds(0, 128)], load_sem.at[m])
        for m in range(3)
    ]
    loads.append(pltpu.make_async_copy(w_out.at[lane, :], wo.at[pl.ds(0, 128), :], load_sem.at[3]))
    for h in range(2):
        hidden = pl.ds(pl.multiple_of(c * 512 + h * 256, 256), 256)
        loads.append(pltpu.make_async_copy(w_fc.at[:, hidden], fcw.at[0, h], load_sem.at[4 + 2 * h]))
        loads.append(pltpu.make_async_copy(w_proj.at[hidden, :], pw.at[0, h], load_sem.at[5 + 2 * h]))
    for load in loads:
        load.start()
    own_rows = pltpu.make_async_copy(
        tokens.at[pl.ds(pl.multiple_of(t * 256, 256), 256), :], tokr, load_sem.at[8]
    )
    own_rows.start()

    barrier = pltpu.get_barrier_semaphore()
    partners = [nbr] + plane + zs + cross
    for device in partners:
        pl.semaphore_signal(barrier, inc=1, device_id=device, device_id_type=MESH)
    pl.semaphore_wait(barrier, len(partners))

    doc = [
        (tokens.at[pl.ds(256 * r, 256), :], tok.at[pl.ds(256 * r, 256), :], r) for r in range(4)
    ] + [
        (grad_out.at[pl.ds(block_row[i], 128), :], go.at[pl.ds(128 * i, 128), :], 4 + i) for i in range(4)
    ]

    @pl.when(c == y)
    def _():
        for src, dst, index in doc:
            to_nbr(src, dst, index).start()
            pltpu.make_async_copy(src, dst, rsem.at[index]).start()

    def doc_wait(index):
        to_nbr(*doc[index]).wait_recv()

    def piece(slot, group):
        if group < ATTN_GROUPS:
            m, a = group // 2, group % 2
            if m < 3:
                return wa.at[m, pl.ds(512 * a, 512), pl.ds(128 * slot, 128)]
            return wo.at[pl.ds(128 * slot + 64 * a, 64), :]
        h, r = (group - ATTN_GROUPS) // 8, (group - ATTN_GROUPS) % 8
        if r < 4:
            return fcw.at[slot, h, pl.ds(256 * r, 256), :]
        return pw.at[slot, h, pl.ds(64 * (r - 4), 64), :]

    def hop(slot, group):
        return remote(
            piece(1 if slot > 1 else 0, group),
            piece(slot, group),
            chain_send.at[slot - 1, group],
            chain_recv.at[slot - 1, group],
            (prim, zn, sec)[slot - 1],
        )

    for load in loads:
        load.wait()
    for group in range(GROUPS):
        hop(1, group).start()

    def pump(group):
        hop(1, group).wait_recv()
        hop(2, group).start()
        hop(3, group).start()

    fpad[...] = jnp.zeros_like(fpad)
    fpad[0:4, :] = factors[0]
    fpad[4:8, :] = factors[2]
    f02[...] = fpad[...].astype(BF)
    fpad[...] = jnp.zeros_like(fpad)
    for s in range(4):
        fpad[0:4, 128 * s : 128 * s + 128] = factors[1, :, pl.ds(column[s], 128)]
        fpad[4:8, 512 + 128 * s : 640 + 128 * s] = factors[3, :, pl.ds(column[s], 128)]
    f1p[...] = fpad[:, :512].astype(BF)
    f3p[...] = fpad[:, 512:].astype(BF)
    attn[...] = jnp.zeros_like(attn)
    mlp_acc[...] = jnp.zeros_like(mlp_acc)
    gnt_acc[...] = jnp.zeros_like(gnt_acc)
    dk_acc[...] = jnp.zeros_like(dk_acc)
    dv_acc[...] = jnp.zeros_like(dv_acc)
    fg_a[...] = jnp.zeros_like(fg_a)
    fg_b[...] = jnp.zeros_like(fg_b)
    ps[...] = jnp.zeros_like(ps)

    gain_one, bias_one = norm_params[0:1, :], norm_params[1:2, :]
    gain_two, bias_two = norm_params[2:3, :], norm_params[3:4, :]
    for r in range(4):
        doc_wait(r)

    @pl.loop(0, 8)
    def _(r):
        rows = pl.ds(pl.multiple_of(r * 128, 128), 128)
        unit, _ = unit_of(tok[rows, :].astype(F32))
        n1[rows, :] = (unit * gain_one + bias_one).astype(BF)

    @pl.loop(0, 4)
    def _(r):
        rows = pl.ds(pl.multiple_of(r * 256, 256), 256)
        down[rows, :] = mm_nt(n1[rows, :], f02[...]).astype(BF)

    for group in range(ATTN_GROUPS):
        pump(group)
    for group in range(ATTN_GROUPS):
        hop(2, group).wait_recv()
        hop(3, group).wait_recv()
    pump(8)

    first_head = lax.broadcasted_iota(jnp.int32, (128, 512), 1) % 128 < 64

    def stacked(rows):
        return jnp.concatenate(
            (jnp.where(first_head, rows, 0.0), jnp.where(first_head, 0.0, rows)), 0
        ).astype(BF)

    for i in range(4):
        rows = pl.ds(block_row[i], 128)
        query = mm(n1[rows, :], wa[0]) + ADAPTER_SCALING * mm(down[rows, :], f1p[...])
        qs[i] = stacked(query.astype(BF).astype(F32) * 0.125)
    pump(9)

    @pl.loop(0, 4)
    def _(r):
        rows = pl.ds(pl.multiple_of(r * 256, 256), 256)
        k_all[rows, :] = mm(n1[rows, :], wa[1]).astype(BF)

    pump(10)

    @pl.loop(0, 4)
    def _(r):
        rows = pl.ds(pl.multiple_of(r * 256, 256), 256)
        v_all[rows, :] = (
            mm(n1[rows, :], wa[2]) + ADAPTER_SCALING * mm(down[rows, :], f3p[...])
        ).astype(BF)

    pump(11)

    def forward(i):
        keys = 256 * (i + 1)
        query_pos = lax.broadcasted_iota(jnp.int32, (256, keys), 0) % 128 + block[i] * 128
        allowed = lax.broadcasted_iota(jnp.int32, (256, keys), 1) <= query_pos

        @pl.loop(0, 4)
        def _(s):
            lanes = pl.ds(pl.multiple_of(s * 128, 128), 128)
            scores = mm_nt(qs[i, :, lanes], k_all[0:keys, lanes])
            scores = jnp.where(allowed, scores, NEG_LARGE)
            exponent = jnp.exp(scores - jnp.max(scores, -1, keepdims=True))
            probability = (exponent / jnp.sum(exponent, -1, keepdims=True)).astype(BF)
            p_refs[i][s] = probability
            both = mm(probability, v_all[0:keys, lanes])
            mix[128 * i : 128 * i + 128, lanes] = jnp.where(
                first_head[:, 0:128], both[0:128], both[128:256]
            ).astype(BF)

    forward(0)
    forward(1)
    pump(12)
    forward(2)
    pump(13)
    forward(3)
    pump(14)

    @pl.loop(0, 2)
    def _(r):
        rows = pl.ds(pl.multiple_of(r * 256, 256), 256)
        attn[rows, :] = mm(mix[rows, :], wo[...])

    attn_s[...] = attn[pl.ds(other, 256), :].astype(BF)
    to_nbr(attn_s, attn_r, 8).start()
    pump(15)
    to_nbr(attn_s, attn_r, 8).wait_recv()
    for j in range(2):
        part = slice(128 * j, 128 * j + 128)
        start = pl.multiple_of(128 * (4 * c + 2 * j + (j + x) % 2), 128)
        rows = (
            tok[pl.ds(start, 128), :].astype(F32)
            + attn[pl.ds(pl.multiple_of(own + 128 * j, 128), 128), :]
            + attn_r[part, :].astype(F32)
        )
        res[part, :] = rows
        unit, _ = unit_of(rows)
        n2[pl.ds(pl.multiple_of(own + 128 * j, 128), 128), :] = (unit * gain_two + bias_two).astype(BF)
    half = pl.ds(own, 256)
    to_nbr(n2.at[half, :], n2.at[half, :], 9).start()
    for i in range(4):
        doc_wait(4 + i)

    def feed_forward(slot, h):
        @pl.loop(0, 2)
        def _(r):
            rows = pl.ds(pl.multiple_of(r * 256, 256), 256)
            pre = mm(n2[rows, :], fcw[slot, h])
            square = pre * pre
            tanh = jnp.tanh(GELU_SCALE * pre * (1.0 + GELU_CUBE * square))
            half_up = 0.5 * (1.0 + tanh)
            slope = half_up + (0.5 * GELU_SCALE) * pre * (1.0 - tanh * tanh) * (
                1.0 + 3.0 * GELU_CUBE * square
            )
            mlp_acc[rows, :] += mm((pre * half_up).astype(BF), pw[slot, h])
            grad_pre = (mm_nt(go[rows, :], pw[slot, h]) * slope).astype(BF)
            gnt_acc[rows, :] += mm_nt(grad_pre, fcw[slot, h])

    rest = pl.ds(other, 256)
    to_nbr(n2.at[rest, :], n2.at[rest, :], 9).wait_recv()
    feed_forward(0, 0)
    pump(16)
    feed_forward(0, 1)
    pump(17)
    feed_forward(1, 0)
    pump(18)
    for slot in (2, 3):
        for group in range(8, 16):
            hop(slot, group).wait_recv()
        feed_forward(slot, 0)
        pump(17 + slot)
    for group in range(21, GROUPS):
        pump(group)
    feed_forward(1, 1)
    for slot in (2, 3):
        for group in range(16, GROUPS):
            hop(slot, group).wait_recv()
        feed_forward(slot, 1)

    gnt_s[...] = gnt_acc[rest, :].astype(BF)
    to_nbr(gnt_s, gnt_r, 11).start()
    mlp_s[...] = mlp_acc[rest, :].astype(BF)
    to_nbr(mlp_s, mlp_r, 10).start()
    to_nbr(gnt_s, gnt_r, 11).wait_recv()
    for j in range(2):
        part = slice(128 * j, 128 * j + 128)
        mine = pl.ds(pl.multiple_of(own + 128 * j, 128), 128)
        unit, inverse = unit_of(res[part, :])
        scaled = (gnt_acc[mine, :] + gnt_r[part, :].astype(F32)) * gain_two
        grad = go[mine, :].astype(F32) + inverse * (
            scaled
            - jnp.mean(scaled, -1, keepdims=True)
            - unit * jnp.mean(scaled * unit, -1, keepdims=True)
        )
        gr_b[mine, :] = grad.astype(BF)
    to_nbr(gr_b.at[half, :], gr_b.at[half, :], 12).start()

    def to_owner(src, dst, j, first):
        send, recv = ssem.at[first + j], rsem.at[first + x]

        @pl.when(same[j])
        def _():
            pltpu.make_async_copy(src, dst, recv).start()

        @pl.when(jnp.logical_not(same[j]))
        def _():
            remote(src, dst, send, recv, dests[j]).start()

    def owner_sent(src, dst, j, first):
        @pl.when(jnp.logical_not(same[j]))
        def _():
            remote(src, dst, ssem.at[first + j], rsem.at[first + x], dests[j]).wait_send()

    to_nbr(mlp_s, mlp_r, 10).wait_recv()
    for j in range(2):
        part = slice(128 * j, 128 * j + 128)
        mine = pl.ds(pl.multiple_of(own + 128 * j, 128), 128)
        bo_s[part, :] = (res[part, :] + mlp_acc[mine, :] + mlp_r[part, :].astype(F32)).astype(BF)
    late = []
    for j in range(2):
        place = pl.ds(pl.multiple_of(128 * ((j + x) % 2), 128), 128)
        mine = pl.ds(pl.multiple_of(own + 128 * j, 128), 128)
        late.append((gr_b.at[mine, :], grf.at[place, :], j, 20))
        late.append((bo_s.at[pl.ds(128 * j, 128), :], bo_r.at[place, :], j, 22))
    for item in late:
        to_owner(*item)
    to_nbr(gr_b.at[rest, :], gr_b.at[rest, :], 12).wait_recv()

    for i in range(4):
        grad_mixture = mm_nt(gr_b[128 * i : 128 * i + 128, :], wo[...])
        dos[i] = stacked(grad_mixture.astype(BF).astype(F32))

    def backward(i):
        keys = 256 * (i + 1)

        @pl.loop(0, 4)
        def _(s):
            lanes = pl.ds(pl.multiple_of(s * 128, 128), 128)
            prob_low = p_refs[i][s]
            probability = prob_low.astype(F32)
            grad_rows = dos[i, :, lanes]
            grad_prob = mm_nt(grad_rows, v_all[0:keys, lanes])
            delta = jnp.sum(grad_prob * probability, -1, keepdims=True)
            dscore = (probability * (grad_prob - delta)).astype(BF)
            both = 0.125 * mm(dscore, k_all[0:keys, lanes])
            gq_scr[:, lanes] = jnp.where(first_head[:, 0:128], both[0:128], both[128:256]).astype(BF)
            dk_acc[0:keys, lanes] += mm_tn(dscore, qs[i, :, lanes])
            dv_acc[0:keys, lanes] += mm_tn(prob_low, grad_rows)

        rows = slice(256 * i, 256 * i + 256)
        place = pl.ds(pl.multiple_of(128 * ((i + x) % 2), 128), 128)
        grad_query = gq_scr[...]
        grad_keys = dk_acc[rows, :].astype(BF)
        grad_values = dv_acc[rows, :].astype(BF)
        gd_scr[...] = ADAPTER_SCALING * mm_nt(grad_values, f3p[...])
        gd_scr[place, :] += ADAPTER_SCALING * mm_nt(grad_query, f1p[...])
        grad_down = gd_scr[...].astype(BF)
        gno_scr[...] = mm_nt(grad_keys, wa[1]) + mm_nt(grad_values, wa[2]) + mm(grad_down, f02[...])
        gno_scr[place, :] += mm_nt(grad_query, wa[0])
        gno_s[i] = gno_scr[...].astype(BF)

        @pl.when(c != i // 2)
        def _():
            to_nbr(gno_s.at[i], gno_r.at[i % 2], 13 + i).start()

        fg_a[...] += mm_tn(grad_down, n1[rows, :])[0:8]
        up_query = mm_tn(down[pl.ds(block_row[i], 128), :], grad_query)[0:8]
        up_value = mm_tn(down[rows, :], grad_values)[0:8]
        upper = lax.broadcasted_iota(jnp.int32, (8, 512), 0) < 4
        fg_b[...] += ADAPTER_SCALING * jnp.where(upper, up_query, up_value)

    def reduce_rows(i):
        @pl.when(c == i // 2)
        def _():
            to_nbr(gno_s.at[i], gno_r.at[i % 2], 13 + i).wait_recv()
            chip_s[i % 2] = (gno_s[i].astype(F32) + gno_r[i % 2].astype(F32)).astype(BF)
            to_owner(chip_s.at[i % 2], fin_r.at[x], i % 2, 24)

    backward(3)
    backward(2)
    reduce_rows(3)
    backward(1)
    reduce_rows(2)
    backward(0)
    reduce_rows(1)

    ps[0:8, :] = fg_a[...]
    for s in range(4):
        ps[8:16, pl.ds(column[s], 128)] = fg_b[:, 128 * s : 128 * s + 128]
    to_nbr(ps, ps_r, 17).start()
    reduce_rows(0)
    to_nbr(ps, ps_r, 17).wait_recv()
    mine = pl.ds(pl.multiple_of(8 * c, 8), 8)
    plane_buf[t] = ps[mine, :] + ps_r[mine, :]
    copies = []
    for k, device in enumerate(plane):
        copies.append(remote(plane_buf.at[t], plane_buf.at[t], ssem.at[28 + k], rsem.at[28 + k], device))
        copies[-1].start()
    for copy in copies:
        copy.wait_recv()
    z_buf[z] = plane_buf[0] + plane_buf[1] + plane_buf[2] + plane_buf[3]
    z_copies = []
    for k, device in enumerate(zs):
        z_copies.append(remote(z_buf.at[z], z_buf.at[z], ssem.at[31 + k], rsem.at[31 + k], device))
        z_copies[-1].start()

    own_rows.wait()
    for first in (20, 22):
        for sender in range(2):
            place = pl.ds(128 * sender, 128)
            remote(bo_s.at[pl.ds(0, 128), :], bo_r.at[place, :], ssem.at[first], rsem.at[first + sender], dests[0]).wait_recv()
    block_out[...] = bo_r[...]
    for sender in range(2):
        remote(chip_s.at[0], fin_r.at[sender], ssem.at[24], rsem.at[24 + sender], dests[0]).wait_recv()

    @pl.loop(0, 2)
    def _(r):
        rows = pl.ds(pl.multiple_of(r * 128, 128), 128)
        unit, inverse = unit_of(tokr[rows, :].astype(F32))
        scaled = (fin_r[0, rows, :].astype(F32) + fin_r[1, rows, :].astype(F32)) * gain_one
        input_grad[rows, :] = grf[rows, :].astype(F32) + inverse * (
            scaled
            - jnp.mean(scaled, -1, keepdims=True)
            - unit * jnp.mean(scaled * unit, -1, keepdims=True)
        )

    for copy in z_copies:
        copy.wait_recv()
    total = z_buf[0]
    for k in range(1, planes):
        total = total + z_buf[k]
    fin[mine, :] = total
    to_nbr(fin.at[mine, :], fin.at[mine, :], 18).start()
    theirs = pl.ds(pl.multiple_of(8 - 8 * c, 8), 8)
    to_nbr(fin.at[theirs, :], fin.at[theirs, :], 18).wait_recv()

    grad = fin[...]
    norm = jnp.sqrt(jnp.sum(grad * grad, (0, 1), keepdims=True))
    grad_norm[...] = norm
    grad = grad * (CLIP_NORM / jnp.maximum(norm, CLIP_NORM))
    for index, first in enumerate((0, 8, 4, 12)):
        value, weights = grad[first : first + 4], factors[index]
        first_value = BETA_ONE * first_moment[index] + (1.0 - BETA_ONE) * value
        second_value = BETA_TWO * second_moment[index] + (1.0 - BETA_TWO) * value * value
        first_hat = first_value / (1.0 - BETA_ONE**STEP)
        second_hat = second_value / (1.0 - BETA_TWO**STEP)
        clipped[index] = value
        first_new[index] = first_value
        second_new[index] = second_value
        factors_new[index] = weights - LEARN_RATE * (
            first_hat / (jnp.sqrt(second_hat) + ADAM_EPSILON) + WEIGHT_DECAY * weights
        )

    @pl.when(c == y)
    def _():
        for item in doc:
            to_nbr(*item).wait_send()

    for slot in (1, 2, 3):
        for group in range(GROUPS):
            hop(slot, group).wait_send()
    to_nbr(attn_s, attn_r, 8).wait_send()
    to_nbr(n2.at[half, :], n2.at[half, :], 9).wait_send()
    to_nbr(mlp_s, mlp_r, 10).wait_send()
    to_nbr(gnt_s, gnt_r, 11).wait_send()
    to_nbr(gr_b.at[half, :], gr_b.at[half, :], 12).wait_send()
    to_nbr(ps, ps_r, 17).wait_send()
    to_nbr(fin.at[mine, :], fin.at[mine, :], 18).wait_send()
    for item in late:
        owner_sent(*item)
    for i in range(4):

        @pl.when(c != i // 2)
        def _():
            to_nbr(gno_s.at[i], gno_r.at[i % 2], 13 + i).wait_send()

    for j in range(2):
        owner_sent(chip_s.at[j], fin_r.at[x], j, 24)
    for copy in copies + z_copies:
        copy.wait_send()


def fused(planes, *args):
    vmem = pl.BlockSpec(memory_space=pltpu.VMEM)
    hbm = pl.BlockSpec(memory_space=pl.ANY)

    def buf(*shape, dtype=BF):
        return pltpu.VMEM(shape, dtype)

    def acc(*shape):
        return pltpu.VMEM(shape, F32)

    scratch = [
        buf(1024, 1024), buf(1024, 1024), buf(512, 1024), buf(3, 1024, 512), buf(512, 1024),
        buf(4, 2, 1024, 256), buf(4, 2, 256, 1024), buf(1024, 512), buf(1024, 512), buf(4, 256, 512),
        buf(4, 256, 256), buf(4, 256, 512), buf(4, 256, 768), buf(4, 256, 1024), buf(512, 512),
        acc(512, 1024), buf(256, 1024), buf(256, 1024),
        acc(256, 1024), buf(512, 1024), acc(512, 1024), acc(512, 1024),
        buf(256, 1024), buf(256, 1024), buf(256, 1024), buf(256, 1024), buf(512, 1024),
        buf(256, 1024), buf(256, 1024), buf(256, 1024),
        acc(1024, 512), acc(1024, 512), buf(128, 512), buf(4, 256, 512), acc(256, 1024),
        buf(4, 256, 1024), buf(2, 256, 1024), buf(2, 256, 1024), buf(2, 256, 1024), buf(256, 1024),
        acc(128, 1024), buf(128, 1024), buf(128, 512), buf(128, 512), buf(1024, 128), acc(256, 128),
        acc(8, 1024), acc(8, 512), acc(16, 1024), acc(16, 1024), acc(4, 8, 1024), acc(planes, 8, 1024),
        acc(16, 1024),
        pltpu.SemaphoreType.DMA((3, GROUPS)), pltpu.SemaphoreType.DMA((3, GROUPS)),
        pltpu.SemaphoreType.DMA((9,)), pltpu.SemaphoreType.DMA((31 + planes,)),
        pltpu.SemaphoreType.DMA((31 + planes,)),
    ]
    small = jax.ShapeDtypeStruct((4, 4, 1024), F32)
    outs = pl.pallas_call(
        functools.partial(fused_kernel, planes),
        name="block_step",
        out_shape=(
            jax.ShapeDtypeStruct((256, 1024), BF), jax.ShapeDtypeStruct((256, 1024), F32), small,
            jax.ShapeDtypeStruct((1, 1), F32), small, small, small,
        ),
        in_specs=[hbm, vmem, hbm, hbm, hbm, hbm, vmem, vmem, vmem, hbm],
        out_specs=(vmem,) * 7,
        scratch_shapes=scratch,
        compiler_params=pltpu.CompilerParams(
            collective_id=1, has_side_effects=True, vmem_limit_bytes=62 << 20
        ),
    )(*args)
    return outs[:3] + (outs[3].reshape(()),) + outs[4:]


def solution(mesh):
    placed = (
        P("dp", None),
        P(),
        P(None, None, "tensor"),
        P("tensor", None),
        P(None, "tensor"),
        P("tensor", None),
        P(),
        P(),
        P(),
        P("dp", None),
    )
    planes = mesh.shape["dp"] // 2

    def step(*args):
        rows, width = args[0].shape
        shapes = (rows, width, args[4].shape[1], args[2].shape[2], args[6].shape[1])
        fits = mesh.shape["tensor"] == 4 and mesh.shape["dp"] % 4 == 0
        if fits and shapes == (SEQ, 1024, 1024, 256, 4):
            return fused(planes, *args)
        return body(*args)

    return jax.shard_map(
        step,
        mesh=mesh,
        in_specs=placed,
        out_specs=(P(("dp", "tensor"), None), P(("dp", "tensor"), None), P(), P(), P(), P(), P()),
        check_vma=False,
    )
```

```python
import functools

import jax
import jax.numpy as jnp
from jax import lax
from jax.experimental import pallas as pl
from jax.experimental.pallas import tpu as pltpu
from jax.sharding import PartitionSpec as P

HD = 64
SEQ = 1024
STEP = 5


EPSILON = 1e-05
ADAPTER_SCALING = 8.0
CLIP_NORM = 16.0
LEARN_RATE = 0.03
BETA_ONE = 0.5
BETA_TWO = 0.5
WEIGHT_DECAY = 0.01
ADAM_EPSILON = 1e-08
NEG_LARGE = -1e30
GELU_SCALE = 0.7978845608028654
GELU_CUBE = 0.044715


def matrix_product(left, right):
    return jnp.dot(left, right, preferred_element_type=jnp.float32)


def product_with_transpose(left, right):
    return lax.dot_general(
        left, right, (((1,), (1,)), ((), ())), preferred_element_type=jnp.float32
    )


def transpose_then_product(left, right):
    return lax.dot_general(
        left, right, (((0,), (0,)), ((), ())), preferred_element_type=jnp.float32
    )


def normalize(value_rows_local, gain_vec, bias_vec):
    centered = value_rows_local - jnp.mean(value_rows_local, -1, keepdims=True)
    inverse = lax.rsqrt(jnp.mean(centered * centered, -1, keepdims=True) + EPSILON)
    unit_rows = centered * inverse
    return (unit_rows * gain_vec + bias_vec, unit_rows, inverse)


def normalize_back(incoming, unit_rows, inverse, gain_vec):
    scaled = incoming * gain_vec
    return inverse * (
        scaled
        - jnp.mean(scaled, -1, keepdims=True)
        - unit_rows * jnp.mean(scaled * unit_rows, -1, keepdims=True)
    )


def causal_scores(query_block, key_all, block_index, block_len):
    scores = (
        jnp.einsum("bqhd,bkhd->bhqk", query_block, key_all, preferred_element_type=jnp.float32)
        * 0.125
    )
    query_pos = block_index * block_len + jnp.arange(block_len)
    allowed = jnp.arange(SEQ)[None, :] <= query_pos[:, None]
    return jnp.where(allowed, scores, NEG_LARGE)


def attention_forward(query_rows_local, key_all, value_all):
    block_len = min(512, SEQ)
    outputs = []
    logsums = []
    for block_index in range(SEQ // block_len):
        query_block = query_rows_local[:, block_index * block_len : (block_index + 1) * block_len]
        scores = causal_scores(query_block, key_all, block_index, block_len)
        row_max = jnp.max(scores, -1, keepdims=True)
        exponent = jnp.exp(scores - row_max)
        row_total = jnp.sum(exponent, -1, keepdims=True)
        probability = (exponent / row_total).astype(jnp.bfloat16)
        mixture = jnp.einsum(
            "bhqk,bkhd->bqhd", probability, value_all, preferred_element_type=jnp.float32
        )
        outputs.append(mixture.astype(jnp.bfloat16))
        logsums.append(row_max[..., 0] + jnp.log(row_total[..., 0]))
    return (jnp.concatenate(outputs, 1), jnp.concatenate(logsums, 2))


def attention_backward(query_rows_local, key_all, value_all, grad_mixture, logsums):
    block_len = min(512, SEQ)
    grad_queries = []
    grad_keys = jnp.zeros(key_all.shape, jnp.float32)
    value_gradient_rows = jnp.zeros(value_all.shape, jnp.float32)
    for block_index in range(SEQ // block_len):
        lower = block_index * block_len
        query_block = query_rows_local[:, lower : lower + block_len]
        grad_block = grad_mixture[:, lower : lower + block_len]
        scores = causal_scores(query_block, key_all, block_index, block_len)
        probability = jnp.exp(scores - logsums[:, :, lower : lower + block_len, None])
        grad_prob = jnp.einsum(
            "bqhd,bkhd->bhqk", grad_block, value_all, preferred_element_type=jnp.float32
        )
        row_delta = jnp.sum(grad_prob * probability, -1, keepdims=True)
        dscore = (0.125 * (probability * (grad_prob - row_delta))).astype(jnp.bfloat16)
        grad_queries.append(
            jnp.einsum(
                "bhqk,bkhd->bqhd", dscore, key_all, preferred_element_type=jnp.float32
            ).astype(jnp.bfloat16)
        )
        grad_keys = grad_keys + jnp.einsum(
            "bhqk,bqhd->bkhd", dscore, query_block, preferred_element_type=jnp.float32
        )
        value_gradient_rows = value_gradient_rows + jnp.einsum(
            "bhqk,bqhd->bkhd",
            probability.astype(jnp.bfloat16),
            grad_block,
            preferred_element_type=jnp.float32,
        )
    return (
        jnp.concatenate(grad_queries, 1),
        grad_keys.astype(jnp.bfloat16),
        value_gradient_rows.astype(jnp.bfloat16),
    )


def adam_step(factor_grad, weights, first_old, second_old, grad_norm):
    clipped = factor_grad * (CLIP_NORM / jnp.maximum(grad_norm, CLIP_NORM))
    first_new = BETA_ONE * first_old + (1.0 - BETA_ONE) * clipped
    second_new = BETA_TWO * second_old + (1.0 - BETA_TWO) * clipped * clipped
    first_hat = first_new / (1.0 - BETA_ONE**STEP)
    second_hat = second_new / (1.0 - BETA_TWO**STEP)
    weights_new = weights - LEARN_RATE * (
        first_hat / (jnp.sqrt(second_hat) + ADAM_EPSILON) + WEIGHT_DECAY * weights
    )
    return (clipped, weights_new, first_new, second_new)


def body(
    tokens_in,
    norm_params,
    query_key_value_weight,
    out_weight,
    fc_weight,
    proj_weight,
    factors,
    first_moment,
    second_moment,
    grad_out,
):
    tensor_size = lax.axis_size("tensor")
    tensor_rank = lax.axis_index("tensor")
    token_count = tokens_in.shape[0]
    doc_count = token_count // SEQ
    local_width = query_key_value_weight.shape[2]
    heads_here = local_width // HD
    row_count = token_count // tensor_size
    row_start = tensor_rank * row_count
    rank_count = factors.shape[1]
    full_width = factors.shape[2]
    inputs = tokens_in.astype(jnp.float32)
    first_normalized, unit_one, inverse_one = normalize(inputs, norm_params[0], norm_params[1])
    first_normalized_reduced = first_normalized.astype(jnp.bfloat16)
    factor_reduced_precision = factors.astype(jnp.bfloat16)
    column_offset = tensor_rank * local_width
    query_adapter_output = lax.dynamic_slice_in_dim(
        factor_reduced_precision[1], column_offset, local_width, 1
    )
    value_adapter_output = lax.dynamic_slice_in_dim(
        factor_reduced_precision[3], column_offset, local_width, 1
    )
    query_down_factor = product_with_transpose(
        first_normalized_reduced, factor_reduced_precision[0]
    ).astype(jnp.bfloat16)
    value_down_factor = product_with_transpose(
        first_normalized_reduced, factor_reduced_precision[2]
    ).astype(jnp.bfloat16)
    query_rows_local = (
        matrix_product(first_normalized_reduced, query_key_value_weight[0])
        + ADAPTER_SCALING * matrix_product(query_down_factor, query_adapter_output)
    ).astype(jnp.bfloat16)
    keys_low = matrix_product(first_normalized_reduced, query_key_value_weight[1]).astype(
        jnp.bfloat16
    )
    values_low = (
        matrix_product(first_normalized_reduced, query_key_value_weight[2])
        + ADAPTER_SCALING * matrix_product(value_down_factor, value_adapter_output)
    ).astype(jnp.bfloat16)
    head_shape = (doc_count, SEQ, heads_here, HD)
    query_heads = query_rows_local.reshape(head_shape)
    keys_heads = keys_low.reshape(head_shape)
    values_heads = values_low.reshape(head_shape)
    mixture, logsums = attention_forward(query_heads, keys_heads, values_heads)
    attn_part = matrix_product(mixture.reshape(token_count, local_width), out_weight)
    grad_full = grad_out.astype(jnp.float32)
    attn_rows = lax.psum_scatter(
        attn_part.astype(jnp.bfloat16), "tensor", scatter_dimension=0, tiled=True
    ).astype(jnp.float32)
    resid_rows = lax.dynamic_slice_in_dim(inputs, row_start, row_count, 0) + attn_rows
    normed_two_rows, unit_two, inverse_two = normalize(resid_rows, norm_params[2], norm_params[3])
    normed_two_low = lax.all_gather(
        normed_two_rows.astype(jnp.bfloat16), "tensor", axis=0, tiled=True
    )
    hidden_pre = matrix_product(normed_two_low, fc_weight)
    hidden_act, gelu_pull = jax.vjp(
        lambda argument: jax.nn.gelu(argument, approximate=True), hidden_pre
    )
    mlp_part = matrix_product(hidden_act.astype(jnp.bfloat16), proj_weight)
    grad_hidden = product_with_transpose(grad_out, proj_weight)
    grad_pre = gelu_pull(grad_hidden)[0].astype(jnp.bfloat16)
    second_part = product_with_transpose(grad_pre, fc_weight)
    out_rows = resid_rows + lax.psum_scatter(
        mlp_part.astype(jnp.bfloat16), "tensor", scatter_dimension=0, tiled=True
    ).astype(jnp.float32)
    second_rows = lax.psum_scatter(
        second_part.astype(jnp.bfloat16), "tensor", scatter_dimension=0, tiled=True
    ).astype(jnp.float32)
    resid_grad_rows = lax.dynamic_slice_in_dim(grad_full, row_start, row_count, 0) + normalize_back(
        second_rows, unit_two, inverse_two, norm_params[2]
    )
    resid_grad_low = lax.all_gather(
        resid_grad_rows.astype(jnp.bfloat16), "tensor", axis=0, tiled=True
    )
    grad_mixture = product_with_transpose(resid_grad_low, out_weight).astype(jnp.bfloat16)
    query_gradient, grad_keys, value_gradient_rows = attention_backward(
        query_heads, keys_heads, values_heads, grad_mixture.reshape(head_shape), logsums
    )
    query_gradient = query_gradient.reshape(token_count, local_width)
    grad_keys = grad_keys.reshape(token_count, local_width)
    value_gradient_rows = value_gradient_rows.reshape(token_count, local_width)
    stacked = jnp.stack((query_gradient, grad_keys, value_gradient_rows))
    first_part = jnp.einsum(
        "stc,sdc->td", stacked, query_key_value_weight, preferred_element_type=jnp.float32
    )
    query_up_factor = ADAPTER_SCALING * product_with_transpose(query_gradient, query_adapter_output)
    value_up_factor = ADAPTER_SCALING * product_with_transpose(
        value_gradient_rows, value_adapter_output
    )
    first_part = first_part + jnp.dot(
        query_up_factor,
        factor_reduced_precision[0].astype(jnp.float32),
        precision=lax.Precision.HIGHEST,
    )
    first_part = first_part + jnp.dot(
        value_up_factor,
        factor_reduced_precision[2].astype(jnp.float32),
        precision=lax.Precision.HIGHEST,
    )
    first_rows = lax.psum_scatter(
        first_part.astype(jnp.bfloat16), "tensor", scatter_dimension=0, tiled=True
    ).astype(jnp.float32)
    unit_rows = lax.dynamic_slice_in_dim(unit_one, row_start, row_count, 0)
    inverse_rows = lax.dynamic_slice_in_dim(inverse_one, row_start, row_count, 0)
    input_rows = resid_grad_rows + normalize_back(
        first_rows, unit_rows, inverse_rows, norm_params[0]
    )
    query_cross_term = transpose_then_product(query_gradient, first_normalized_reduced)
    value_cross_term = transpose_then_product(value_gradient_rows, first_normalized_reduced)
    query_down_gradient = ADAPTER_SCALING * jnp.dot(
        query_adapter_output.astype(jnp.float32), query_cross_term, precision=lax.Precision.HIGHEST
    )
    value_down_gradient = ADAPTER_SCALING * jnp.dot(
        value_adapter_output.astype(jnp.float32), value_cross_term, precision=lax.Precision.HIGHEST
    )
    empty_slot = jnp.zeros((rank_count, full_width), jnp.float32)
    up_grad_query = lax.dynamic_update_slice_in_dim(
        empty_slot,
        ADAPTER_SCALING * transpose_then_product(query_down_factor, query_gradient),
        column_offset,
        1,
    )
    up_grad_value = lax.dynamic_update_slice_in_dim(
        empty_slot,
        ADAPTER_SCALING * transpose_then_product(value_down_factor, value_gradient_rows),
        column_offset,
        1,
    )
    partial_grad = jnp.stack(
        (query_down_gradient, up_grad_query, value_down_gradient, up_grad_value)
    )
    reduced = lax.psum(partial_grad, ("dp", "tensor"))
    grad_norm = jnp.sqrt(jnp.sum(reduced * reduced))
    clipped, weights_new, first_new, second_new = adam_step(
        reduced, factors, first_moment, second_moment, grad_norm
    )
    return (
        out_rows.astype(jnp.bfloat16),
        input_rows,
        clipped,
        grad_norm,
        weights_new,
        first_new,
        second_new,
    )


MESH = pl.DeviceIdType.MESH
BF = jnp.bfloat16
F32 = jnp.float32
GROUPS = 24
ATTN_GROUPS = 8


def mm(left, right):
    return jnp.dot(left, right, preferred_element_type=F32)


def mm_nt(left, right):
    return lax.dot_general(left, right, (((1,), (1,)), ((), ())), preferred_element_type=F32)


def mm_tn(left, right):
    return lax.dot_general(left, right, (((0,), (0,)), ((), ())), preferred_element_type=F32)


def flip(value, bit):
    return value + bit - 2 * bit * ((value // bit) % 2)


def unit_of(rows):
    centered = rows - jnp.mean(rows, -1, keepdims=True)
    inverse = lax.rsqrt(jnp.mean(centered * centered, -1, keepdims=True) + EPSILON)
    return centered * inverse, inverse


def fused_kernel(
    planes,
    tokens, norm_params, wqkv, w_out, w_fc, w_proj, factors, grad_out,
    bo_r, grf, fin_r, tokr, summed,
    tok, n1, go, wa, wo, fcw, pw, k_all, v_all, qs, p0, p1, p2, p3, mix, attn, attn_s, attn_r,
    res, n2, mlp_acc, gnt_acc, mlp_s, mlp_r, gnt_s, gnt_r, gr_b, bo_s,
    dk_acc, dv_acc, gq_scr, dos, gno_scr, gno_s, gno_r, chip_s,
    fpad, f02, f1p, f3p, down, gd_scr, fg_a, fg_b, ps, ps_r, plane_buf, z_buf, fin,
    chain_send, chain_recv, load_sem, ssem, rsem,
):
    d = lax.axis_index("dp")
    t = lax.axis_index("tensor")
    z, c, x, y = d // 2, d % 2, t % 2, t // 2
    odd = z % 2
    nbr = (flip(d, 1), t)
    prim = (d, flip(t, 1 + odd))
    sec = (d, flip(t, 2 - odd))
    plane = [(d, flip(t, 1)), (d, flip(t, 2)), (d, 3 - t)]
    zs = [(flip(d, 2 << k), t) for k in range(planes.bit_length() - 1)]
    dests = [(2 * z + y, 2 * c + j) for j in range(2)]
    same = [jnp.logical_and(c == y, x == j) for j in range(2)]
    quarter = [t, flip(t, 1 + odd), flip(t, 2 - odd), 3 - t]
    column = [pl.multiple_of(q * 256 + c * 128, 128) for q in quarter]
    block = [2 * i + (i + x) % 2 for i in range(4)]
    block_row = [pl.multiple_of(b * 128, 128) for b in block]
    own = pl.multiple_of(c * 256, 256)
    other = pl.multiple_of(256 - c * 256, 256)
    p_refs = (p0, p1, p2, p3)

    def remote(src, dst, send, recv, device):
        return pltpu.make_async_remote_copy(
            src_ref=src, dst_ref=dst, send_sem=send, recv_sem=recv, device_id=device, device_id_type=MESH
        )

    def to_nbr(src, dst, index):
        return remote(src, dst, ssem.at[index], rsem.at[index], nbr)

    pending = []

    def drain():
        for wait in pending:
            wait()

    def send(copy):
        copy.start()
        pending.append(copy.wait_send)

    lane = pl.ds(pl.multiple_of(c * 128, 128), 128)
    loads = [
        pltpu.make_async_copy(wqkv.at[m, :, lane], wa.at[m, :, pl.ds(0, 128)], load_sem.at[m])
        for m in range(3)
    ]
    loads.append(pltpu.make_async_copy(w_out.at[lane, :], wo.at[pl.ds(0, 128), :], load_sem.at[3]))
    for h in range(2):
        hidden = pl.ds(pl.multiple_of(c * 512 + h * 256, 256), 256)
        loads.append(pltpu.make_async_copy(w_fc.at[:, hidden], fcw.at[0, h], load_sem.at[4 + 2 * h]))
        loads.append(pltpu.make_async_copy(w_proj.at[hidden, :], pw.at[0, h], load_sem.at[5 + 2 * h]))
    for load in loads:
        load.start()
    own_rows = pltpu.make_async_copy(
        tokens.at[pl.ds(pl.multiple_of(t * 256, 256), 256), :], tokr, load_sem.at[8]
    )
    own_rows.start()

    barrier = pltpu.get_barrier_semaphore()
    partners = [nbr] + plane[:2] + zs
    for device in partners:
        pl.semaphore_signal(barrier, inc=1, device_id=device, device_id_type=MESH)
    pl.semaphore_wait(barrier, len(partners))

    doc = [
        (tokens.at[pl.ds(256 * r, 256), :], tok.at[pl.ds(256 * r, 256), :], r) for r in range(4)
    ] + [
        (grad_out.at[pl.ds(block_row[i], 128), :], go.at[pl.ds(128 * i, 128), :], 4 + i) for i in range(4)
    ]

    @pl.when(c == y)
    def _():
        for src, dst, index in doc:
            to_nbr(src, dst, index).start()
            pltpu.make_async_copy(src, dst, rsem.at[index]).start()

    def doc_sent():
        @pl.when(c == y)
        def _():
            for item in doc:
                to_nbr(*item).wait_send()

    pending.append(doc_sent)

    def doc_wait(index):
        to_nbr(*doc[index]).wait_recv()

    def piece(slot, group):
        if group < ATTN_GROUPS:
            m, a = group // 2, group % 2
            if m < 3:
                return wa.at[m, pl.ds(512 * a, 512), pl.ds(128 * slot, 128)]
            return wo.at[pl.ds(128 * slot + 64 * a, 64), :]
        h, r = (group - ATTN_GROUPS) // 8, (group - ATTN_GROUPS) % 8
        if r < 4:
            return fcw.at[slot, h, pl.ds(256 * r, 256), :]
        return pw.at[slot, h, pl.ds(64 * (r - 4), 64), :]

    def hop(slot, group):
        return remote(
            piece(1 if slot > 1 else 0, group),
            piece(slot, group),
            chain_send.at[slot - 1, group],
            chain_recv.at[slot - 1, group],
            (prim, zs[0], sec)[slot - 1],
        )

    for load in loads:
        load.wait()
    for group in range(GROUPS):
        send(hop(1, group))

    def pump(group):
        hop(1, group).wait_recv()
        send(hop(2, group))
        send(hop(3, group))

    fpad[...] = jnp.zeros_like(fpad)
    fpad[0:4, :] = factors[0]
    fpad[4:8, :] = factors[2]
    f02[...] = fpad[...].astype(BF)
    fpad[...] = jnp.zeros_like(fpad)
    for s in range(4):
        fpad[0:4, 128 * s : 128 * s + 128] = factors[1, :, pl.ds(column[s], 128)]
        fpad[4:8, 512 + 128 * s : 640 + 128 * s] = factors[3, :, pl.ds(column[s], 128)]
    f1p[...] = fpad[:, :512].astype(BF)
    f3p[...] = fpad[:, 512:].astype(BF)
    attn[...] = jnp.zeros_like(attn)
    mlp_acc[...] = jnp.zeros_like(mlp_acc)
    gnt_acc[...] = jnp.zeros_like(gnt_acc)
    dk_acc[...] = jnp.zeros_like(dk_acc)
    dv_acc[...] = jnp.zeros_like(dv_acc)
    fg_a[...] = jnp.zeros_like(fg_a)
    fg_b[...] = jnp.zeros_like(fg_b)
    ps[...] = jnp.zeros_like(ps)

    gain_one, bias_one = norm_params[0:1, :], norm_params[1:2, :]
    gain_two, bias_two = norm_params[2:3, :], norm_params[3:4, :]
    for r in range(4):
        doc_wait(r)

    @pl.loop(0, 8)
    def _(r):
        rows = pl.ds(pl.multiple_of(r * 128, 128), 128)
        unit, _ = unit_of(tok[rows, :].astype(F32))
        n1[rows, :] = (unit * gain_one + bias_one).astype(BF)

    @pl.loop(0, 4)
    def _(r):
        rows = pl.ds(pl.multiple_of(r * 256, 256), 256)
        down[rows, :] = mm_nt(n1[rows, :], f02[...]).astype(BF)

    for group in range(ATTN_GROUPS):
        pump(group)
    for group in range(ATTN_GROUPS):
        hop(2, group).wait_recv()
        hop(3, group).wait_recv()
    pump(8)

    first_head = lax.broadcasted_iota(jnp.int32, (128, 512), 1) % 128 < 64

    def stacked(rows):
        return jnp.concatenate(
            (jnp.where(first_head, rows, 0.0), jnp.where(first_head, 0.0, rows)), 0
        ).astype(BF)

    for i in range(4):
        rows = pl.ds(block_row[i], 128)
        query = mm(n1[rows, :], wa[0]) + ADAPTER_SCALING * mm(down[rows, :], f1p[...])
        qs[i] = stacked(query.astype(BF).astype(F32) * 0.125)
    pump(9)

    @pl.loop(0, 4)
    def _(r):
        rows = pl.ds(pl.multiple_of(r * 256, 256), 256)
        k_all[rows, :] = mm(n1[rows, :], wa[1]).astype(BF)

    pump(10)

    @pl.loop(0, 4)
    def _(r):
        rows = pl.ds(pl.multiple_of(r * 256, 256), 256)
        v_all[rows, :] = (
            mm(n1[rows, :], wa[2]) + ADAPTER_SCALING * mm(down[rows, :], f3p[...])
        ).astype(BF)

    pump(11)

    def forward(i):
        keys = 256 * (i + 1)
        query_pos = lax.broadcasted_iota(jnp.int32, (256, keys), 0) % 128 + block[i] * 128
        allowed = lax.broadcasted_iota(jnp.int32, (256, keys), 1) <= query_pos

        @pl.loop(0, 4)
        def _(s):
            lanes = pl.ds(pl.multiple_of(s * 128, 128), 128)
            scores = mm_nt(qs[i, :, lanes], k_all[0:keys, lanes])
            scores = jnp.where(allowed, scores, NEG_LARGE)
            exponent = jnp.exp(scores - jnp.max(scores, -1, keepdims=True))
            probability = (exponent / jnp.sum(exponent, -1, keepdims=True)).astype(BF)
            p_refs[i][s] = probability
            both = mm(probability, v_all[0:keys, lanes])
            mix[128 * i : 128 * i + 128, lanes] = jnp.where(
                first_head[:, 0:128], both[0:128], both[128:256]
            ).astype(BF)

    forward(0)
    forward(1)
    pump(12)
    forward(2)
    pump(13)
    forward(3)
    pump(14)

    @pl.loop(0, 2)
    def _(r):
        rows = pl.ds(pl.multiple_of(r * 256, 256), 256)
        attn[rows, :] = mm(mix[rows, :], wo[...])

    attn_s[...] = attn[pl.ds(other, 256), :].astype(BF)
    send(to_nbr(attn_s, attn_r, 8))
    pump(15)
    to_nbr(attn_s, attn_r, 8).wait_recv()
    for j in range(2):
        part = slice(128 * j, 128 * j + 128)
        start = pl.multiple_of(128 * (4 * c + 2 * j + (j + x) % 2), 128)
        rows = (
            tok[pl.ds(start, 128), :].astype(F32)
            + attn[pl.ds(pl.multiple_of(own + 128 * j, 128), 128), :]
            + attn_r[part, :].astype(F32)
        )
        res[part, :] = rows
        unit, _ = unit_of(rows)
        n2[pl.ds(pl.multiple_of(own + 128 * j, 128), 128), :] = (unit * gain_two + bias_two).astype(BF)
    half = pl.ds(own, 256)
    send(to_nbr(n2.at[half, :], n2.at[half, :], 9))
    for i in range(4):
        doc_wait(4 + i)

    def feed_forward(slot, h):
        @pl.loop(0, 2)
        def _(r):
            rows = pl.ds(pl.multiple_of(r * 256, 256), 256)
            pre = mm(n2[rows, :], fcw[slot, h])
            square = pre * pre
            tanh = jnp.tanh(GELU_SCALE * pre * (1.0 + GELU_CUBE * square))
            half_up = 0.5 * (1.0 + tanh)
            slope = half_up + (0.5 * GELU_SCALE) * pre * (1.0 - tanh * tanh) * (
                1.0 + 3.0 * GELU_CUBE * square
            )
            mlp_acc[rows, :] += mm((pre * half_up).astype(BF), pw[slot, h])
            grad_pre = (mm_nt(go[rows, :], pw[slot, h]) * slope).astype(BF)
            gnt_acc[rows, :] += mm_nt(grad_pre, fcw[slot, h])

    rest = pl.ds(other, 256)
    to_nbr(n2.at[rest, :], n2.at[rest, :], 9).wait_recv()
    feed_forward(0, 0)
    pump(16)
    feed_forward(0, 1)
    pump(17)
    feed_forward(1, 0)
    pump(18)
    for slot in (2, 3):
        for group in range(8, 16):
            hop(slot, group).wait_recv()
        feed_forward(slot, 0)
        pump(17 + slot)
    for group in range(21, GROUPS):
        pump(group)
    feed_forward(1, 1)
    for slot in (2, 3):
        for group in range(16, GROUPS):
            hop(slot, group).wait_recv()
        feed_forward(slot, 1)

    gnt_s[...] = gnt_acc[rest, :].astype(BF)
    send(to_nbr(gnt_s, gnt_r, 11))
    mlp_s[...] = mlp_acc[rest, :].astype(BF)
    send(to_nbr(mlp_s, mlp_r, 10))
    to_nbr(gnt_s, gnt_r, 11).wait_recv()
    for j in range(2):
        part = slice(128 * j, 128 * j + 128)
        mine = pl.ds(pl.multiple_of(own + 128 * j, 128), 128)
        unit, inverse = unit_of(res[part, :])
        scaled = (gnt_acc[mine, :] + gnt_r[part, :].astype(F32)) * gain_two
        grad = go[mine, :].astype(F32) + inverse * (
            scaled
            - jnp.mean(scaled, -1, keepdims=True)
            - unit * jnp.mean(scaled * unit, -1, keepdims=True)
        )
        gr_b[mine, :] = grad.astype(BF)
    send(to_nbr(gr_b.at[half, :], gr_b.at[half, :], 12))

    def to_owner(src, dst, j, first):
        recv = rsem.at[first + x]

        @pl.when(same[j])
        def _():
            pltpu.make_async_copy(src, dst, recv).start()

        @pl.when(jnp.logical_not(same[j]))
        def _():
            remote(src, dst, ssem.at[first + j], recv, dests[j]).start()

    def owner_sent(src, dst, j, first):
        @pl.when(jnp.logical_not(same[j]))
        def _():
            remote(src, dst, ssem.at[first + j], rsem.at[first + x], dests[j]).wait_send()

    to_nbr(mlp_s, mlp_r, 10).wait_recv()
    for j in range(2):
        part = slice(128 * j, 128 * j + 128)
        mine = pl.ds(pl.multiple_of(own + 128 * j, 128), 128)
        bo_s[part, :] = (res[part, :] + mlp_acc[mine, :] + mlp_r[part, :].astype(F32)).astype(BF)
    late = []
    for j in range(2):
        place = pl.ds(pl.multiple_of(128 * ((j + x) % 2), 128), 128)
        mine = pl.ds(pl.multiple_of(own + 128 * j, 128), 128)
        late.append((gr_b.at[mine, :], grf.at[place, :], j, 20))
        late.append((bo_s.at[pl.ds(128 * j, 128), :], bo_r.at[place, :], j, 22))
    for item in late:
        to_owner(*item)
        pending.append(functools.partial(owner_sent, *item))
    to_nbr(gr_b.at[rest, :], gr_b.at[rest, :], 12).wait_recv()

    for i in range(4):
        grad_mixture = mm_nt(gr_b[128 * i : 128 * i + 128, :], wo[...])
        dos[i] = stacked(grad_mixture.astype(BF).astype(F32))

    def scores_back(i):
        keys = 256 * (i + 1)

        @pl.loop(0, 4)
        def _(s):
            lanes = pl.ds(pl.multiple_of(s * 128, 128), 128)
            prob_low = p_refs[i][s]
            probability = prob_low.astype(F32)
            grad_rows = dos[i, :, lanes]
            grad_prob = mm_nt(grad_rows, v_all[0:keys, lanes])
            delta = jnp.sum(grad_prob * probability, -1, keepdims=True)
            dscore = (probability * (grad_prob - delta)).astype(BF)
            both = 0.125 * mm(dscore, k_all[0:keys, lanes])
            gq_scr[:, lanes] = jnp.where(first_head[:, 0:128], both[0:128], both[128:256]).astype(BF)
            dk_acc[0:keys, lanes] += mm_tn(dscore, qs[i, :, lanes])
            dv_acc[0:keys, lanes] += mm_tn(prob_low, grad_rows)

    def factors_back(i):
        rows = slice(256 * i, 256 * i + 256)
        place = pl.ds(pl.multiple_of(128 * ((i + x) % 2), 128), 128)
        grad_query = gq_scr[...]
        grad_values = dv_acc[rows, :].astype(BF)
        gd_scr[...] = ADAPTER_SCALING * mm_nt(grad_values, f3p[...])
        gd_scr[place, :] += ADAPTER_SCALING * mm_nt(grad_query, f1p[...])
        fg_a[...] += mm_tn(gd_scr[...].astype(BF), n1[rows, :])[0:8]
        up_query = mm_tn(down[pl.ds(block_row[i], 128), :], grad_query)[0:8]
        up_value = mm_tn(down[rows, :], grad_values)[0:8]
        upper = lax.broadcasted_iota(jnp.int32, (8, 512), 0) < 4
        fg_b[...] += ADAPTER_SCALING * jnp.where(upper, up_query, up_value)

    def rows_back(i):
        rows = slice(256 * i, 256 * i + 256)
        place = pl.ds(pl.multiple_of(128 * ((i + x) % 2), 128), 128)
        gno_scr[...] = (
            mm_nt(dk_acc[rows, :].astype(BF), wa[1])
            + mm_nt(dv_acc[rows, :].astype(BF), wa[2])
            + mm(gd_scr[...].astype(BF), f02[...])
        )
        gno_scr[place, :] += mm_nt(gq_scr[...], wa[0])
        gno_s[i] = gno_scr[...].astype(BF)

        @pl.when(c != i // 2)
        def _():
            to_nbr(gno_s.at[i], gno_r.at[i % 2], 13 + i).start()

        def rows_sent():
            @pl.when(c != i // 2)
            def _():
                to_nbr(gno_s.at[i], gno_r.at[i % 2], 13 + i).wait_send()

        pending.append(rows_sent)

    def reduce_rows(i):
        @pl.when(c == i // 2)
        def _():
            to_nbr(gno_s.at[i], gno_r.at[i % 2], 13 + i).wait_recv()
            chip_s[i % 2] = (gno_s[i].astype(F32) + gno_r[i % 2].astype(F32)).astype(BF)
            to_owner(chip_s.at[i % 2], fin_r.at[x], i % 2, 24)

        if i < 2:
            pending.append(functools.partial(owner_sent, chip_s.at[i], fin_r.at[x], i, 24))

    for i in (3, 2, 1):
        scores_back(i)
        factors_back(i)
        rows_back(i)
        if i < 3:
            reduce_rows(i + 1)
    scores_back(0)
    factors_back(0)

    ps[0:8, :] = fg_a[...]
    for s in range(4):
        ps[8:16, pl.ds(column[s], 128)] = fg_b[:, 128 * s : 128 * s + 128]
    send(to_nbr(ps, ps_r, 17))
    rows_back(0)
    to_nbr(ps, ps_r, 17).wait_recv()
    mine = pl.ds(pl.multiple_of(8 * c, 8), 8)
    plane_buf[t] = ps[mine, :] + ps_r[mine, :]
    copies = [
        remote(plane_buf.at[t], plane_buf.at[t], ssem.at[28 + k], rsem.at[28 + k], device)
        for k, device in enumerate(plane)
    ]
    for copy in copies:
        send(copy)
    reduce_rows(1)
    reduce_rows(0)
    for copy in copies:
        copy.wait_recv()
    z_buf[0] = plane_buf[0] + plane_buf[1] + plane_buf[2] + plane_buf[3]
    for k, device in enumerate(zs):
        copy = remote(z_buf.at[2 * k], z_buf.at[2 * k + 1], ssem.at[31 + k], rsem.at[31 + k], device)
        send(copy)
        copy.wait_recv()
        z_buf[2 * k + 2] = z_buf[2 * k] + z_buf[2 * k + 1]
    fin[mine, :] = z_buf[2 * len(zs)]
    send(to_nbr(fin.at[mine, :], fin.at[mine, :], 18))
    theirs = pl.ds(pl.multiple_of(8 - 8 * c, 8), 8)
    to_nbr(fin.at[theirs, :], fin.at[theirs, :], 18).wait_recv()
    result = pltpu.make_async_copy(fin, summed, load_sem.at[0])
    result.start()

    own_rows.wait()
    for first in (20, 22):
        for sender in range(2):
            place = pl.ds(128 * sender, 128)
            remote(
                bo_s.at[pl.ds(0, 128), :], bo_r.at[place, :], ssem.at[first], rsem.at[first + sender], dests[0]
            ).wait_recv()
    for sender in range(2):
        remote(chip_s.at[0], fin_r.at[sender], ssem.at[24], rsem.at[24 + sender], dests[0]).wait_recv()
    result.wait()
    drain()


def finish_kernel(
    norm_params, factors, first_moment, second_moment, bo_r, grf_in, fin_in, tok_in, sum_in,
    block_out, input_grad, clipped, grad_norm, factors_new, first_new, second_new,
    bo, grf, fin_r, tokr, summed, grads, sem, out_sem,
):
    pairs = [(sum_in, summed), (bo_r, bo)]
    for r in range(2):
        rows = pl.ds(128 * r, 128)
        pairs += [(ref.at[rows, :], to.at[rows, :]) for ref, to in ((tok_in, tokr), (grf_in, grf))]
        pairs.append((fin_in.at[:, rows, :], fin_r.at[:, rows, :]))
    loads = [pltpu.make_async_copy(*pair, sem.at[k]) for k, pair in enumerate(pairs)]
    for load in loads:
        load.start()
    loads[0].wait()

    grad = summed[...]
    norm = jnp.sqrt(jnp.sum(grad * grad, (0, 1), keepdims=True))
    grad_norm[...] = norm
    grad = grad * (CLIP_NORM / jnp.maximum(norm, CLIP_NORM))
    for index, first in enumerate((0, 8, 4, 12)):
        value, weights = grad[first : first + 4], factors[index]
        first_value = BETA_ONE * first_moment[index] + (1.0 - BETA_ONE) * value
        second_value = BETA_TWO * second_moment[index] + (1.0 - BETA_TWO) * value * value
        first_hat = first_value / (1.0 - BETA_ONE**STEP)
        second_hat = second_value / (1.0 - BETA_TWO**STEP)
        clipped[index] = value
        first_new[index] = first_value
        second_new[index] = second_value
        factors_new[index] = weights - LEARN_RATE * (
            first_hat / (jnp.sqrt(second_hat) + ADAM_EPSILON) + WEIGHT_DECAY * weights
        )
    loads[1].wait()
    stores = [pltpu.make_async_copy(bo, block_out, out_sem.at[2])]
    stores[0].start()
    for r in range(2):
        for load in loads[2 + 3 * r : 5 + 3 * r]:
            load.wait()
        half = pl.ds(128 * r, 128)

        @pl.loop(0, 2)
        def _(q):
            rows = pl.ds(pl.multiple_of(128 * r + q * 64, 64), 64)
            unit, inverse = unit_of(tokr[rows, :].astype(F32))
            scaled = (fin_r[0, rows, :].astype(F32) + fin_r[1, rows, :].astype(F32)) * norm_params[0:1, :]
            grads[rows, :] = grf[rows, :].astype(F32) + inverse * (
                scaled
                - jnp.mean(scaled, -1, keepdims=True)
                - unit * jnp.mean(scaled * unit, -1, keepdims=True)
            )

        stores.append(pltpu.make_async_copy(grads.at[half, :], input_grad.at[half, :], out_sem.at[r]))
        stores[-1].start()
    for store in stores:
        store.wait()


def fused(planes, tokens, norm_params, wqkv, w_out, w_fc, w_proj, factors, first, second, grad_out):
    vmem = pl.BlockSpec(memory_space=pltpu.VMEM)
    hbm = pl.BlockSpec(memory_space=pl.ANY)

    def buf(*shape, dtype=BF):
        return pltpu.VMEM(shape, dtype)

    def acc(*shape):
        return pltpu.VMEM(shape, F32)

    scratch = [
        buf(1024, 1024), buf(1024, 1024), buf(512, 1024), buf(3, 1024, 512), buf(512, 1024),
        buf(4, 2, 1024, 256), buf(4, 2, 256, 1024), buf(1024, 512), buf(1024, 512), buf(4, 256, 512),
        buf(4, 256, 256), buf(4, 256, 512), buf(4, 256, 768), buf(4, 256, 1024), buf(512, 512),
        acc(512, 1024), buf(256, 1024), buf(256, 1024),
        acc(256, 1024), buf(512, 1024), acc(512, 1024), acc(512, 1024),
        buf(256, 1024), buf(256, 1024), buf(256, 1024), buf(256, 1024), buf(512, 1024),
        buf(256, 1024),
        acc(1024, 512), acc(1024, 512), buf(128, 512), buf(4, 256, 512), acc(256, 1024),
        buf(4, 256, 1024), buf(2, 256, 1024), buf(2, 256, 1024),
        acc(128, 1024), buf(128, 1024), buf(128, 512), buf(128, 512), buf(1024, 128), acc(256, 128),
        acc(8, 1024), acc(8, 512), acc(16, 1024), acc(16, 1024), acc(4, 8, 1024), acc(2 * planes, 8, 1024),
        acc(16, 1024),
        pltpu.SemaphoreType.DMA((3, GROUPS)), pltpu.SemaphoreType.DMA((3, GROUPS)),
        pltpu.SemaphoreType.DMA((9,)), pltpu.SemaphoreType.DMA((31 + planes,)),
        pltpu.SemaphoreType.DMA((31 + planes,)),
    ]
    rows = jax.ShapeDtypeStruct((256, 1024), BF)
    passed = pl.pallas_call(
        functools.partial(fused_kernel, planes),
        name="block_step",
        out_shape=(
            rows, rows, jax.ShapeDtypeStruct((2, 256, 1024), BF), rows, jax.ShapeDtypeStruct((16, 1024), F32),
        ),
        in_specs=[hbm, vmem, hbm, hbm, hbm, hbm, vmem, hbm],
        out_specs=(hbm,) * 5,
        scratch_shapes=scratch,
        compiler_params=pltpu.CompilerParams(
            collective_id=1, has_side_effects=True, vmem_limit_bytes=62 << 20
        ),
    )(tokens, norm_params, wqkv, w_out, w_fc, w_proj, factors, grad_out)
    small = jax.ShapeDtypeStruct((4, 4, 1024), F32)
    outs = pl.pallas_call(
        finish_kernel,
        name="finish_step",
        out_shape=(
            rows, jax.ShapeDtypeStruct((256, 1024), F32), small,
            jax.ShapeDtypeStruct((1, 1), F32), small, small, small,
        ),
        in_specs=[vmem] * 4 + [hbm] * 5,
        out_specs=(hbm, hbm) + (vmem,) * 5,
        scratch_shapes=[
            buf(256, 1024), buf(256, 1024), buf(2, 256, 1024), buf(256, 1024), acc(16, 1024), acc(256, 1024),
            pltpu.SemaphoreType.DMA((8,)), pltpu.SemaphoreType.DMA((3,)),
        ],
        compiler_params=pltpu.CompilerParams(vmem_limit_bytes=62 << 20),
    )(norm_params, factors, first, second, *passed)
    return outs[:3] + (outs[3].reshape(()),) + outs[4:]


def solution(mesh):
    placed = (
        P("dp", None),
        P(),
        P(None, None, "tensor"),
        P("tensor", None),
        P(None, "tensor"),
        P("tensor", None),
        P(),
        P(),
        P(),
        P("dp", None),
    )
    planes = mesh.shape["dp"] // 2

    def step(*args):
        rows, width = args[0].shape
        shapes = (rows, width, args[4].shape[1], args[2].shape[2], args[6].shape[1])
        fits = mesh.shape["tensor"] == 4 and mesh.shape["dp"] % 4 == 0
        if fits and shapes == (SEQ, 1024, 1024, 256, 4):
            return fused(planes, *args)
        return body(*args)

    return jax.shard_map(
        step,
        mesh=mesh,
        in_specs=placed,
        out_specs=(P(("dp", "tensor"), None), P(("dp", "tensor"), None), P(), P(), P(), P(), P()),
        check_vma=False,
    )
```

```python
import functools

import jax
import jax.numpy as jnp
from jax import lax
from jax.experimental import pallas as pl
from jax.experimental.pallas import tpu as pltpu
from jax.sharding import PartitionSpec as P

HD = 64
SEQ = 1024
STEP = 5


EPSILON = 1e-05
ADAPTER_SCALING = 8.0
CLIP_NORM = 16.0
LEARN_RATE = 0.03
BETA_ONE = 0.5
BETA_TWO = 0.5
WEIGHT_DECAY = 0.01
ADAM_EPSILON = 1e-08
NEG_LARGE = -1e30
GELU_SCALE = 0.7978845608028654
GELU_CUBE = 0.044715


def matrix_product(left, right):
    return jnp.dot(left, right, preferred_element_type=jnp.float32)


def product_with_transpose(left, right):
    return lax.dot_general(
        left, right, (((1,), (1,)), ((), ())), preferred_element_type=jnp.float32
    )


def transpose_then_product(left, right):
    return lax.dot_general(
        left, right, (((0,), (0,)), ((), ())), preferred_element_type=jnp.float32
    )


def normalize(value_rows_local, gain_vec, bias_vec):
    centered = value_rows_local - jnp.mean(value_rows_local, -1, keepdims=True)
    inverse = lax.rsqrt(jnp.mean(centered * centered, -1, keepdims=True) + EPSILON)
    unit_rows = centered * inverse
    return (unit_rows * gain_vec + bias_vec, unit_rows, inverse)


def normalize_back(incoming, unit_rows, inverse, gain_vec):
    scaled = incoming * gain_vec
    return inverse * (
        scaled
        - jnp.mean(scaled, -1, keepdims=True)
        - unit_rows * jnp.mean(scaled * unit_rows, -1, keepdims=True)
    )


def causal_scores(query_block, key_all, block_index, block_len):
    scores = (
        jnp.einsum("bqhd,bkhd->bhqk", query_block, key_all, preferred_element_type=jnp.float32)
        * 0.125
    )
    query_pos = block_index * block_len + jnp.arange(block_len)
    allowed = jnp.arange(SEQ)[None, :] <= query_pos[:, None]
    return jnp.where(allowed, scores, NEG_LARGE)


def attention_forward(query_rows_local, key_all, value_all):
    block_len = min(512, SEQ)
    outputs = []
    logsums = []
    for block_index in range(SEQ // block_len):
        query_block = query_rows_local[:, block_index * block_len : (block_index + 1) * block_len]
        scores = causal_scores(query_block, key_all, block_index, block_len)
        row_max = jnp.max(scores, -1, keepdims=True)
        exponent = jnp.exp(scores - row_max)
        row_total = jnp.sum(exponent, -1, keepdims=True)
        probability = (exponent / row_total).astype(jnp.bfloat16)
        mixture = jnp.einsum(
            "bhqk,bkhd->bqhd", probability, value_all, preferred_element_type=jnp.float32
        )
        outputs.append(mixture.astype(jnp.bfloat16))
        logsums.append(row_max[..., 0] + jnp.log(row_total[..., 0]))
    return (jnp.concatenate(outputs, 1), jnp.concatenate(logsums, 2))


def attention_backward(query_rows_local, key_all, value_all, grad_mixture, logsums):
    block_len = min(512, SEQ)
    grad_queries = []
    grad_keys = jnp.zeros(key_all.shape, jnp.float32)
    value_gradient_rows = jnp.zeros(value_all.shape, jnp.float32)
    for block_index in range(SEQ // block_len):
        lower = block_index * block_len
        query_block = query_rows_local[:, lower : lower + block_len]
        grad_block = grad_mixture[:, lower : lower + block_len]
        scores = causal_scores(query_block, key_all, block_index, block_len)
        probability = jnp.exp(scores - logsums[:, :, lower : lower + block_len, None])
        grad_prob = jnp.einsum(
            "bqhd,bkhd->bhqk", grad_block, value_all, preferred_element_type=jnp.float32
        )
        row_delta = jnp.sum(grad_prob * probability, -1, keepdims=True)
        dscore = (0.125 * (probability * (grad_prob - row_delta))).astype(jnp.bfloat16)
        grad_queries.append(
            jnp.einsum(
                "bhqk,bkhd->bqhd", dscore, key_all, preferred_element_type=jnp.float32
            ).astype(jnp.bfloat16)
        )
        grad_keys = grad_keys + jnp.einsum(
            "bhqk,bqhd->bkhd", dscore, query_block, preferred_element_type=jnp.float32
        )
        value_gradient_rows = value_gradient_rows + jnp.einsum(
            "bhqk,bqhd->bkhd",
            probability.astype(jnp.bfloat16),
            grad_block,
            preferred_element_type=jnp.float32,
        )
    return (
        jnp.concatenate(grad_queries, 1),
        grad_keys.astype(jnp.bfloat16),
        value_gradient_rows.astype(jnp.bfloat16),
    )


def adam_step(factor_grad, weights, first_old, second_old, grad_norm):
    clipped = factor_grad * (CLIP_NORM / jnp.maximum(grad_norm, CLIP_NORM))
    first_new = BETA_ONE * first_old + (1.0 - BETA_ONE) * clipped
    second_new = BETA_TWO * second_old + (1.0 - BETA_TWO) * clipped * clipped
    first_hat = first_new / (1.0 - BETA_ONE**STEP)
    second_hat = second_new / (1.0 - BETA_TWO**STEP)
    weights_new = weights - LEARN_RATE * (
        first_hat / (jnp.sqrt(second_hat) + ADAM_EPSILON) + WEIGHT_DECAY * weights
    )
    return (clipped, weights_new, first_new, second_new)


def body(
    tokens_in,
    norm_params,
    query_key_value_weight,
    out_weight,
    fc_weight,
    proj_weight,
    factors,
    first_moment,
    second_moment,
    grad_out,
):
    tensor_size = lax.axis_size("tensor")
    tensor_rank = lax.axis_index("tensor")
    token_count = tokens_in.shape[0]
    doc_count = token_count // SEQ
    local_width = query_key_value_weight.shape[2]
    heads_here = local_width // HD
    row_count = token_count // tensor_size
    row_start = tensor_rank * row_count
    rank_count = factors.shape[1]
    full_width = factors.shape[2]
    inputs = tokens_in.astype(jnp.float32)
    first_normalized, unit_one, inverse_one = normalize(inputs, norm_params[0], norm_params[1])
    first_normalized_reduced = first_normalized.astype(jnp.bfloat16)
    factor_reduced_precision = factors.astype(jnp.bfloat16)
    column_offset = tensor_rank * local_width
    query_adapter_output = lax.dynamic_slice_in_dim(
        factor_reduced_precision[1], column_offset, local_width, 1
    )
    value_adapter_output = lax.dynamic_slice_in_dim(
        factor_reduced_precision[3], column_offset, local_width, 1
    )
    query_down_factor = product_with_transpose(
        first_normalized_reduced, factor_reduced_precision[0]
    ).astype(jnp.bfloat16)
    value_down_factor = product_with_transpose(
        first_normalized_reduced, factor_reduced_precision[2]
    ).astype(jnp.bfloat16)
    query_rows_local = (
        matrix_product(first_normalized_reduced, query_key_value_weight[0])
        + ADAPTER_SCALING * matrix_product(query_down_factor, query_adapter_output)
    ).astype(jnp.bfloat16)
    keys_low = matrix_product(first_normalized_reduced, query_key_value_weight[1]).astype(
        jnp.bfloat16
    )
    values_low = (
        matrix_product(first_normalized_reduced, query_key_value_weight[2])
        + ADAPTER_SCALING * matrix_product(value_down_factor, value_adapter_output)
    ).astype(jnp.bfloat16)
    head_shape = (doc_count, SEQ, heads_here, HD)
    query_heads = query_rows_local.reshape(head_shape)
    keys_heads = keys_low.reshape(head_shape)
    values_heads = values_low.reshape(head_shape)
    mixture, logsums = attention_forward(query_heads, keys_heads, values_heads)
    attn_part = matrix_product(mixture.reshape(token_count, local_width), out_weight)
    grad_full = grad_out.astype(jnp.float32)
    attn_rows = lax.psum_scatter(
        attn_part.astype(jnp.bfloat16), "tensor", scatter_dimension=0, tiled=True
    ).astype(jnp.float32)
    resid_rows = lax.dynamic_slice_in_dim(inputs, row_start, row_count, 0) + attn_rows
    normed_two_rows, unit_two, inverse_two = normalize(resid_rows, norm_params[2], norm_params[3])
    normed_two_low = lax.all_gather(
        normed_two_rows.astype(jnp.bfloat16), "tensor", axis=0, tiled=True
    )
    hidden_pre = matrix_product(normed_two_low, fc_weight)
    hidden_act, gelu_pull = jax.vjp(
        lambda argument: jax.nn.gelu(argument, approximate=True), hidden_pre
    )
    mlp_part = matrix_product(hidden_act.astype(jnp.bfloat16), proj_weight)
    grad_hidden = product_with_transpose(grad_out, proj_weight)
    grad_pre = gelu_pull(grad_hidden)[0].astype(jnp.bfloat16)
    second_part = product_with_transpose(grad_pre, fc_weight)
    out_rows = resid_rows + lax.psum_scatter(
        mlp_part.astype(jnp.bfloat16), "tensor", scatter_dimension=0, tiled=True
    ).astype(jnp.float32)
    second_rows = lax.psum_scatter(
        second_part.astype(jnp.bfloat16), "tensor", scatter_dimension=0, tiled=True
    ).astype(jnp.float32)
    resid_grad_rows = lax.dynamic_slice_in_dim(grad_full, row_start, row_count, 0) + normalize_back(
        second_rows, unit_two, inverse_two, norm_params[2]
    )
    resid_grad_low = lax.all_gather(
        resid_grad_rows.astype(jnp.bfloat16), "tensor", axis=0, tiled=True
    )
    grad_mixture = product_with_transpose(resid_grad_low, out_weight).astype(jnp.bfloat16)
    query_gradient, grad_keys, value_gradient_rows = attention_backward(
        query_heads, keys_heads, values_heads, grad_mixture.reshape(head_shape), logsums
    )
    query_gradient = query_gradient.reshape(token_count, local_width)
    grad_keys = grad_keys.reshape(token_count, local_width)
    value_gradient_rows = value_gradient_rows.reshape(token_count, local_width)
    stacked = jnp.stack((query_gradient, grad_keys, value_gradient_rows))
    first_part = jnp.einsum(
        "stc,sdc->td", stacked, query_key_value_weight, preferred_element_type=jnp.float32
    )
    query_up_factor = ADAPTER_SCALING * product_with_transpose(query_gradient, query_adapter_output)
    value_up_factor = ADAPTER_SCALING * product_with_transpose(
        value_gradient_rows, value_adapter_output
    )
    first_part = first_part + jnp.dot(
        query_up_factor,
        factor_reduced_precision[0].astype(jnp.float32),
        precision=lax.Precision.HIGHEST,
    )
    first_part = first_part + jnp.dot(
        value_up_factor,
        factor_reduced_precision[2].astype(jnp.float32),
        precision=lax.Precision.HIGHEST,
    )
    first_rows = lax.psum_scatter(
        first_part.astype(jnp.bfloat16), "tensor", scatter_dimension=0, tiled=True
    ).astype(jnp.float32)
    unit_rows = lax.dynamic_slice_in_dim(unit_one, row_start, row_count, 0)
    inverse_rows = lax.dynamic_slice_in_dim(inverse_one, row_start, row_count, 0)
    input_rows = resid_grad_rows + normalize_back(
        first_rows, unit_rows, inverse_rows, norm_params[0]
    )
    query_cross_term = transpose_then_product(query_gradient, first_normalized_reduced)
    value_cross_term = transpose_then_product(value_gradient_rows, first_normalized_reduced)
    query_down_gradient = ADAPTER_SCALING * jnp.dot(
        query_adapter_output.astype(jnp.float32), query_cross_term, precision=lax.Precision.HIGHEST
    )
    value_down_gradient = ADAPTER_SCALING * jnp.dot(
        value_adapter_output.astype(jnp.float32), value_cross_term, precision=lax.Precision.HIGHEST
    )
    empty_slot = jnp.zeros((rank_count, full_width), jnp.float32)
    up_grad_query = lax.dynamic_update_slice_in_dim(
        empty_slot,
        ADAPTER_SCALING * transpose_then_product(query_down_factor, query_gradient),
        column_offset,
        1,
    )
    up_grad_value = lax.dynamic_update_slice_in_dim(
        empty_slot,
        ADAPTER_SCALING * transpose_then_product(value_down_factor, value_gradient_rows),
        column_offset,
        1,
    )
    partial_grad = jnp.stack(
        (query_down_gradient, up_grad_query, value_down_gradient, up_grad_value)
    )
    reduced = lax.psum(partial_grad, ("dp", "tensor"))
    grad_norm = jnp.sqrt(jnp.sum(reduced * reduced))
    clipped, weights_new, first_new, second_new = adam_step(
        reduced, factors, first_moment, second_moment, grad_norm
    )
    return (
        out_rows.astype(jnp.bfloat16),
        input_rows,
        clipped,
        grad_norm,
        weights_new,
        first_new,
        second_new,
    )


MESH = pl.DeviceIdType.MESH
BF = jnp.bfloat16
F32 = jnp.float32
GROUPS = 8
PAIRS = 8


def mm(left, right):
    return jnp.dot(left, right, preferred_element_type=F32)


def mm_nt(left, right):
    return lax.dot_general(left, right, (((1,), (1,)), ((), ())), preferred_element_type=F32)


def mm_tn(left, right):
    return lax.dot_general(left, right, (((0,), (0,)), ((), ())), preferred_element_type=F32)


def flip(value, bit):
    return value + bit - 2 * bit * ((value // bit) % 2)


def unit_of(rows):
    centered = rows - jnp.mean(rows, -1, keepdims=True)
    inverse = lax.rsqrt(jnp.mean(centered * centered, -1, keepdims=True) + EPSILON)
    return centered * inverse, inverse


def unit_back(scaled, unit, inverse):
    return inverse * (
        scaled - jnp.mean(scaled, -1, keepdims=True) - unit * jnp.mean(scaled * unit, -1, keepdims=True)
    )


def fused_kernel(
    planes,
    tokens, norm_params, wqkv, w_out, w_fc, w_proj, factors, grad_out,
    bo_r, ig_r, summed,
    tok, n1, go, wq, wkv, wo, fcw, pw, kv, qs, p0, p1, mix, inv, attn_own, attn_s, attn_r,
    res, n2, acc_a, acc_b, gnt_s, gnt_r, gnt_xs, gnt_xr, mlp_s, mlp_r, mlp_xs, mlp_xr,
    gr, gr_b, bo_s, gq, dos, gno_s, gno_r, gno_xs, gno_xr, ig_s,
    fpad, f02, f1p, f3kv, down, gd_scr, fg_a, fg_q, fg_v, ps, ps_r, plane_buf, z_buf, fin,
    chain_send, chain_recv, pair_send, pair_recv, load_sem, ssem, rsem,
):
    d = lax.axis_index("dp")
    t = lax.axis_index("tensor")
    z, c, x, y = d // 2, d % 2, t % 2, t // 2
    odd = z % 2
    nbr = (flip(d, 1), t)
    prim = (d, flip(t, 1 + odd))
    sec = (d, flip(t, 2 - odd))
    plane = [(d, flip(t, 1)), (d, flip(t, 2)), (d, 3 - t)]
    x_nbr, y_nbr = plane[0], plane[1]
    zs = [(flip(d, 2 << k), t) for k in range(planes.bit_length() - 1)]
    owner = (2 * z + y, 2 * c + x)
    quarter = [t, flip(t, 1 + odd), flip(t, 2 - odd), 3 - t]
    column = [pl.multiple_of(q * 256 + c * 128, 128) for q in quarter]

    def at(start, size):
        return pl.ds(pl.multiple_of(start, size), size)

    def rows_of(half, side):
        return at(512 * half + 256 * side, 256)

    mine, mine_x = rows_of(c, x), rows_of(c, 1 - x)

    def remote(src, dst, index, device):
        return pltpu.make_async_remote_copy(
            src_ref=src, dst_ref=dst, send_sem=ssem.at[index], recv_sem=rsem.at[index],
            device_id=device, device_id_type=MESH,
        )

    pending = []

    def drain():
        for wait in pending:
            wait()

    def send(copy):
        copy.start()
        pending.append(copy.wait_send)
        return copy

    lane = at(c * 128, 128)
    loads = [
        pltpu.make_async_copy(wqkv.at[1, :, lane], wkv.at[:, pl.ds(0, 128)], load_sem.at[0]),
        pltpu.make_async_copy(wqkv.at[2, :, lane], wkv.at[:, pl.ds(128, 128)], load_sem.at[1]),
        pltpu.make_async_copy(wqkv.at[0, :, lane], wq.at[:, pl.ds(0, 128)], load_sem.at[2]),
        pltpu.make_async_copy(w_out.at[lane, :], wo.at[pl.ds(0, 128), :], load_sem.at[3]),
        pltpu.make_async_copy(w_fc.at[:, at(c * 512, 512)], fcw.at[0], load_sem.at[4]),
        pltpu.make_async_copy(w_proj.at[at(c * 512, 512), :], pw.at[0], load_sem.at[5]),
    ]
    for load in loads:
        load.start()

    barrier = pltpu.get_barrier_semaphore()
    partners = [nbr, x_nbr, y_nbr] + zs
    for device in partners:
        pl.semaphore_signal(barrier, inc=1, device_id=device, device_id_type=MESH)
    pl.semaphore_wait(barrier, len(partners))

    doc = []
    for first, source, target in ((0, tokens, tok), (4, grad_out, go)):
        for r in range(4):
            part = pl.ds(256 * r, 256)
            doc.append((source.at[part, :], target.at[part, :], first + r))

    @pl.when(c == y)
    def _():
        for src, dst, index in doc:
            remote(src, dst, index, nbr).start()
            pltpu.make_async_copy(src, dst, rsem.at[index]).start()

    def doc_sent():
        @pl.when(c == y)
        def _():
            for item in doc:
                remote(*item, nbr).wait_send()

    pending.append(doc_sent)

    def doc_wait(index):
        remote(*doc[index], nbr).wait_recv()

    def piece(slot, group):
        matrix, a = group // 2, group % 2
        if matrix < 2:
            return wkv.at[pl.ds(512 * a, 512), pl.ds(256 * slot + 128 * matrix, 128)]
        if matrix == 2:
            return wq.at[pl.ds(512 * a, 512), pl.ds(128 * slot, 128)]
        return wo.at[pl.ds(128 * slot + 64 * a, 64), :]

    def hop(slot, group):
        return pltpu.make_async_remote_copy(
            src_ref=piece(1 if slot > 1 else 0, group), dst_ref=piece(slot, group),
            send_sem=chain_send.at[slot - 1, group], recv_sem=chain_recv.at[slot - 1, group],
            device_id=(prim, zs[0], sec)[slot - 1], device_id_type=MESH,
        )

    def pump(group):
        hop(1, group).wait_recv()
        send(hop(2, group))
        send(hop(3, group))

    def passed(groups):
        for group in groups:
            hop(2, group).wait_recv()
            hop(3, group).wait_recv()

    def pair_piece(slot, pair, parity):
        h, q = pair // 4, pair % 4
        if q < 2:
            return fcw.at[slot, at(512 * q + 256 * parity, 256), pl.ds(256 * h, 256)]
        return pw.at[slot, at(256 * h + 128 * (q - 2) + 64 * parity, 64), :]

    def pair_hop(step, pair, parity):
        return pltpu.make_async_remote_copy(
            src_ref=pair_piece(step, pair, parity), dst_ref=pair_piece(1, pair, parity),
            send_sem=pair_send.at[step, pair], recv_sem=pair_recv.at[step, pair],
            device_id=(y_nbr, zs[0])[step], device_id_type=MESH,
        )

    def pair_pump(pair):
        pair_hop(0, pair, odd).wait_recv()
        send(pair_hop(1, pair, odd))

    def pair_wait(pairs):
        for pair in pairs:
            pair_hop(1, pair, 1 - odd).wait_recv()

    for load in loads:
        load.wait()
    for group in range(GROUPS):
        send(hop(1, group))

    fpad[...] = jnp.zeros_like(fpad)
    fpad[0:4, :] = factors[0]
    fpad[4:8, :] = factors[2]
    f02[...] = fpad[...].astype(BF)
    fpad[...] = jnp.zeros_like(fpad)
    for s in range(4):
        fpad[0:4, 128 * s : 128 * s + 128] = factors[1, :, pl.ds(column[s], 128)]
    f1p[...] = fpad[:, :512].astype(BF)
    fpad[...] = jnp.zeros_like(fpad)
    for s in range(4):
        fpad[4:8, 256 * s + 128 : 256 * s + 256] = factors[3, :, pl.ds(column[s], 128)]
    f3kv[...] = fpad[...].astype(BF)
    ps[...] = jnp.zeros_like(ps)

    gain_one, bias_one = norm_params[0:1, :], norm_params[1:2, :]
    gain_two, bias_two = norm_params[2:3, :], norm_params[3:4, :]
    for r in range(4):
        doc_wait(r)

        @pl.loop(0, 2)
        def _(q):
            rows = at(256 * r + 128 * q, 128)
            unit, _ = unit_of(tok[rows, :].astype(F32))
            n1[rows, :] = (unit * gain_one + bias_one).astype(BF)

    pump(0)
    for r in range(2):
        rows = slice(512 * r, 512 * r + 512)
        down[rows, :] = mm_nt(n1[rows, :], f02[...]).astype(BF)
    pump(1)

    first_head = lax.broadcasted_iota(jnp.int32, (256, 512), 1) % 128 < 64
    first_lanes = first_head[:, 0:128]

    def stacked(rows, lanes):
        return jnp.concatenate((jnp.where(lanes, rows, 0.0), jnp.where(lanes, 0.0, rows)), 0)

    def project_keys(s):
        lanes = slice(256 * s, 256 * s + 256)
        for r in range(2):
            rows = slice(512 * r, 512 * r + 512)
            kv[rows, lanes] = (
                mm(n1[rows, :], wkv[:, lanes]) + ADAPTER_SCALING * mm(down[rows, :], f3kv[:, lanes])
            ).astype(BF)

    def project_queries(s):
        lanes = slice(128 * s, 128 * s + 128)
        for h in range(2):
            rows = rows_of(h, x)
            query = mm(n1[rows, :], wq[:, lanes]) + ADAPTER_SCALING * mm(down[rows, :], f1p[:, lanes])
            qs[h, :, lanes] = stacked(query.astype(BF).astype(F32) * 0.125, first_lanes).astype(BF)

    p_refs = (p0, p1)
    column_pos = lax.broadcasted_iota(jnp.int32, (512, 512), 1)
    row_pos = lax.broadcasted_iota(jnp.int32, (512, 512), 0) % 256 + 256 * x
    allowed = column_pos <= row_pos

    def attend(s):
        keys, values = slice(256 * s, 256 * s + 128), slice(256 * s + 128, 256 * s + 256)
        lanes = slice(128 * s, 128 * s + 128)
        scores = [mm_nt(qs[h, :, lanes], kv[0 : 512 * (h + 1), keys]) for h in range(2)]
        kept = []
        for h in range(2):
            last = jnp.where(allowed, scores[h][:, 512 * h :], NEG_LARGE)
            block = jnp.concatenate((scores[h][:, :512], last), 1) if h else last
            exponent = jnp.exp(block - jnp.max(block, -1, keepdims=True))
            inverse = 1.0 / jnp.sum(exponent, -1, keepdims=True)
            p_refs[h][s] = exponent.astype(BF)
            inv[h, :, lanes] = jnp.broadcast_to(inverse, (512, 128))
            kept.append((exponent.astype(BF), inverse))
        for h in range(2):
            both = mm(kept[h][0], kv[0 : 512 * (h + 1), values]) * kept[h][1]
            mix[256 * h : 256 * h + 256, lanes] = jnp.where(first_lanes, both[0:256], both[256:512])

    project_keys(0)
    pump(2)
    project_queries(0)
    attend(0)
    pump(3)
    project_keys(1)
    pump(4)
    passed(range(0, 4))
    project_keys(2)
    project_keys(3)
    pump(5)
    project_queries(1)
    attend(1)
    pump(6)
    passed(range(4, 6))
    project_queries(2)
    project_queries(3)
    pump(7)
    for pair in range(PAIRS):
        send(pair_hop(0, pair, odd))
    attend(2)
    attend(3)
    passed(range(6, 8))

    attn_s[...] = mm(mix[at(256 - 256 * c, 256), :].astype(BF), wo[...]).astype(BF)
    to_nbr = send(remote(attn_s, attn_r, 8, nbr))
    attn_own[...] = mm(mix[at(256 * c, 256), :].astype(BF), wo[...])
    to_nbr.wait_recv()

    def part_of(start, j):
        return at(start + 128 * j, 128)

    own_start, own_start_x = 512 * c + 256 * x, 512 * c + 256 * (1 - x)
    gathered = []
    for j in range(2):
        part = slice(128 * j, 128 * j + 128)
        rows = part_of(own_start, j)
        residual = tok[rows, :].astype(F32) + attn_own[part, :] + attn_r[part, :].astype(F32)
        res[part, :] = residual
        unit, _ = unit_of(residual)
        n2[rows, :] = (unit * gain_two + bias_two).astype(BF)
        gathered.append(send(remote(n2.at[rows, :], n2.at[rows, :], 11 + j, x_nbr)))
        gathered.append(send(remote(n2.at[rows, :], n2.at[rows, :], 9 + j, nbr)))
    for r in range(4):
        doc_wait(4 + r)

    def feed_forward(slot, side, lanes, first):
        tiles = [rows_of(h, side) for h in range(2)]
        pre = [mm(n2[rows, :], fcw[slot, :, lanes]) for rows in tiles]
        grad_act = [mm_nt(go[rows, :], pw[slot, lanes, :]) for rows in tiles]
        for rows, hidden, grad in zip(tiles, pre, grad_act):
            square = hidden * hidden
            tanh = jnp.tanh(GELU_SCALE * hidden * (1.0 + GELU_CUBE * square))
            half_up = 0.5 * (1.0 + tanh)
            slope = half_up + (0.5 * GELU_SCALE) * hidden * (1.0 - tanh * tanh) * (
                1.0 + 3.0 * GELU_CUBE * square
            )
            out = mm((hidden * half_up).astype(BF), pw[slot, lanes, :])
            back = mm_nt((grad * slope).astype(BF), fcw[slot, :, lanes])
            acc_a[rows, :] = out if first else acc_a[rows, :] + out
            acc_b[rows, :] = back if first else acc_b[rows, :] + back

    every, lower, upper = slice(0, 512), slice(0, 256), slice(256, 512)
    pair_pump(0)
    gathered[1].wait_recv()
    gathered[3].wait_recv()
    feed_forward(0, x, every, True)
    pair_pump(1)
    pair_pump(2)

    def pass_on(j):
        gathered[2 * j].wait_recv()
        rows = part_of(own_start_x, j)
        return send(remote(n2.at[rows, :], n2.at[rows, :], 13 + j, nbr))

    forwarded = [pass_on(0)]
    pair_pump(3)
    pair_pump(4)
    forwarded.append(pass_on(1))
    pair_pump(5)
    pair_wait(range(0, 4))
    feed_forward(1, x, lower, False)
    pair_pump(6)
    for copy in forwarded:
        copy.wait_recv()
    feed_forward(0, 1 - x, every, True)
    pair_pump(7)
    feed_forward(1, 1 - x, lower, False)
    pair_wait(range(4, 8))
    feed_forward(1, 1 - x, upper, False)

    def to_core(acc, source, target, first, j):
        side = (1 - x) if j == 0 else x
        part = pl.ds(256 * j, 256)
        source[part, :] = acc[rows_of(1 - c, side), :].astype(BF)
        return send(remote(source.at[part, :], target.at[part, :], first + j, nbr))

    def to_side(acc, target, out, out_target, first, j):
        part = slice(128 * j, 128 * j + 128)
        out[part, :] = (acc[part_of(own_start_x, j), :] + target[part, :].astype(F32)).astype(BF)
        return send(remote(out.at[part, :], out_target.at[part, :], first + j, x_nbr))

    gnt_core = [to_core(acc_b, gnt_s, gnt_r, 15, 0)]
    feed_forward(1, x, upper, False)
    gnt_core.append(to_core(acc_b, gnt_s, gnt_r, 15, 1))
    gnt_core[0].wait_recv()
    gnt_side = [to_side(acc_b, gnt_r, gnt_xs, gnt_xr, 17, j) for j in range(2)]
    mlp_core = [to_core(acc_a, mlp_s, mlp_r, 19, j) for j in range(2)]
    mlp_core[0].wait_recv()
    mlp_side = [to_side(acc_a, mlp_r, mlp_xs, mlp_xr, 21, j) for j in range(2)]
    mlp_core[1].wait_recv()
    for j in range(2):
        part = slice(128 * j, 128 * j + 128)
        gr[part, :] = (
            res[part, :] + acc_a[part_of(own_start, j), :] + mlp_r[256 + 128 * j : 384 + 128 * j, :].astype(F32)
        )
    gnt_core[1].wait_recv()
    mixed = []
    for j in range(2):
        part = slice(128 * j, 128 * j + 128)
        rows = part_of(own_start, j)
        total = acc_b[rows, :] + gnt_r[256 + 128 * j : 384 + 128 * j, :].astype(F32)
        unit, inverse = unit_of(res[part, :])
        gnt_side[j].wait_recv()
        scaled = (total + gnt_xr[part, :].astype(F32)) * gain_two
        grad = go[rows, :].astype(F32) + unit_back(scaled, unit, inverse)
        res[part, :] = gr[part, :]
        gr[part, :] = grad
        local = part_of(256 * c, j)
        gr_b[local, :] = grad.astype(BF)
        mixed.append(send(remote(gr_b.at[local, :], gr_b.at[local, :], 23 + j, nbr)))

    for copy in mixed:
        copy.wait_recv()
    for h in range(2):
        grad_mixture = mm_nt(gr_b[256 * h : 256 * h + 256, :], wo[...])
        dos[h] = (stacked(grad_mixture, first_head) * inv[h]).astype(BF)

    def scores_back(h, group):
        size = 512 * (h + 1)
        grads = [dos[h, :, 128 * s : 128 * s + 128] for s in group]
        grad_prob = [
            mm_nt(grad, kv[0:size, 256 * s + 128 : 256 * s + 256]) for s, grad in zip(group, grads)
        ]
        dscores = []
        for s, grad, block in zip(group, grads, grad_prob):
            mixture = mix[256 * h : 256 * h + 256, 128 * s : 128 * s + 128]
            delta = jnp.sum(
                grad.astype(F32) * jnp.concatenate((mixture, mixture), 0), -1, keepdims=True
            )
            dscores.append((p_refs[h][s].astype(F32) * (block - delta)).astype(BF))
        for s, grad, dscore in zip(group, grads, dscores):
            lanes = slice(128 * s, 128 * s + 128)
            both = 0.125 * mm(dscore, kv[0:size, 256 * s : 256 * s + 128])
            gq[:, lanes] = jnp.where(first_lanes, both[0:256], both[256:512]).astype(BF)
            grad_keys = mm_tn(dscore, qs[h, :, lanes])
            grad_values = mm_tn(p_refs[h][s], grad)
            k_lanes, v_lanes = slice(256 * s, 256 * s + 128), slice(256 * s + 128, 256 * s + 256)
            if h:
                acc_a[:, k_lanes] = grad_keys
                acc_a[:, v_lanes] = grad_values
            else:
                acc_a[0:512, k_lanes] += grad_keys
                acc_a[0:512, v_lanes] += grad_values

    def factors_back(h):
        rows = slice(512 * h, 512 * h + 512)
        grads = acc_a[rows, :].astype(BF)
        query = gq[...]
        gd_scr[...] = ADAPTER_SCALING * mm_nt(grads, f3kv[...])
        gd_scr[at(256 * x, 256), :] += ADAPTER_SCALING * mm_nt(query, f1p[...])
        terms = (
            mm_tn(gd_scr[...].astype(BF), n1[rows, :])[0:8],
            mm_tn(down[rows_of(h, x), :], query)[0:8],
            mm_tn(down[rows, :], grads)[0:8],
        )
        for total, term in zip((fg_a, fg_q, fg_v), terms):
            total[...] = term if h else total[...] + term

    def rows_back(h):
        for j, side in enumerate((1 - x, x)):
            rows = rows_of(h, side)
            part = slice(256 * j, 256 * j + 256)
            grad = mm_nt(acc_a[rows, :].astype(BF), wkv[...])
            grad += mm(gd_scr[at(256 * side, 256), :].astype(BF), f02[...])
            if j:
                grad += mm_nt(gq[...], wq[...])
            acc_b[part, :] = grad

            @pl.when(c != h)
            def _():
                gno_s[part, :] = acc_b[part, :].astype(BF)
                remote(gno_s.at[part, :], gno_r.at[part, :], 27 + j, nbr).start()

    def gno_sent():
        for j in range(2):
            part = slice(256 * j, 256 * j + 256)
            remote(gno_s.at[part, :], gno_r.at[part, :], 27 + j, nbr).wait_send()

    pending.append(gno_sent)

    def side_copy(j):
        part = slice(128 * j, 128 * j + 128)
        return remote(gno_xs.at[part, :], gno_xr.at[part, :], 31 + j, x_nbr)

    def reduce_rows(h):
        @pl.when(c == h)
        def _():
            for j in range(2):
                part = slice(256 * j, 256 * j + 256)
                remote(gno_s.at[part, :], gno_r.at[part, :], 27 + j, nbr).wait_recv()
                acc_b[part, :] += gno_r[part, :].astype(F32)
                if j == 0:
                    for k in range(2):
                        half = slice(128 * k, 128 * k + 128)
                        gno_xs[half, :] = acc_b[half, :].astype(BF)
                        side_copy(k).start()
            acc_b[512:768, :] = acc_b[256:512, :]

    pending.append(side_copy(0).wait_send)
    pending.append(side_copy(1).wait_send)

    def to_owner(src, dst, index):
        @pl.when(c == y)
        def _():
            pltpu.make_async_copy(src, dst, rsem.at[index]).start()

        @pl.when(c != y)
        def _():
            remote(src, dst, index, owner).start()

        def sent():
            @pl.when(c != y)
            def _():
                remote(src, dst, index, owner).wait_send()

        return sent

    def input_rows(h):
        @pl.when(c == h)
        def _():
            for j in range(2):
                part = slice(128 * j, 128 * j + 128)
                unit, inverse = unit_of(tok[part_of(own_start, j), :].astype(F32))
                side_copy(j).wait_recv()
                scaled = (acc_b[512 + 128 * j : 640 + 128 * j, :] + gno_xr[part, :].astype(F32)) * gain_one
                ig_s[part, :] = (gr[part, :] + unit_back(scaled, unit, inverse)).astype(BF)
                to_owner(ig_s.at[part, :], ig_r.at[part, :], 25 + j)

    def rows_sent():
        @pl.when(c != y)
        def _():
            for j in range(2):
                part = slice(128 * j, 128 * j + 128)
                remote(ig_s.at[part, :], ig_r.at[part, :], 25 + j, owner).wait_send()

    pending.append(rows_sent)

    scores_back(1, (0, 1))
    scores_back(1, (2, 3))
    factors_back(1)
    rows_back(1)

    for j in range(2):
        mlp_side[j].wait_recv()
    bo_s[...] = (res[...] + mlp_xr[...].astype(F32)).astype(BF)
    pending.append(to_owner(bo_s, bo_r, 29))

    reduce_rows(1)
    scores_back(0, (0, 1, 2, 3))
    factors_back(0)

    ps[0:8, :] = fg_a[...]
    down_rows = lax.broadcasted_iota(jnp.int32, (8, 128), 0) < 4
    for s in range(4):
        ps[8:16, pl.ds(column[s], 128)] = ADAPTER_SCALING * jnp.where(
            down_rows, fg_q[:, 128 * s : 128 * s + 128], fg_v[:, 256 * s + 128 : 256 * s + 256]
        )
    core_sum = send(remote(ps, ps_r, 33, nbr))
    rows_back(0)
    core_sum.wait_recv()
    eight = at(8 * c, 8)
    plane_buf[t] = ps[eight, :] + ps_r[eight, :]
    copies = [
        send(remote(plane_buf.at[t], plane_buf.at[t], 35 + k, device)) for k, device in enumerate(plane)
    ]
    reduce_rows(0)
    input_rows(1)
    for copy in copies:
        copy.wait_recv()
    z_buf[0] = plane_buf[0] + plane_buf[1] + plane_buf[2] + plane_buf[3]
    for k, device in enumerate(zs):
        copy = send(remote(z_buf.at[2 * k], z_buf.at[2 * k + 1], 38 + k, device))
        copy.wait_recv()
        z_buf[2 * k + 2] = z_buf[2 * k] + z_buf[2 * k + 1]
    fin[eight, :] = z_buf[2 * len(zs)]
    send(remote(fin.at[eight, :], fin.at[eight, :], 34, nbr))
    input_rows(0)
    theirs = at(8 - 8 * c, 8)
    remote(fin.at[theirs, :], fin.at[theirs, :], 34, nbr).wait_recv()
    result = pltpu.make_async_copy(fin, summed, load_sem.at[0])
    result.start()

    remote(bo_s, bo_r, 29, owner).wait_recv()
    for j in range(2):
        part = slice(128 * j, 128 * j + 128)
        remote(ig_s.at[part, :], ig_r.at[part, :], 25 + j, owner).wait_recv()
    result.wait()
    drain()


def finish_kernel(
    factors, first_moment, second_moment, bo_in, ig_in, sum_in,
    block_out, input_grad, clipped, grad_norm, factors_new, first_new, second_new,
    bo, ig, summed, grads, sem, out_sem,
):
    pairs = [(sum_in, summed), (bo_in, bo), (ig_in, ig)]
    loads = [pltpu.make_async_copy(*pair, sem.at[k]) for k, pair in enumerate(pairs)]
    for load in loads:
        load.start()
    loads[0].wait()
    grad = summed[...]
    norm = jnp.sqrt(jnp.sum(grad * grad, (0, 1), keepdims=True))
    grad_norm[...] = norm
    grad = grad * (CLIP_NORM / jnp.maximum(norm, CLIP_NORM))
    for index, first in enumerate((0, 8, 4, 12)):
        value, weights = grad[first : first + 4], factors[index]
        first_value = BETA_ONE * first_moment[index] + (1.0 - BETA_ONE) * value
        second_value = BETA_TWO * second_moment[index] + (1.0 - BETA_TWO) * value * value
        first_hat = first_value / (1.0 - BETA_ONE**STEP)
        second_hat = second_value / (1.0 - BETA_TWO**STEP)
        clipped[index] = value
        first_new[index] = first_value
        second_new[index] = second_value
        factors_new[index] = weights - LEARN_RATE * (
            first_hat / (jnp.sqrt(second_hat) + ADAM_EPSILON) + WEIGHT_DECAY * weights
        )
    loads[1].wait()
    stores = [pltpu.make_async_copy(bo, block_out, out_sem.at[0])]
    stores[0].start()
    loads[2].wait()
    grads[...] = ig[...].astype(F32)
    stores.append(pltpu.make_async_copy(grads, input_grad, out_sem.at[1]))
    stores[1].start()
    for store in stores:
        store.wait()


def fused(planes, tokens, norm_params, wqkv, w_out, w_fc, w_proj, factors, first, second, grad_out):
    vmem = pl.BlockSpec(memory_space=pltpu.VMEM)
    hbm = pl.BlockSpec(memory_space=pl.ANY)

    def buf(*shape):
        return pltpu.VMEM(shape, BF)

    def acc(*shape):
        return pltpu.VMEM(shape, F32)

    def sems(*shape):
        return pltpu.SemaphoreType.DMA(shape)

    quarter = [buf(256, 1024)] * 2
    scratch = [
        buf(1024, 1024), buf(1024, 1024), buf(1024, 1024), buf(1024, 512), buf(1024, 1024), buf(512, 1024),
        buf(2, 1024, 512), buf(2, 512, 1024), buf(1024, 1024), buf(2, 512, 512), buf(4, 512, 512),
        buf(4, 512, 1024), acc(512, 512), acc(2, 512, 512), acc(256, 1024), *quarter,
        acc(256, 1024), buf(1024, 1024), acc(1024, 1024), acc(1024, 1024),
        buf(512, 1024), buf(512, 1024), *quarter, buf(512, 1024), buf(512, 1024), *quarter,
        acc(256, 1024), buf(512, 1024), buf(256, 1024), buf(256, 512), buf(2, 512, 512),
        buf(512, 1024), buf(512, 1024), *quarter, buf(256, 1024),
        acc(128, 1024), buf(128, 1024), buf(128, 512), buf(128, 1024), buf(1024, 128), acc(512, 128),
        acc(8, 1024), acc(8, 512), acc(8, 1024), acc(16, 1024), acc(16, 1024), acc(4, 8, 1024),
        acc(2 * planes, 8, 1024), acc(16, 1024),
        sems(3, GROUPS), sems(3, GROUPS), sems(2, PAIRS), sems(2, PAIRS), sems(6), sems(38 + planes),
        sems(38 + planes),
    ]
    rows = jax.ShapeDtypeStruct((256, 1024), BF)
    passed = pl.pallas_call(
        functools.partial(fused_kernel, planes),
        name="block_step",
        out_shape=(rows, rows, jax.ShapeDtypeStruct((16, 1024), F32)),
        in_specs=[hbm, vmem, hbm, hbm, hbm, hbm, vmem, hbm],
        out_specs=(hbm,) * 3,
        scratch_shapes=scratch,
        compiler_params=pltpu.CompilerParams(
            collective_id=1, has_side_effects=True, vmem_limit_bytes=63 << 20
        ),
    )(tokens, norm_params, wqkv, w_out, w_fc, w_proj, factors, grad_out)
    small = jax.ShapeDtypeStruct((4, 4, 1024), F32)
    outs = pl.pallas_call(
        finish_kernel,
        name="finish_step",
        out_shape=(
            rows, jax.ShapeDtypeStruct((256, 1024), F32), small,
            jax.ShapeDtypeStruct((1, 1), F32), small, small, small,
        ),
        in_specs=[vmem] * 3 + [hbm] * 3,
        out_specs=(hbm, hbm) + (vmem,) * 5,
        scratch_shapes=[*quarter, acc(16, 1024), acc(256, 1024), sems(3), sems(2)],
        compiler_params=pltpu.CompilerParams(vmem_limit_bytes=62 << 20),
    )(factors, first, second, *passed)
    return outs[:3] + (outs[3].reshape(()),) + outs[4:]


def solution(mesh):
    placed = (
        P("dp", None),
        P(),
        P(None, None, "tensor"),
        P("tensor", None),
        P(None, "tensor"),
        P("tensor", None),
        P(),
        P(),
        P(),
        P("dp", None),
    )
    planes = mesh.shape["dp"] // 2

    def step(*args):
        rows, width = args[0].shape
        shapes = (rows, width, args[4].shape[1], args[2].shape[2], args[6].shape[1])
        fits = mesh.shape["tensor"] == 4 and mesh.shape["dp"] % 4 == 0
        if fits and shapes == (SEQ, 1024, 1024, 256, 4):
            return fused(planes, *args)
        return body(*args)

    return jax.shard_map(
        step,
        mesh=mesh,
        in_specs=placed,
        out_specs=(P(("dp", "tensor"), None), P(("dp", "tensor"), None), P(), P(), P(), P(), P()),
        check_vma=False,
    )
```

```python
import functools

import jax
import jax.numpy as jnp
from jax import lax
from jax.experimental import pallas as pl
from jax.experimental.pallas import tpu as pltpu
from jax.sharding import PartitionSpec as P

HD = 64
SEQ = 1024
STEP = 5


EPSILON = 1e-05
ADAPTER_SCALING = 8.0
CLIP_NORM = 16.0
LEARN_RATE = 0.03
BETA_ONE = 0.5
BETA_TWO = 0.5
WEIGHT_DECAY = 0.01
ADAM_EPSILON = 1e-08
NEG_LARGE = -1e30
GELU_SCALE = 0.7978845608028654
GELU_CUBE = 0.044715


def matrix_product(left, right):
    return jnp.dot(left, right, preferred_element_type=jnp.float32)


def product_with_transpose(left, right):
    return lax.dot_general(
        left, right, (((1,), (1,)), ((), ())), preferred_element_type=jnp.float32
    )


def transpose_then_product(left, right):
    return lax.dot_general(
        left, right, (((0,), (0,)), ((), ())), preferred_element_type=jnp.float32
    )


def normalize(value_rows_local, gain_vec, bias_vec):
    centered = value_rows_local - jnp.mean(value_rows_local, -1, keepdims=True)
    inverse = lax.rsqrt(jnp.mean(centered * centered, -1, keepdims=True) + EPSILON)
    unit_rows = centered * inverse
    return (unit_rows * gain_vec + bias_vec, unit_rows, inverse)


def normalize_back(incoming, unit_rows, inverse, gain_vec):
    scaled = incoming * gain_vec
    return inverse * (
        scaled
        - jnp.mean(scaled, -1, keepdims=True)
        - unit_rows * jnp.mean(scaled * unit_rows, -1, keepdims=True)
    )


def causal_scores(query_block, key_all, block_index, block_len):
    scores = (
        jnp.einsum("bqhd,bkhd->bhqk", query_block, key_all, preferred_element_type=jnp.float32)
        * 0.125
    )
    query_pos = block_index * block_len + jnp.arange(block_len)
    allowed = jnp.arange(SEQ)[None, :] <= query_pos[:, None]
    return jnp.where(allowed, scores, NEG_LARGE)


def attention_forward(query_rows_local, key_all, value_all):
    block_len = min(512, SEQ)
    outputs = []
    logsums = []
    for block_index in range(SEQ // block_len):
        query_block = query_rows_local[:, block_index * block_len : (block_index + 1) * block_len]
        scores = causal_scores(query_block, key_all, block_index, block_len)
        row_max = jnp.max(scores, -1, keepdims=True)
        exponent = jnp.exp(scores - row_max)
        row_total = jnp.sum(exponent, -1, keepdims=True)
        probability = (exponent / row_total).astype(jnp.bfloat16)
        mixture = jnp.einsum(
            "bhqk,bkhd->bqhd", probability, value_all, preferred_element_type=jnp.float32
        )
        outputs.append(mixture.astype(jnp.bfloat16))
        logsums.append(row_max[..., 0] + jnp.log(row_total[..., 0]))
    return (jnp.concatenate(outputs, 1), jnp.concatenate(logsums, 2))


def attention_backward(query_rows_local, key_all, value_all, grad_mixture, logsums):
    block_len = min(512, SEQ)
    grad_queries = []
    grad_keys = jnp.zeros(key_all.shape, jnp.float32)
    value_gradient_rows = jnp.zeros(value_all.shape, jnp.float32)
    for block_index in range(SEQ // block_len):
        lower = block_index * block_len
        query_block = query_rows_local[:, lower : lower + block_len]
        grad_block = grad_mixture[:, lower : lower + block_len]
        scores = causal_scores(query_block, key_all, block_index, block_len)
        probability = jnp.exp(scores - logsums[:, :, lower : lower + block_len, None])
        grad_prob = jnp.einsum(
            "bqhd,bkhd->bhqk", grad_block, value_all, preferred_element_type=jnp.float32
        )
        row_delta = jnp.sum(grad_prob * probability, -1, keepdims=True)
        dscore = (0.125 * (probability * (grad_prob - row_delta))).astype(jnp.bfloat16)
        grad_queries.append(
            jnp.einsum(
                "bhqk,bkhd->bqhd", dscore, key_all, preferred_element_type=jnp.float32
            ).astype(jnp.bfloat16)
        )
        grad_keys = grad_keys + jnp.einsum(
            "bhqk,bqhd->bkhd", dscore, query_block, preferred_element_type=jnp.float32
        )
        value_gradient_rows = value_gradient_rows + jnp.einsum(
            "bhqk,bqhd->bkhd",
            probability.astype(jnp.bfloat16),
            grad_block,
            preferred_element_type=jnp.float32,
        )
    return (
        jnp.concatenate(grad_queries, 1),
        grad_keys.astype(jnp.bfloat16),
        value_gradient_rows.astype(jnp.bfloat16),
    )


def adam_step(factor_grad, weights, first_old, second_old, grad_norm):
    clipped = factor_grad * (CLIP_NORM / jnp.maximum(grad_norm, CLIP_NORM))
    first_new = BETA_ONE * first_old + (1.0 - BETA_ONE) * clipped
    second_new = BETA_TWO * second_old + (1.0 - BETA_TWO) * clipped * clipped
    first_hat = first_new / (1.0 - BETA_ONE**STEP)
    second_hat = second_new / (1.0 - BETA_TWO**STEP)
    weights_new = weights - LEARN_RATE * (
        first_hat / (jnp.sqrt(second_hat) + ADAM_EPSILON) + WEIGHT_DECAY * weights
    )
    return (clipped, weights_new, first_new, second_new)


def body(
    tokens_in,
    norm_params,
    query_key_value_weight,
    out_weight,
    fc_weight,
    proj_weight,
    factors,
    first_moment,
    second_moment,
    grad_out,
):
    tensor_size = lax.axis_size("tensor")
    tensor_rank = lax.axis_index("tensor")
    token_count = tokens_in.shape[0]
    doc_count = token_count // SEQ
    local_width = query_key_value_weight.shape[2]
    heads_here = local_width // HD
    row_count = token_count // tensor_size
    row_start = tensor_rank * row_count
    rank_count = factors.shape[1]
    full_width = factors.shape[2]
    inputs = tokens_in.astype(jnp.float32)
    first_normalized, unit_one, inverse_one = normalize(inputs, norm_params[0], norm_params[1])
    first_normalized_reduced = first_normalized.astype(jnp.bfloat16)
    factor_reduced_precision = factors.astype(jnp.bfloat16)
    column_offset = tensor_rank * local_width
    query_adapter_output = lax.dynamic_slice_in_dim(
        factor_reduced_precision[1], column_offset, local_width, 1
    )
    value_adapter_output = lax.dynamic_slice_in_dim(
        factor_reduced_precision[3], column_offset, local_width, 1
    )
    query_down_factor = product_with_transpose(
        first_normalized_reduced, factor_reduced_precision[0]
    ).astype(jnp.bfloat16)
    value_down_factor = product_with_transpose(
        first_normalized_reduced, factor_reduced_precision[2]
    ).astype(jnp.bfloat16)
    query_rows_local = (
        matrix_product(first_normalized_reduced, query_key_value_weight[0])
        + ADAPTER_SCALING * matrix_product(query_down_factor, query_adapter_output)
    ).astype(jnp.bfloat16)
    keys_low = matrix_product(first_normalized_reduced, query_key_value_weight[1]).astype(
        jnp.bfloat16
    )
    values_low = (
        matrix_product(first_normalized_reduced, query_key_value_weight[2])
        + ADAPTER_SCALING * matrix_product(value_down_factor, value_adapter_output)
    ).astype(jnp.bfloat16)
    head_shape = (doc_count, SEQ, heads_here, HD)
    query_heads = query_rows_local.reshape(head_shape)
    keys_heads = keys_low.reshape(head_shape)
    values_heads = values_low.reshape(head_shape)
    mixture, logsums = attention_forward(query_heads, keys_heads, values_heads)
    attn_part = matrix_product(mixture.reshape(token_count, local_width), out_weight)
    grad_full = grad_out.astype(jnp.float32)
    attn_rows = lax.psum_scatter(
        attn_part.astype(jnp.bfloat16), "tensor", scatter_dimension=0, tiled=True
    ).astype(jnp.float32)
    resid_rows = lax.dynamic_slice_in_dim(inputs, row_start, row_count, 0) + attn_rows
    normed_two_rows, unit_two, inverse_two = normalize(resid_rows, norm_params[2], norm_params[3])
    normed_two_low = lax.all_gather(
        normed_two_rows.astype(jnp.bfloat16), "tensor", axis=0, tiled=True
    )
    hidden_pre = matrix_product(normed_two_low, fc_weight)
    hidden_act, gelu_pull = jax.vjp(
        lambda argument: jax.nn.gelu(argument, approximate=True), hidden_pre
    )
    mlp_part = matrix_product(hidden_act.astype(jnp.bfloat16), proj_weight)
    grad_hidden = product_with_transpose(grad_out, proj_weight)
    grad_pre = gelu_pull(grad_hidden)[0].astype(jnp.bfloat16)
    second_part = product_with_transpose(grad_pre, fc_weight)
    out_rows = resid_rows + lax.psum_scatter(
        mlp_part.astype(jnp.bfloat16), "tensor", scatter_dimension=0, tiled=True
    ).astype(jnp.float32)
    second_rows = lax.psum_scatter(
        second_part.astype(jnp.bfloat16), "tensor", scatter_dimension=0, tiled=True
    ).astype(jnp.float32)
    resid_grad_rows = lax.dynamic_slice_in_dim(grad_full, row_start, row_count, 0) + normalize_back(
        second_rows, unit_two, inverse_two, norm_params[2]
    )
    resid_grad_low = lax.all_gather(
        resid_grad_rows.astype(jnp.bfloat16), "tensor", axis=0, tiled=True
    )
    grad_mixture = product_with_transpose(resid_grad_low, out_weight).astype(jnp.bfloat16)
    query_gradient, grad_keys, value_gradient_rows = attention_backward(
        query_heads, keys_heads, values_heads, grad_mixture.reshape(head_shape), logsums
    )
    query_gradient = query_gradient.reshape(token_count, local_width)
    grad_keys = grad_keys.reshape(token_count, local_width)
    value_gradient_rows = value_gradient_rows.reshape(token_count, local_width)
    stacked = jnp.stack((query_gradient, grad_keys, value_gradient_rows))
    first_part = jnp.einsum(
        "stc,sdc->td", stacked, query_key_value_weight, preferred_element_type=jnp.float32
    )
    query_up_factor = ADAPTER_SCALING * product_with_transpose(query_gradient, query_adapter_output)
    value_up_factor = ADAPTER_SCALING * product_with_transpose(
        value_gradient_rows, value_adapter_output
    )
    first_part = first_part + jnp.dot(
        query_up_factor,
        factor_reduced_precision[0].astype(jnp.float32),
        precision=lax.Precision.HIGHEST,
    )
    first_part = first_part + jnp.dot(
        value_up_factor,
        factor_reduced_precision[2].astype(jnp.float32),
        precision=lax.Precision.HIGHEST,
    )
    first_rows = lax.psum_scatter(
        first_part.astype(jnp.bfloat16), "tensor", scatter_dimension=0, tiled=True
    ).astype(jnp.float32)
    unit_rows = lax.dynamic_slice_in_dim(unit_one, row_start, row_count, 0)
    inverse_rows = lax.dynamic_slice_in_dim(inverse_one, row_start, row_count, 0)
    input_rows = resid_grad_rows + normalize_back(
        first_rows, unit_rows, inverse_rows, norm_params[0]
    )
    query_cross_term = transpose_then_product(query_gradient, first_normalized_reduced)
    value_cross_term = transpose_then_product(value_gradient_rows, first_normalized_reduced)
    query_down_gradient = ADAPTER_SCALING * jnp.dot(
        query_adapter_output.astype(jnp.float32), query_cross_term, precision=lax.Precision.HIGHEST
    )
    value_down_gradient = ADAPTER_SCALING * jnp.dot(
        value_adapter_output.astype(jnp.float32), value_cross_term, precision=lax.Precision.HIGHEST
    )
    empty_slot = jnp.zeros((rank_count, full_width), jnp.float32)
    up_grad_query = lax.dynamic_update_slice_in_dim(
        empty_slot,
        ADAPTER_SCALING * transpose_then_product(query_down_factor, query_gradient),
        column_offset,
        1,
    )
    up_grad_value = lax.dynamic_update_slice_in_dim(
        empty_slot,
        ADAPTER_SCALING * transpose_then_product(value_down_factor, value_gradient_rows),
        column_offset,
        1,
    )
    partial_grad = jnp.stack(
        (query_down_gradient, up_grad_query, value_down_gradient, up_grad_value)
    )
    reduced = lax.psum(partial_grad, ("dp", "tensor"))
    grad_norm = jnp.sqrt(jnp.sum(reduced * reduced))
    clipped, weights_new, first_new, second_new = adam_step(
        reduced, factors, first_moment, second_moment, grad_norm
    )
    return (
        out_rows.astype(jnp.bfloat16),
        input_rows,
        clipped,
        grad_norm,
        weights_new,
        first_new,
        second_new,
    )


MESH = pl.DeviceIdType.MESH
BF = jnp.bfloat16
F32 = jnp.float32
GROUPS = 8
PAIRS = 8


def mm(left, right):
    return jnp.dot(left, right, preferred_element_type=F32)


def mm_nt(left, right):
    return lax.dot_general(left, right, (((1,), (1,)), ((), ())), preferred_element_type=F32)


def mm_tn(left, right):
    return lax.dot_general(left, right, (((0,), (0,)), ((), ())), preferred_element_type=F32)


def flip(value, bit):
    return value + bit - 2 * bit * ((value // bit) % 2)


def unit_of(rows):
    centered = rows - jnp.mean(rows, -1, keepdims=True)
    inverse = lax.rsqrt(jnp.mean(centered * centered, -1, keepdims=True) + EPSILON)
    return centered * inverse, inverse


def unit_back(scaled, unit, inverse):
    return inverse * (
        scaled - jnp.mean(scaled, -1, keepdims=True) - unit * jnp.mean(scaled * unit, -1, keepdims=True)
    )


def fused_kernel(
    planes,
    tokens, norm_params, wqkv, w_out, w_fc, w_proj, factors, grad_out,
    bo_r, ig_r, summed,
    tok, n1, go, wq, wkv, wo, fcw, pw, kv, qs, p0, p1, mix, inv, attn_own, attn_s, attn_r,
    res, n2, acc_a, acc_b, gnt_s, gnt_r, gnt_xs, gnt_xr, mlp_s, mlp_r, mlp_xs, mlp_xr,
    gr, gr_b, bo_f, bo_s, gq, dos, gno_s, gno_r, gno_xs, gno_xr, ig_s,
    fpad, f02, f1p, f3kv, down, gd_scr, fg_a, fg_q, fg_v, ps, ps_r, plane_buf, z_buf, fin,
    chain_send, chain_recv, pair_send, pair_recv, load_sem, ssem, rsem,
):
    d = lax.axis_index("dp")
    t = lax.axis_index("tensor")
    z, c, x, y = d // 2, d % 2, t % 2, t // 2
    odd = z % 2
    nbr = (flip(d, 1), t)
    prim = (d, flip(t, 1 + odd))
    sec = (d, flip(t, 2 - odd))
    plane = [(d, flip(t, 1)), (d, flip(t, 2)), (d, 3 - t)]
    x_nbr, y_nbr = plane[0], plane[1]
    zs = [(flip(d, 2 << k), t) for k in range(planes.bit_length() - 1)]
    owners = [(2 * z + y, 2 * h + x) for h in range(2)]
    at_home = [jnp.logical_and(c == y, h == y) for h in range(2)]
    quarter = [t, flip(t, 1 + odd), flip(t, 2 - odd), 3 - t]
    column = [pl.multiple_of(q * 256 + c * 128, 128) for q in quarter]

    def at(start, size):
        return pl.ds(pl.multiple_of(start, size), size)

    def rows_of(half, side):
        return at(512 * half + 256 * side, 256)

    def own_rows(h, side):
        return at(512 * h + 256 * side + 128 * c, 128)

    def other_rows(h, side):
        return at(512 * h + 256 * side + 128 * (1 - c), 128)

    def remote_to(src, dst, out_index, in_index, device):
        return pltpu.make_async_remote_copy(
            src_ref=src, dst_ref=dst, send_sem=ssem.at[out_index], recv_sem=rsem.at[in_index],
            device_id=device, device_id_type=MESH,
        )

    def remote(src, dst, index, device):
        return remote_to(src, dst, index, index, device)

    pending = []

    def drain():
        for wait in pending:
            wait()

    def send(copy):
        copy.start()
        pending.append(copy.wait_send)
        return copy

    lane = at(c * 128, 128)
    loads = [
        pltpu.make_async_copy(wqkv.at[1, :, lane], wkv.at[:, pl.ds(0, 128)], load_sem.at[0]),
        pltpu.make_async_copy(wqkv.at[2, :, lane], wkv.at[:, pl.ds(128, 128)], load_sem.at[1]),
        pltpu.make_async_copy(wqkv.at[0, :, lane], wq.at[:, pl.ds(0, 128)], load_sem.at[2]),
        pltpu.make_async_copy(w_out.at[lane, :], wo.at[pl.ds(0, 128), :], load_sem.at[3]),
        pltpu.make_async_copy(w_fc.at[:, at(c * 512, 512)], fcw.at[0], load_sem.at[4]),
        pltpu.make_async_copy(w_proj.at[at(c * 512, 512), :], pw.at[0], load_sem.at[5]),
    ]
    for load in loads:
        load.start()

    barrier = pltpu.get_barrier_semaphore()
    partners = [nbr, x_nbr, y_nbr] + zs
    for device in partners:
        pl.semaphore_signal(barrier, inc=1, device_id=device, device_id_type=MESH)
    pl.semaphore_wait(barrier, len(partners))

    doc = []
    for first, source, target in ((0, tokens, tok), (4, grad_out, go)):
        for r in range(4):
            part = pl.ds(256 * r, 256)
            doc.append((source.at[part, :], target.at[part, :], first + r))

    @pl.when(c == y)
    def _():
        for src, dst, index in doc:
            remote(src, dst, index, nbr).start()
            pltpu.make_async_copy(src, dst, rsem.at[index]).start()

    def doc_sent():
        @pl.when(c == y)
        def _():
            for item in doc:
                remote(*item, nbr).wait_send()

    pending.append(doc_sent)

    def doc_wait(index):
        remote(*doc[index], nbr).wait_recv()

    def piece(slot, group):
        matrix, a = group // 2, group % 2
        if matrix < 2:
            return wkv.at[pl.ds(512 * a, 512), pl.ds(256 * slot + 128 * matrix, 128)]
        if matrix == 2:
            return wq.at[pl.ds(512 * a, 512), pl.ds(128 * slot, 128)]
        return wo.at[pl.ds(128 * slot + 64 * a, 64), :]

    def hop(slot, group):
        return pltpu.make_async_remote_copy(
            src_ref=piece(1 if slot > 1 else 0, group), dst_ref=piece(slot, group),
            send_sem=chain_send.at[slot - 1, group], recv_sem=chain_recv.at[slot - 1, group],
            device_id=(prim, zs[0], sec)[slot - 1], device_id_type=MESH,
        )

    def pump(group, later=True):
        hop(1, group).wait_recv()
        for slot in (2, 3):
            hop(slot, group).start()
            if later:
                pending.append(hop(slot, group).wait_send)

    def passed(groups):
        for group in groups:
            hop(2, group).wait_recv()
            hop(3, group).wait_recv()

    def pair_piece(slot, pair, parity):
        h, q = pair // 4, pair % 4
        if q < 2:
            return fcw.at[slot, at(512 * q + 256 * parity, 256), pl.ds(256 * h, 256)]
        return pw.at[slot, at(256 * h + 128 * (q - 2) + 64 * parity, 64), :]

    def pair_hop(step, pair, parity):
        return pltpu.make_async_remote_copy(
            src_ref=pair_piece(step, pair, parity), dst_ref=pair_piece(1, pair, parity),
            send_sem=pair_send.at[step, pair], recv_sem=pair_recv.at[step, pair],
            device_id=(y_nbr, zs[0])[step], device_id_type=MESH,
        )

    def pair_pump(pair):
        pair_hop(0, pair, odd).wait_recv()
        pair_hop(1, pair, odd).start()

    def pair_wait(pairs):
        for pair in pairs:
            pair_hop(1, pair, 1 - odd).wait_recv()

    for matrix in range(4):
        loads[matrix].wait()
        send(hop(1, 2 * matrix))
        send(hop(1, 2 * matrix + 1))

    fpad[...] = jnp.zeros_like(fpad)
    fpad[0:4, :] = factors[0]
    fpad[4:8, :] = factors[2]
    f02[...] = fpad[...].astype(BF)
    fpad[...] = jnp.zeros_like(fpad)
    for s in range(4):
        fpad[0:4, 128 * s : 128 * s + 128] = factors[1, :, pl.ds(column[s], 128)]
    f1p[...] = fpad[:, :512].astype(BF)
    fpad[...] = jnp.zeros_like(fpad)
    for s in range(4):
        fpad[4:8, 256 * s + 128 : 256 * s + 256] = factors[3, :, pl.ds(column[s], 128)]
    f3kv[...] = fpad[...].astype(BF)
    ps[...] = jnp.zeros_like(ps)

    gain_one, bias_one = norm_params[0:1, :], norm_params[1:2, :]
    gain_two, bias_two = norm_params[2:3, :], norm_params[3:4, :]
    def first_norm(r):
        doc_wait(r)

        @pl.loop(0, 2)
        def _(q):
            rows = at(256 * r + 128 * q, 128)
            unit, _ = unit_of(tok[rows, :].astype(F32))
            n1[rows, :] = (unit * gain_one + bias_one).astype(BF)

    first_norm(0)
    first_norm(1)
    pump(0)
    first_norm(2)
    first_norm(3)

    @pl.loop(0, 2)
    def _(r):
        rows = at(512 * r, 512)
        down[rows, :] = mm_nt(n1[rows, :], f02[...]).astype(BF)

    pump(1)
    acc_a[...] = jnp.zeros_like(acc_a)
    acc_b[...] = jnp.zeros_like(acc_b)
    first_head = lax.broadcasted_iota(jnp.int32, (256, 512), 1) % 128 < 64
    first_lanes = first_head[:, 0:128]

    def stacked(rows, lanes):
        return jnp.concatenate((jnp.where(lanes, rows, 0.0), jnp.where(lanes, 0.0, rows)), 0)

    p_refs = (p0, p1)
    column_pos = lax.broadcasted_iota(jnp.int32, (512, 512), 1)
    row_pos = lax.broadcasted_iota(jnp.int32, (512, 512), 0) % 256 + 256 * x
    allowed = column_pos <= row_pos

    loads[4].wait()
    loads[5].wait()

    @pl.loop(0, 4)
    def _(s):
        @pl.when(s == 1)
        def _():
            for group in range(2, 6):
                pump(group, False)

        @pl.when(s == 2)
        def _():
            pump(6, False)
            passed(range(0, 6))

        @pl.when(s == 3)
        def _():
            pump(7, False)
            for pair in range(PAIRS):
                pair_hop(0, pair, odd).start()

        both_lanes, lanes = at(256 * s, 256), at(128 * s, 128)
        keys, values = at(256 * s, 128), at(256 * s + 128, 128)

        @pl.loop(0, 2)
        def _(r):
            rows = at(512 * r, 512)
            kv[rows, both_lanes] = (
                mm(n1[rows, :], wkv[:, both_lanes]) + ADAPTER_SCALING * mm(down[rows, :], f3kv[:, both_lanes])
            ).astype(BF)

        for h in range(2):
            rows = rows_of(h, x)
            query = mm(n1[rows, :], wq[:, lanes]) + ADAPTER_SCALING * mm(down[rows, :], f1p[:, lanes])
            qs[h, :, lanes] = stacked(query.astype(BF).astype(F32) * 0.125, first_lanes).astype(BF)
        scores = [mm_nt(qs[h, :, lanes], kv[0 : 512 * (h + 1), keys]) for h in range(2)]
        kept = []
        for h in range(2):
            last = jnp.where(allowed, scores[h][:, 512 * h :], NEG_LARGE)
            block = jnp.concatenate((scores[h][:, :512], last), 1) if h else last
            exponent = jnp.exp(block - jnp.max(block, -1, keepdims=True))
            inverse = 1.0 / jnp.sum(exponent, -1, keepdims=True)
            p_refs[h][s] = exponent.astype(BF)
            inv[h, :, lanes] = jnp.broadcast_to(inverse, (512, 128))
            kept.append((exponent.astype(BF), inverse))
        for h in range(2):
            both = mm(kept[h][0], kv[0 : 512 * (h + 1), values]) * kept[h][1]
            mix[256 * h : 256 * h + 256, lanes] = jnp.where(first_lanes, both[0:256], both[256:512])

    for group in range(2, GROUPS):
        pending.append(hop(2, group).wait_send)
        pending.append(hop(3, group).wait_send)
    for pair in range(PAIRS):
        pending.append(pair_hop(0, pair, odd).wait_send)
    passed(range(6, 8))

    def heads_out(sub):
        rows = [mix[at(256 * h + 128 * sub, 128), :].astype(BF) for h in range(2)]
        return mm(jnp.concatenate(rows, 0), wo[...])

    attn_s[...] = heads_out(1 - c).astype(BF)
    to_nbr = send(remote(attn_s, attn_r, 8, nbr))
    attn_own[...] = heads_out(c)
    to_nbr.wait_recv()

    gathered = []
    for h in range(2):
        part = slice(128 * h, 128 * h + 128)
        rows = own_rows(h, x)
        residual = tok[rows, :].astype(F32) + attn_own[part, :] + attn_r[part, :].astype(F32)
        res[part, :] = residual
        unit, _ = unit_of(residual)
        n2[rows, :] = (unit * gain_two + bias_two).astype(BF)
        gathered.append(send(remote(n2.at[rows, :], n2.at[rows, :], 11 + h, x_nbr)))
        gathered.append(send(remote(n2.at[rows, :], n2.at[rows, :], 9 + h, nbr)))
    for r in range(4):
        doc_wait(4 + r)
    gathered[1].wait_recv()
    gathered[3].wait_recv()

    def pass_on(h):
        gathered[2 * h].wait_recv()
        rows = own_rows(h, 1 - x)
        remote(n2.at[rows, :], n2.at[rows, :], 13 + h, nbr).start()

    def passed_on(h):
        rows = own_rows(h, 1 - x)
        return remote(n2.at[rows, :], n2.at[rows, :], 13 + h, nbr)

    def sum_copy(source, target, first, h, j):
        part = pl.ds(128 * j, 128)
        return remote(source.at[h, part, :], target.at[h, part, :], first + 2 * h + j, nbr)

    def to_core(acc, source, target, first, h):
        for j, side in enumerate((1 - x, x)):
            source[h, 128 * j : 128 * j + 128, :] = acc[other_rows(h, side), :].astype(BF)
            sum_copy(source, target, first, h, j).start()

    def to_side(acc, source, target, out, out_target, first, side_first, h):
        sum_copy(source, target, first, h, 0).wait_recv()
        out[h] = (acc[own_rows(h, 1 - x), :] + target[h, 0:128, :].astype(F32)).astype(BF)
        return send(remote(out.at[h], out_target.at[h], side_first + h, x_nbr))

    @pl.loop(0, 8)
    def _(unit):
        @pl.when(unit == 0)
        def _():
            pair_pump(0)

        @pl.when(unit == 2)
        def _():
            for pair in (1, 2):
                pair_pump(pair)
            pass_on(0)
            for pair in (3, 4):
                pair_pump(pair)
            pair_wait(range(0, 4))

        @pl.when(unit == 3)
        def _():
            pass_on(1)
            pair_pump(5)
            for h in range(2):
                passed_on(h).wait_recv()

        @pl.when(unit == 5)
        def _():
            pair_pump(6)

        @pl.when(unit == 6)
        def _():
            pair_pump(7)
            pair_wait(range(4, 8))

        @pl.when(unit == 7)
        def _():
            to_core(acc_b, gnt_s, gnt_r, 40, 1)

        flag = lambda value: jnp.where(value, 1, 0)
        slot = flag(jnp.logical_or(unit == 2, unit >= 5))
        part = flag(jnp.logical_or(unit >= 6, jnp.logical_or(unit == 1, unit == 4)))
        side = jnp.where(unit < 3, x, 1 - x)
        last_half = 7 - unit
        starts = [
            jnp.where(unit < 6, 512 * h + 256 * side, 512 * last_half + 256 * h) for h in range(2)
        ]
        tiles = [at(start, 256) for start in starts]
        lanes = at(256 * part, 256)
        pre = [mm(n2[rows, :], fcw[slot, :, lanes]) for rows in tiles]
        grad_act = [mm_nt(go[rows, :], pw[slot, lanes, :]) for rows in tiles]
        for rows, hidden, grad in zip(tiles, pre, grad_act):
            square = hidden * hidden
            tanh = jnp.tanh(GELU_SCALE * hidden * (1.0 + GELU_CUBE * square))
            half_up = 0.5 * (1.0 + tanh)
            slope = half_up + (0.5 * GELU_SCALE) * hidden * (1.0 - tanh * tanh) * (
                1.0 + 3.0 * GELU_CUBE * square
            )
            acc_b[rows, :] += mm_nt((grad * slope).astype(BF), fcw[slot, :, lanes])
            acc_a[rows, :] += mm((hidden * half_up).astype(BF), pw[slot, lanes, :])

    for pair in range(PAIRS):
        pending.append(pair_hop(1, pair, odd).wait_send)
    for h in range(2):
        pending.append(passed_on(h).wait_send)
        for j in range(2):
            pending.append(sum_copy(gnt_s, gnt_r, 40, h, j).wait_send)
            pending.append(sum_copy(mlp_s, mlp_r, 44, h, j).wait_send)

    gnt_side, mlp_side = [None, None], [None, None]
    to_core(acc_b, gnt_s, gnt_r, 40, 0)
    for h in (1, 0):
        gnt_side[h] = to_side(acc_b, gnt_s, gnt_r, gnt_xs, gnt_xr, 40, 17, h)
    for h in (1, 0):
        to_core(acc_a, mlp_s, mlp_r, 44, h)
    for h in (1, 0):
        mlp_side[h] = to_side(acc_a, mlp_s, mlp_r, mlp_xs, mlp_xr, 44, 21, h)
    for h in range(2):
        part = slice(128 * h, 128 * h + 128)
        sum_copy(mlp_s, mlp_r, 44, h, 1).wait_recv()
        bo_f[part, :] = res[part, :] + acc_a[own_rows(h, x), :] + mlp_r[h, 128:256, :].astype(F32)

    def residual_back(h):
        part = slice(128 * h, 128 * h + 128)
        unit, inverse = unit_of(res[part, :])
        sum_copy(gnt_s, gnt_r, 40, h, 1).wait_recv()
        total = acc_b[own_rows(h, x), :] + gnt_r[h, 128:256, :].astype(F32)
        gnt_side[h].wait_recv()
        scaled = (total + gnt_xr[h].astype(F32)) * gain_two
        grad = go[own_rows(h, x), :].astype(F32) + unit_back(scaled, unit, inverse)
        gr[part, :] = grad
        local = at(256 * h + 128 * c, 128)
        gr_b[local, :] = grad.astype(BF)
        return send(remote(gr_b.at[local, :], gr_b.at[local, :], 23 + h, nbr))

    def mixture_back(h):
        grad_mixture = mm_nt(gr_b[256 * h : 256 * h + 256, :], wo[...])
        dos[h] = (stacked(grad_mixture, first_head) * inv[h]).astype(BF)

    to_nbr = residual_back(1)
    to_nbr.wait_recv()
    mixture_back(1)

    def scores_back(h, first, count):
        size = 512 * (h + 1)
        group = [first + k for k in range(count)]
        lanes = [at(128 * s, 128) for s in group]
        k_lanes = [at(256 * s, 128) for s in group]
        v_lanes = [at(256 * s + 128, 128) for s in group]
        grads = [dos[h, :, lane] for lane in lanes]
        grad_prob = [mm_nt(grad, kv[0:size, lane]) for lane, grad in zip(v_lanes, grads)]
        dscores = []
        for s, lane, grad, block in zip(group, lanes, grads, grad_prob):
            mixture = mix[256 * h : 256 * h + 256, lane]
            delta = jnp.sum(
                grad.astype(F32) * jnp.concatenate((mixture, mixture), 0), -1, keepdims=True
            )
            dscores.append((p_refs[h][s].astype(F32) * (block - delta)).astype(BF))
        for k, (s, lane, grad, dscore) in enumerate(zip(group, lanes, grads, dscores)):
            both = 0.125 * mm(dscore, kv[0:size, k_lanes[k]])
            gq[:, lane] = jnp.where(first_lanes, both[0:256], both[256:512]).astype(BF)
            grad_keys = mm_tn(dscore, qs[h, :, lane])
            grad_values = mm_tn(p_refs[h][s], grad)
            if h:
                acc_a[:, k_lanes[k]] = grad_keys
                acc_a[:, v_lanes[k]] = grad_values
            else:
                acc_a[0:512, k_lanes[k]] += grad_keys
                acc_a[0:512, v_lanes[k]] += grad_values

    def factors_back(h):
        rows = slice(512 * h, 512 * h + 512)
        grads = acc_a[rows, :].astype(BF)
        query = gq[...]
        gd_scr[...] = ADAPTER_SCALING * mm_nt(grads, f3kv[...])
        gd_scr[at(256 * x, 256), :] += ADAPTER_SCALING * mm_nt(query, f1p[...])
        terms = (
            mm_tn(gd_scr[...].astype(BF), n1[rows, :])[0:8],
            mm_tn(down[rows_of(h, x), :], query)[0:8],
            mm_tn(down[rows, :], grads)[0:8],
        )
        for total, term in zip((fg_a, fg_q, fg_v), terms):
            total[...] = term if h else total[...] + term

    def rows_copy(h, j):
        part = pl.ds(128 * j, 128)
        return remote(gno_s.at[h, part, :], gno_r.at[h, part, :], 27 + 2 * h + j, nbr)

    def rows_back(h):
        for j, side in enumerate((1 - x, x)):
            rows = rows_of(h, side)
            grad = mm_nt(acc_a[rows, :].astype(BF), wkv[...])
            grad += mm(gd_scr[at(256 * side, 256), :].astype(BF), f02[...])
            if j:
                grad += mm_nt(gq[...], wq[...])
            acc_b[rows, :] = grad
            gno_s[h, 128 * j : 128 * j + 128, :] = acc_b[other_rows(h, side), :].astype(BF)
            send(rows_copy(h, j))

    side_copies = {}

    def reduce_rows(h):
        rows_copy(h, 0).wait_recv()
        gno_xs[h] = (acc_b[own_rows(h, 1 - x), :] + gno_r[h, 0:128, :].astype(F32)).astype(BF)
        for k in range(2):
            part = pl.ds(64 * k, 64)
            side_copies[h, k] = send(
                remote(gno_xs.at[h, part, :], gno_xr.at[h, part, :], 48 + 2 * h + k, x_nbr)
            )

    def to_owner(src, dst, h, out_index, in_index):
        @pl.when(at_home[h])
        def _():
            pltpu.make_async_copy(src, dst, rsem.at[in_index + c]).start()

        @pl.when(jnp.logical_not(at_home[h]))
        def _():
            remote_to(src, dst, out_index, in_index + c, owners[h]).start()

        def sent():
            @pl.when(jnp.logical_not(at_home[h]))
            def _():
                remote_to(src, dst, out_index, in_index + c, owners[h]).wait_send()

        pending.append(sent)

    def input_rows(h, k):
        if k == 0:
            rows_copy(h, 1).wait_recv()
        start = 512 * h + 256 * x + 128 * c + 64 * k
        rows, part = at(start, 64), slice(64 * k, 64 * k + 64)
        unit, inverse = unit_of(tok[rows, :].astype(F32))
        total = acc_b[rows, :] + gno_r[h, 128 + 64 * k : 192 + 64 * k, :].astype(F32)
        side_copies[h, k].wait_recv()
        scaled = (total + gno_xr[h, part, :].astype(F32)) * gain_one
        out = slice(128 * h + 64 * k, 128 * h + 64 * k + 64)
        ig_s[out, :] = (gr[out, :] + unit_back(scaled, unit, inverse)).astype(BF)
        to_owner(ig_s.at[out, :], ig_r.at[at(128 * c + 64 * k, 64), :], h, 52 + 2 * h + k, 56 + 2 * k)

    @pl.loop(0, 2)
    def _(group):
        scores_back(1, 2 * group, 2)

    to_nbr = residual_back(0)
    factors_back(1)
    rows_back(1)
    to_nbr.wait_recv()
    mixture_back(0)
    reduce_rows(1)
    scores_back(0, 0, 4)

    for h in (1, 0):
        part = slice(128 * h, 128 * h + 128)
        mlp_side[h].wait_recv()
        bo_s[part, :] = (bo_f[part, :] + mlp_xr[h].astype(F32)).astype(BF)
        to_owner(bo_s.at[part, :], bo_r.at[at(128 * c, 128), :], h, 60 + h, 62)
    factors_back(0)

    ps[0:8, :] = fg_a[...]
    down_rows = lax.broadcasted_iota(jnp.int32, (8, 128), 0) < 4
    for s in range(4):
        ps[8:16, pl.ds(column[s], 128)] = ADAPTER_SCALING * jnp.where(
            down_rows, fg_q[:, 128 * s : 128 * s + 128], fg_v[:, 256 * s + 128 : 256 * s + 256]
        )
    core_sum = send(remote(ps, ps_r, 33, nbr))
    rows_back(0)
    core_sum.wait_recv()
    eight = at(8 * c, 8)
    plane_buf[t] = ps[eight, :] + ps_r[eight, :]
    copies = [
        send(remote(plane_buf.at[t], plane_buf.at[t], 35 + k, device)) for k, device in enumerate(plane)
    ]
    reduce_rows(0)
    for k in range(2):
        input_rows(1, k)
    for copy in copies:
        copy.wait_recv()
    z_buf[0] = plane_buf[0] + plane_buf[1] + plane_buf[2] + plane_buf[3]

    def z_copy(k):
        return remote(z_buf.at[2 * k], z_buf.at[2 * k + 1], 64 + k, zs[k])

    for k in range(len(zs)):
        send(z_copy(k))
        if k < 2:
            input_rows(0, k)
        z_copy(k).wait_recv()
        z_buf[2 * k + 2] = z_buf[2 * k] + z_buf[2 * k + 1]
    for k in range(len(zs), 2):
        input_rows(0, k)
    fin[eight, :] = z_buf[2 * len(zs)]
    send(remote(fin.at[eight, :], fin.at[eight, :], 34, nbr))
    theirs = at(8 - 8 * c, 8)
    remote(fin.at[theirs, :], fin.at[theirs, :], 34, nbr).wait_recv()
    result = pltpu.make_async_copy(fin, summed, load_sem.at[0])
    result.start()

    for core in range(2):
        part = pl.ds(128 * core, 128)
        remote_to(bo_s.at[pl.ds(0, 128), :], bo_r.at[part, :], 60, 62 + core, nbr).wait_recv()
        for k in range(2):
            part = pl.ds(128 * core + 64 * k, 64)
            remote_to(ig_s.at[pl.ds(0, 64), :], ig_r.at[part, :], 52, 56 + 2 * k + core, nbr).wait_recv()
    result.wait()
    drain()


def finish_kernel(
    factors, first_moment, second_moment, bo_in, ig_in, sum_in,
    block_out, input_grad, clipped, grad_norm, factors_new, first_new, second_new,
    bo, ig, summed, grads, sem, out_sem,
):
    pairs = [(sum_in, summed), (bo_in, bo), (ig_in, ig)]
    loads = [pltpu.make_async_copy(*pair, sem.at[k]) for k, pair in enumerate(pairs)]
    for load in loads:
        load.start()
    loads[0].wait()
    grad = summed[...]
    norm = jnp.sqrt(jnp.sum(grad * grad, (0, 1), keepdims=True))
    grad_norm[...] = norm
    grad = grad * (CLIP_NORM / jnp.maximum(norm, CLIP_NORM))
    for index, first in enumerate((0, 8, 4, 12)):
        value, weights = grad[first : first + 4], factors[index]
        first_value = BETA_ONE * first_moment[index] + (1.0 - BETA_ONE) * value
        second_value = BETA_TWO * second_moment[index] + (1.0 - BETA_TWO) * value * value
        first_hat = first_value / (1.0 - BETA_ONE**STEP)
        second_hat = second_value / (1.0 - BETA_TWO**STEP)
        clipped[index] = value
        first_new[index] = first_value
        second_new[index] = second_value
        factors_new[index] = weights - LEARN_RATE * (
            first_hat / (jnp.sqrt(second_hat) + ADAM_EPSILON) + WEIGHT_DECAY * weights
        )
    loads[1].wait()
    stores = [pltpu.make_async_copy(bo, block_out, out_sem.at[0])]
    stores[0].start()
    loads[2].wait()
    grads[...] = ig[...].astype(F32)
    stores.append(pltpu.make_async_copy(grads, input_grad, out_sem.at[1]))
    stores[1].start()
    for store in stores:
        store.wait()


def fused(planes, tokens, norm_params, wqkv, w_out, w_fc, w_proj, factors, first, second, grad_out):
    vmem = pl.BlockSpec(memory_space=pltpu.VMEM)
    hbm = pl.BlockSpec(memory_space=pl.ANY)

    def buf(*shape):
        return pltpu.VMEM(shape, BF)

    def acc(*shape):
        return pltpu.VMEM(shape, F32)

    def sems(*shape):
        return pltpu.SemaphoreType.DMA(shape)

    quarter = [buf(256, 1024)] * 2
    halves, eighths = [buf(2, 256, 1024)] * 2, [buf(2, 128, 1024)] * 2
    scratch = [
        buf(1024, 1024), buf(1024, 1024), buf(1024, 1024), buf(1024, 512), buf(1024, 1024), buf(512, 1024),
        buf(2, 1024, 512), buf(2, 512, 1024), buf(1024, 1024), buf(2, 512, 512), buf(4, 512, 512),
        buf(4, 512, 1024), acc(512, 512), acc(2, 512, 512), acc(256, 1024), *quarter,
        acc(256, 1024), buf(1024, 1024), acc(1024, 1024), acc(1024, 1024),
        *halves, *eighths, *halves, *eighths,
        acc(256, 1024), buf(512, 1024), acc(256, 1024), buf(256, 1024), buf(256, 512), buf(2, 512, 512),
        *halves, *eighths, buf(256, 1024),
        acc(128, 1024), buf(128, 1024), buf(128, 512), buf(128, 1024), buf(1024, 128), acc(512, 128),
        acc(8, 1024), acc(8, 512), acc(8, 1024), acc(16, 1024), acc(16, 1024), acc(4, 8, 1024),
        acc(2 * planes, 8, 1024), acc(16, 1024),
        sems(3, GROUPS), sems(3, GROUPS), sems(2, PAIRS), sems(2, PAIRS), sems(6), sems(64 + planes),
        sems(64 + planes),
    ]
    rows = jax.ShapeDtypeStruct((256, 1024), BF)
    passed = pl.pallas_call(
        functools.partial(fused_kernel, planes),
        name="block_step",
        out_shape=(rows, rows, jax.ShapeDtypeStruct((16, 1024), F32)),
        in_specs=[hbm, vmem, hbm, hbm, hbm, hbm, vmem, hbm],
        out_specs=(hbm,) * 3,
        scratch_shapes=scratch,
        compiler_params=pltpu.CompilerParams(
            collective_id=1, has_side_effects=True, vmem_limit_bytes=63 << 20
        ),
    )(tokens, norm_params, wqkv, w_out, w_fc, w_proj, factors, grad_out)
    small = jax.ShapeDtypeStruct((4, 4, 1024), F32)
    outs = pl.pallas_call(
        finish_kernel,
        name="finish_step",
        out_shape=(
            rows, jax.ShapeDtypeStruct((256, 1024), F32), small,
            jax.ShapeDtypeStruct((1, 1), F32), small, small, small,
        ),
        in_specs=[vmem] * 3 + [hbm] * 3,
        out_specs=(hbm, hbm) + (vmem,) * 5,
        scratch_shapes=[*quarter, acc(16, 1024), acc(256, 1024), sems(3), sems(2)],
        compiler_params=pltpu.CompilerParams(vmem_limit_bytes=62 << 20),
    )(factors, first, second, *passed)
    return outs[:3] + (outs[3].reshape(()),) + outs[4:]


def solution(mesh):
    placed = (
        P("dp", None),
        P(),
        P(None, None, "tensor"),
        P("tensor", None),
        P(None, "tensor"),
        P("tensor", None),
        P(),
        P(),
        P(),
        P("dp", None),
    )
    planes = mesh.shape["dp"] // 2

    def step(*args):
        rows, width = args[0].shape
        shapes = (rows, width, args[4].shape[1], args[2].shape[2], args[6].shape[1])
        fits = mesh.shape["tensor"] == 4 and mesh.shape["dp"] % 4 == 0
        if fits and shapes == (SEQ, 1024, 1024, 256, 4):
            return fused(planes, *args)
        return body(*args)

    return jax.shard_map(
        step,
        mesh=mesh,
        in_specs=placed,
        out_specs=(P(("dp", "tensor"), None), P(("dp", "tensor"), None), P(), P(), P(), P(), P()),
        check_vma=False,
    )
```

```python
import functools

import jax
import jax.numpy as jnp
from jax import lax
from jax.experimental import pallas as pl
from jax.experimental.pallas import tpu as pltpu
from jax.sharding import PartitionSpec as P

HD = 64
SEQ = 1024
STEP = 5


EPSILON = 1e-05
ADAPTER_SCALING = 8.0
CLIP_NORM = 16.0
LEARN_RATE = 0.03
BETA_ONE = 0.5
BETA_TWO = 0.5
WEIGHT_DECAY = 0.01
ADAM_EPSILON = 1e-08
NEG_LARGE = -1e30
GELU_SCALE = 0.7978845608028654
GELU_CUBE = 0.044715


def matrix_product(left, right):
    return jnp.dot(left, right, preferred_element_type=jnp.float32)


def product_with_transpose(left, right):
    return lax.dot_general(
        left, right, (((1,), (1,)), ((), ())), preferred_element_type=jnp.float32
    )


def transpose_then_product(left, right):
    return lax.dot_general(
        left, right, (((0,), (0,)), ((), ())), preferred_element_type=jnp.float32
    )


def normalize(value_rows_local, gain_vec, bias_vec):
    centered = value_rows_local - jnp.mean(value_rows_local, -1, keepdims=True)
    inverse = lax.rsqrt(jnp.mean(centered * centered, -1, keepdims=True) + EPSILON)
    unit_rows = centered * inverse
    return (unit_rows * gain_vec + bias_vec, unit_rows, inverse)


def normalize_back(incoming, unit_rows, inverse, gain_vec):
    scaled = incoming * gain_vec
    return inverse * (
        scaled
        - jnp.mean(scaled, -1, keepdims=True)
        - unit_rows * jnp.mean(scaled * unit_rows, -1, keepdims=True)
    )


def causal_scores(query_block, key_all, block_index, block_len):
    scores = (
        jnp.einsum("bqhd,bkhd->bhqk", query_block, key_all, preferred_element_type=jnp.float32)
        * 0.125
    )
    query_pos = block_index * block_len + jnp.arange(block_len)
    allowed = jnp.arange(SEQ)[None, :] <= query_pos[:, None]
    return jnp.where(allowed, scores, NEG_LARGE)


def attention_forward(query_rows_local, key_all, value_all):
    block_len = min(512, SEQ)
    outputs = []
    logsums = []
    for block_index in range(SEQ // block_len):
        query_block = query_rows_local[:, block_index * block_len : (block_index + 1) * block_len]
        scores = causal_scores(query_block, key_all, block_index, block_len)
        row_max = jnp.max(scores, -1, keepdims=True)
        exponent = jnp.exp(scores - row_max)
        row_total = jnp.sum(exponent, -1, keepdims=True)
        probability = (exponent / row_total).astype(jnp.bfloat16)
        mixture = jnp.einsum(
            "bhqk,bkhd->bqhd", probability, value_all, preferred_element_type=jnp.float32
        )
        outputs.append(mixture.astype(jnp.bfloat16))
        logsums.append(row_max[..., 0] + jnp.log(row_total[..., 0]))
    return (jnp.concatenate(outputs, 1), jnp.concatenate(logsums, 2))


def attention_backward(query_rows_local, key_all, value_all, grad_mixture, logsums):
    block_len = min(512, SEQ)
    grad_queries = []
    grad_keys = jnp.zeros(key_all.shape, jnp.float32)
    value_gradient_rows = jnp.zeros(value_all.shape, jnp.float32)
    for block_index in range(SEQ // block_len):
        lower = block_index * block_len
        query_block = query_rows_local[:, lower : lower + block_len]
        grad_block = grad_mixture[:, lower : lower + block_len]
        scores = causal_scores(query_block, key_all, block_index, block_len)
        probability = jnp.exp(scores - logsums[:, :, lower : lower + block_len, None])
        grad_prob = jnp.einsum(
            "bqhd,bkhd->bhqk", grad_block, value_all, preferred_element_type=jnp.float32
        )
        row_delta = jnp.sum(grad_prob * probability, -1, keepdims=True)
        dscore = (0.125 * (probability * (grad_prob - row_delta))).astype(jnp.bfloat16)
        grad_queries.append(
            jnp.einsum(
                "bhqk,bkhd->bqhd", dscore, key_all, preferred_element_type=jnp.float32
            ).astype(jnp.bfloat16)
        )
        grad_keys = grad_keys + jnp.einsum(
            "bhqk,bqhd->bkhd", dscore, query_block, preferred_element_type=jnp.float32
        )
        value_gradient_rows = value_gradient_rows + jnp.einsum(
            "bhqk,bqhd->bkhd",
            probability.astype(jnp.bfloat16),
            grad_block,
            preferred_element_type=jnp.float32,
        )
    return (
        jnp.concatenate(grad_queries, 1),
        grad_keys.astype(jnp.bfloat16),
        value_gradient_rows.astype(jnp.bfloat16),
    )


def adam_step(factor_grad, weights, first_old, second_old, grad_norm):
    clipped = factor_grad * (CLIP_NORM / jnp.maximum(grad_norm, CLIP_NORM))
    first_new = BETA_ONE * first_old + (1.0 - BETA_ONE) * clipped
    second_new = BETA_TWO * second_old + (1.0 - BETA_TWO) * clipped * clipped
    first_hat = first_new / (1.0 - BETA_ONE**STEP)
    second_hat = second_new / (1.0 - BETA_TWO**STEP)
    weights_new = weights - LEARN_RATE * (
        first_hat / (jnp.sqrt(second_hat) + ADAM_EPSILON) + WEIGHT_DECAY * weights
    )
    return (clipped, weights_new, first_new, second_new)


def body(
    tokens_in,
    norm_params,
    query_key_value_weight,
    out_weight,
    fc_weight,
    proj_weight,
    factors,
    first_moment,
    second_moment,
    grad_out,
):
    tensor_size = lax.axis_size("tensor")
    tensor_rank = lax.axis_index("tensor")
    token_count = tokens_in.shape[0]
    doc_count = token_count // SEQ
    local_width = query_key_value_weight.shape[2]
    heads_here = local_width // HD
    row_count = token_count // tensor_size
    row_start = tensor_rank * row_count
    rank_count = factors.shape[1]
    full_width = factors.shape[2]
    inputs = tokens_in.astype(jnp.float32)
    first_normalized, unit_one, inverse_one = normalize(inputs, norm_params[0], norm_params[1])
    first_normalized_reduced = first_normalized.astype(jnp.bfloat16)
    factor_reduced_precision = factors.astype(jnp.bfloat16)
    column_offset = tensor_rank * local_width
    query_adapter_output = lax.dynamic_slice_in_dim(
        factor_reduced_precision[1], column_offset, local_width, 1
    )
    value_adapter_output = lax.dynamic_slice_in_dim(
        factor_reduced_precision[3], column_offset, local_width, 1
    )
    query_down_factor = product_with_transpose(
        first_normalized_reduced, factor_reduced_precision[0]
    ).astype(jnp.bfloat16)
    value_down_factor = product_with_transpose(
        first_normalized_reduced, factor_reduced_precision[2]
    ).astype(jnp.bfloat16)
    query_rows_local = (
        matrix_product(first_normalized_reduced, query_key_value_weight[0])
        + ADAPTER_SCALING * matrix_product(query_down_factor, query_adapter_output)
    ).astype(jnp.bfloat16)
    keys_low = matrix_product(first_normalized_reduced, query_key_value_weight[1]).astype(
        jnp.bfloat16
    )
    values_low = (
        matrix_product(first_normalized_reduced, query_key_value_weight[2])
        + ADAPTER_SCALING * matrix_product(value_down_factor, value_adapter_output)
    ).astype(jnp.bfloat16)
    head_shape = (doc_count, SEQ, heads_here, HD)
    query_heads = query_rows_local.reshape(head_shape)
    keys_heads = keys_low.reshape(head_shape)
    values_heads = values_low.reshape(head_shape)
    mixture, logsums = attention_forward(query_heads, keys_heads, values_heads)
    attn_part = matrix_product(mixture.reshape(token_count, local_width), out_weight)
    grad_full = grad_out.astype(jnp.float32)
    attn_rows = lax.psum_scatter(
        attn_part.astype(jnp.bfloat16), "tensor", scatter_dimension=0, tiled=True
    ).astype(jnp.float32)
    resid_rows = lax.dynamic_slice_in_dim(inputs, row_start, row_count, 0) + attn_rows
    normed_two_rows, unit_two, inverse_two = normalize(resid_rows, norm_params[2], norm_params[3])
    normed_two_low = lax.all_gather(
        normed_two_rows.astype(jnp.bfloat16), "tensor", axis=0, tiled=True
    )
    hidden_pre = matrix_product(normed_two_low, fc_weight)
    hidden_act, gelu_pull = jax.vjp(
        lambda argument: jax.nn.gelu(argument, approximate=True), hidden_pre
    )
    mlp_part = matrix_product(hidden_act.astype(jnp.bfloat16), proj_weight)
    grad_hidden = product_with_transpose(grad_out, proj_weight)
    grad_pre = gelu_pull(grad_hidden)[0].astype(jnp.bfloat16)
    second_part = product_with_transpose(grad_pre, fc_weight)
    out_rows = resid_rows + lax.psum_scatter(
        mlp_part.astype(jnp.bfloat16), "tensor", scatter_dimension=0, tiled=True
    ).astype(jnp.float32)
    second_rows = lax.psum_scatter(
        second_part.astype(jnp.bfloat16), "tensor", scatter_dimension=0, tiled=True
    ).astype(jnp.float32)
    resid_grad_rows = lax.dynamic_slice_in_dim(grad_full, row_start, row_count, 0) + normalize_back(
        second_rows, unit_two, inverse_two, norm_params[2]
    )
    resid_grad_low = lax.all_gather(
        resid_grad_rows.astype(jnp.bfloat16), "tensor", axis=0, tiled=True
    )
    grad_mixture = product_with_transpose(resid_grad_low, out_weight).astype(jnp.bfloat16)
    query_gradient, grad_keys, value_gradient_rows = attention_backward(
        query_heads, keys_heads, values_heads, grad_mixture.reshape(head_shape), logsums
    )
    query_gradient = query_gradient.reshape(token_count, local_width)
    grad_keys = grad_keys.reshape(token_count, local_width)
    value_gradient_rows = value_gradient_rows.reshape(token_count, local_width)
    stacked = jnp.stack((query_gradient, grad_keys, value_gradient_rows))
    first_part = jnp.einsum(
        "stc,sdc->td", stacked, query_key_value_weight, preferred_element_type=jnp.float32
    )
    query_up_factor = ADAPTER_SCALING * product_with_transpose(query_gradient, query_adapter_output)
    value_up_factor = ADAPTER_SCALING * product_with_transpose(
        value_gradient_rows, value_adapter_output
    )
    first_part = first_part + jnp.dot(
        query_up_factor,
        factor_reduced_precision[0].astype(jnp.float32),
        precision=lax.Precision.HIGHEST,
    )
    first_part = first_part + jnp.dot(
        value_up_factor,
        factor_reduced_precision[2].astype(jnp.float32),
        precision=lax.Precision.HIGHEST,
    )
    first_rows = lax.psum_scatter(
        first_part.astype(jnp.bfloat16), "tensor", scatter_dimension=0, tiled=True
    ).astype(jnp.float32)
    unit_rows = lax.dynamic_slice_in_dim(unit_one, row_start, row_count, 0)
    inverse_rows = lax.dynamic_slice_in_dim(inverse_one, row_start, row_count, 0)
    input_rows = resid_grad_rows + normalize_back(
        first_rows, unit_rows, inverse_rows, norm_params[0]
    )
    query_cross_term = transpose_then_product(query_gradient, first_normalized_reduced)
    value_cross_term = transpose_then_product(value_gradient_rows, first_normalized_reduced)
    query_down_gradient = ADAPTER_SCALING * jnp.dot(
        query_adapter_output.astype(jnp.float32), query_cross_term, precision=lax.Precision.HIGHEST
    )
    value_down_gradient = ADAPTER_SCALING * jnp.dot(
        value_adapter_output.astype(jnp.float32), value_cross_term, precision=lax.Precision.HIGHEST
    )
    empty_slot = jnp.zeros((rank_count, full_width), jnp.float32)
    up_grad_query = lax.dynamic_update_slice_in_dim(
        empty_slot,
        ADAPTER_SCALING * transpose_then_product(query_down_factor, query_gradient),
        column_offset,
        1,
    )
    up_grad_value = lax.dynamic_update_slice_in_dim(
        empty_slot,
        ADAPTER_SCALING * transpose_then_product(value_down_factor, value_gradient_rows),
        column_offset,
        1,
    )
    partial_grad = jnp.stack(
        (query_down_gradient, up_grad_query, value_down_gradient, up_grad_value)
    )
    reduced = lax.psum(partial_grad, ("dp", "tensor"))
    grad_norm = jnp.sqrt(jnp.sum(reduced * reduced))
    clipped, weights_new, first_new, second_new = adam_step(
        reduced, factors, first_moment, second_moment, grad_norm
    )
    return (
        out_rows.astype(jnp.bfloat16),
        input_rows,
        clipped,
        grad_norm,
        weights_new,
        first_new,
        second_new,
    )


MESH = pl.DeviceIdType.MESH
BF = jnp.bfloat16
F32 = jnp.float32
GROUPS = 8
PAIRS = 8


def mm(left, right):
    return jnp.dot(left, right, preferred_element_type=F32)


def mm_nt(left, right):
    return lax.dot_general(left, right, (((1,), (1,)), ((), ())), preferred_element_type=F32)


def mm_tn(left, right):
    return lax.dot_general(left, right, (((0,), (0,)), ((), ())), preferred_element_type=F32)


def flip(value, bit):
    return value + bit - 2 * bit * ((value // bit) % 2)


def unit_of(rows):
    centered = rows - jnp.mean(rows, -1, keepdims=True)
    inverse = lax.rsqrt(jnp.mean(centered * centered, -1, keepdims=True) + EPSILON)
    return centered * inverse, inverse


def unit_back(scaled, unit, inverse):
    return inverse * (
        scaled - jnp.mean(scaled, -1, keepdims=True) - unit * jnp.mean(scaled * unit, -1, keepdims=True)
    )


def fused_kernel(
    planes,
    tokens, norm_params, wqkv, w_out, w_fc, w_proj, factors, grad_out,
    bo_r, ig_r, summed,
    tok, n1, go, wq, wkv, wo, fcw, pw, kv, qs, p0, p1, mix, inv, attn_own, attn_s, attn_r,
    res, n2, acc_a, acc_b, gnt_s, gnt_r, gnt_xs, gnt_xr, mlp_s, mlp_r, mlp_xs, mlp_xr,
    gr_b, bo_f, bo_s, gq, dos, gno_s, gno_r, gno_xs, gno_xr, ig_s,
    f02, f1p, f3kv, down, gd_scr, fg_a, fg_q, fg_v, ps, ps_r, plane_buf, z_buf, fin,
    chain_send, chain_recv, pair_send, pair_recv, load_sem, ssem, rsem,
):
    d = lax.axis_index("dp")
    t = lax.axis_index("tensor")
    z, c, x, y = d // 2, d % 2, t % 2, t // 2
    odd = z % 2
    nbr = (flip(d, 1), t)
    prim = (d, flip(t, 1 + odd))
    sec = (d, flip(t, 2 - odd))
    plane = [(d, flip(t, 1)), (d, flip(t, 2)), (d, 3 - t)]
    x_nbr, y_nbr = plane[0], plane[1]
    zs = [(flip(d, 2 << k), t) for k in range(planes.bit_length() - 1)]
    owners = [(2 * z + y, 2 * h + x) for h in range(2)]
    at_home = [jnp.logical_and(c == y, h == y) for h in range(2)]
    quarter = [t, flip(t, 1 + odd), flip(t, 2 - odd), 3 - t]
    column = [pl.multiple_of(q * 256 + c * 128, 128) for q in quarter]

    def at(start, size):
        return pl.ds(pl.multiple_of(start, size), size)

    def rows_of(half, side):
        return at(512 * half + 256 * side, 256)

    def own_rows(h, side):
        return at(512 * h + 256 * side + 128 * c, 128)

    def other_rows(h, side):
        return at(512 * h + 256 * side + 128 * (1 - c), 128)

    def ff_own(h, side):
        return at(512 * side + 256 * h + 128 * c, 128)

    def ff_other(h, side):
        return at(512 * side + 256 * h + 128 * (1 - c), 128)

    def remote_to(src, dst, out_index, in_index, device):
        return pltpu.make_async_remote_copy(
            src_ref=src, dst_ref=dst, send_sem=ssem.at[out_index], recv_sem=rsem.at[in_index],
            device_id=device, device_id_type=MESH,
        )

    def remote(src, dst, index, device):
        return remote_to(src, dst, index, index, device)

    pending = []

    def drain():
        for wait in pending:
            wait()

    def send(copy):
        copy.start()
        pending.append(copy.wait_send)
        return copy

    lane = at(c * 128, 128)
    loads = [
        pltpu.make_async_copy(wqkv.at[1, :, lane], wkv.at[:, pl.ds(0, 128)], load_sem.at[0]),
        pltpu.make_async_copy(wqkv.at[2, :, lane], wkv.at[:, pl.ds(128, 128)], load_sem.at[1]),
        pltpu.make_async_copy(wqkv.at[0, :, lane], wq.at[:, pl.ds(0, 128)], load_sem.at[2]),
        pltpu.make_async_copy(w_out.at[lane, :], wo.at[pl.ds(0, 128), :], load_sem.at[3]),
        pltpu.make_async_copy(w_fc.at[:, at(c * 512, 512)], fcw.at[0], load_sem.at[4]),
        pltpu.make_async_copy(w_proj.at[at(c * 512, 512), :], pw.at[0], load_sem.at[5]),
    ]
    for load in loads:
        load.start()

    barrier = pltpu.get_barrier_semaphore()
    partners = [nbr, x_nbr, y_nbr] + zs
    for device in partners:
        pl.semaphore_signal(barrier, inc=1, device_id=device, device_id_type=MESH)
    pl.semaphore_wait(barrier, len(partners))

    doc = []
    for r in range(4):
        part = pl.ds(256 * r, 256)
        doc.append((tokens.at[part, :], tok.at[part, :], r))
    place = jnp.where(c == y, 0, 512)
    grads = [
        (grad_out.at[rows_of(h, x), :], go.at[at(place + 256 * h, 256), :], 4 + h) for h in range(2)
    ]
    other_place = 512 - place
    grads_in = [
        (grad_out.at[rows_of(h, x), :], go.at[at(other_place + 256 * h, 256), :], 4 + h) for h in range(2)
    ]
    for h in range(2):
        pltpu.make_async_copy(*grads[h][:2], load_sem.at[6 + h]).start()

    @pl.when(c == y)
    def _():
        for src, dst, index in doc:
            remote(src, dst, index, nbr).start()
            pltpu.make_async_copy(src, dst, rsem.at[index]).start()

    def doc_sent():
        @pl.when(c == y)
        def _():
            for item in doc:
                remote(*item, nbr).wait_send()

    pending.append(doc_sent)
    for item in grads:
        send(remote(*item, nbr))

    def doc_wait(index):
        remote(*doc[index], nbr).wait_recv()

    def piece(slot, group):
        matrix, a = group // 2, group % 2
        if matrix < 2:
            return wkv.at[pl.ds(512 * a, 512), pl.ds(256 * slot + 128 * matrix, 128)]
        if matrix == 2:
            return wq.at[pl.ds(512 * a, 512), pl.ds(128 * slot, 128)]
        return wo.at[pl.ds(128 * slot + 64 * a, 64), :]

    def hop(slot, group):
        return pltpu.make_async_remote_copy(
            src_ref=piece(1 if slot > 1 else 0, group), dst_ref=piece(slot, group),
            send_sem=chain_send.at[slot - 1, group], recv_sem=chain_recv.at[slot - 1, group],
            device_id=(prim, zs[0], sec)[slot - 1], device_id_type=MESH,
        )

    def pump(group, later=True):
        hop(1, group).wait_recv()
        for slot in (2, 3):
            hop(slot, group).start()
            if later:
                pending.append(hop(slot, group).wait_send)

    def passed(groups):
        for group in groups:
            hop(2, group).wait_recv()
            hop(3, group).wait_recv()

    def pair_piece(slot, pair, parity):
        h, q = pair // 4, pair % 4
        if q < 2:
            return fcw.at[slot, at(512 * q + 256 * parity, 256), pl.ds(256 * h, 256)]
        return pw.at[slot, at(256 * h + 128 * (q - 2) + 64 * parity, 64), :]

    def pair_hop(step, pair, parity):
        return pltpu.make_async_remote_copy(
            src_ref=pair_piece(step, pair, parity), dst_ref=pair_piece(1, pair, parity),
            send_sem=pair_send.at[step, pair], recv_sem=pair_recv.at[step, pair],
            device_id=(x_nbr, zs[0])[step], device_id_type=MESH,
        )

    def pair_pump(pair):
        pair_hop(0, pair, odd).wait_recv()
        pair_hop(1, pair, odd).start()

    def pair_wait(pairs):
        for pair in pairs:
            pair_hop(1, pair, 1 - odd).wait_recv()

    for matrix in range(4):
        loads[matrix].wait()
        send(hop(1, 2 * matrix))
        send(hop(1, 2 * matrix + 1))
    loads[4].wait()
    loads[5].wait()
    for pair in range(2):
        pair_hop(0, pair, odd).start()

    fpad = acc_b.at[0:128, :]
    fpad[...] = jnp.zeros(fpad.shape, F32)
    fpad[0:4, :] = factors[0]
    fpad[4:8, :] = factors[2]
    f02[...] = fpad[...].astype(BF)
    fpad[...] = jnp.zeros(fpad.shape, F32)
    for s in range(4):
        fpad[0:4, 128 * s : 128 * s + 128] = factors[1, :, pl.ds(column[s], 128)]
    f1p[...] = fpad[:, :512].astype(BF)
    fpad[...] = jnp.zeros(fpad.shape, F32)
    for s in range(4):
        fpad[4:8, 256 * s + 128 : 256 * s + 256] = factors[3, :, pl.ds(column[s], 128)]
    f3kv[...] = fpad[...].astype(BF)
    ps[...] = jnp.zeros_like(ps)

    gain_one, bias_one = norm_params[0:1, :], norm_params[1:2, :]
    gain_two, bias_two = norm_params[2:3, :], norm_params[3:4, :]
    def first_norm(r):
        doc_wait(r)

        @pl.loop(0, 2)
        def _(q):
            rows = at(256 * r + 128 * q, 128)
            unit, _ = unit_of(tok[rows, :].astype(F32))
            n1[rows, :] = (unit * gain_one + bias_one).astype(BF)

    first_norm(0)
    first_norm(1)
    pump(0)
    first_norm(2)
    first_norm(3)

    @pl.loop(0, 2)
    def _(r):
        rows = at(512 * r, 512)
        down[rows, :] = mm_nt(n1[rows, :], f02[...]).astype(BF)

    pump(1)
    acc_a[...] = jnp.zeros_like(acc_a)
    acc_b[...] = jnp.zeros_like(acc_b)
    first_head = lax.broadcasted_iota(jnp.int32, (256, 512), 1) % 128 < 64
    first_lanes = first_head[:, 0:128]

    def stacked(rows, lanes):
        return jnp.concatenate((jnp.where(lanes, rows, 0.0), jnp.where(lanes, 0.0, rows)), 0)

    p_refs = (p0, p1)
    column_pos = lax.broadcasted_iota(jnp.int32, (512, 512), 1)
    row_pos = lax.broadcasted_iota(jnp.int32, (512, 512), 0) % 256 + 256 * x
    allowed = column_pos <= row_pos

    @pl.loop(0, 4)
    def _(s):
        @pl.when(s == 1)
        def _():
            for group in range(2, 6):
                pump(group, False)

        @pl.when(s == 2)
        def _():
            pump(6, False)
            passed(range(0, 6))

        @pl.when(s == 3)
        def _():
            pump(7, False)
            for pair in range(2, PAIRS):
                pair_hop(0, pair, odd).start()

        both_lanes, lanes = at(256 * s, 256), at(128 * s, 128)
        keys, values = at(256 * s, 128), at(256 * s + 128, 128)

        @pl.loop(0, 2)
        def _(r):
            rows = at(512 * r, 512)
            kv[rows, both_lanes] = (
                mm(n1[rows, :], wkv[:, both_lanes]) + ADAPTER_SCALING * mm(down[rows, :], f3kv[:, both_lanes])
            ).astype(BF)

        for h in range(2):
            rows = rows_of(h, x)
            query = mm(n1[rows, :], wq[:, lanes]) + ADAPTER_SCALING * mm(down[rows, :], f1p[:, lanes])
            qs[h, :, lanes] = stacked(query.astype(BF).astype(F32) * 0.125, first_lanes).astype(BF)
        scores = [mm_nt(qs[h, :, lanes], kv[0 : 512 * (h + 1), keys]) for h in range(2)]
        kept = []
        for h in range(2):
            last = jnp.where(allowed, scores[h][:, 512 * h :], NEG_LARGE)
            block = jnp.concatenate((scores[h][:, :512], last), 1) if h else last
            exponent = jnp.exp(block - jnp.max(block, -1, keepdims=True))
            inverse = 1.0 / jnp.sum(exponent, -1, keepdims=True)
            p_refs[h][s] = exponent.astype(BF)
            inv[h, :, lanes] = jnp.broadcast_to(inverse, (512, 128))
            kept.append((exponent.astype(BF), inverse))
        for h in range(2):
            both = mm(kept[h][0], kv[0 : 512 * (h + 1), values]) * kept[h][1]
            mix[256 * h : 256 * h + 256, lanes] = jnp.where(first_lanes, both[0:256], both[256:512])

    for group in range(2, GROUPS):
        pending.append(hop(2, group).wait_send)
        pending.append(hop(3, group).wait_send)
    for pair in range(PAIRS):
        pending.append(pair_hop(0, pair, odd).wait_send)
    passed(range(6, 8))

    def heads_out(sub):
        rows = [mix[at(256 * h + 128 * sub, 128), :].astype(BF) for h in range(2)]
        return mm(jnp.concatenate(rows, 0), wo[...])

    attn_s[...] = heads_out(1 - c).astype(BF)
    to_nbr = send(remote(attn_s, attn_r, 8, nbr))
    attn_own[...] = heads_out(c)
    pair_pump(0)
    to_nbr.wait_recv()

    gathered = []
    for h in range(2):
        part = slice(128 * h, 128 * h + 128)
        rows = own_rows(h, x)
        residual = tok[rows, :].astype(F32) + attn_own[part, :] + attn_r[part, :].astype(F32)
        res[part, :] = residual
        unit, _ = unit_of(residual)
        rows = ff_own(h, 0)
        n2[rows, :] = (unit * gain_two + bias_two).astype(BF)
        gathered.append(send(remote(n2.at[rows, :], n2.at[ff_own(h, 1), :], 11 + h, y_nbr)))
        gathered.append(send(remote(n2.at[rows, :], n2.at[rows, :], 9 + h, nbr)))
    pair_pump(1)
    for h in range(2):
        pltpu.make_async_copy(*grads[h][:2], load_sem.at[6 + h]).wait()
        remote(*grads_in[h], nbr).wait_recv()
    gathered[1].wait_recv()
    gathered[3].wait_recv()

    def pass_on(h):
        gathered[2 * h].wait_recv()
        rows = ff_own(h, 1)
        remote(n2.at[rows, :], n2.at[rows, :], 13 + h, nbr).start()

    def passed_on(h):
        rows = ff_own(h, 1)
        return remote(n2.at[rows, :], n2.at[rows, :], 13 + h, nbr)

    def sum_copy(source, target, first, h, j):
        part = pl.ds(128 * j, 128)
        return remote(source.at[h, part, :], target.at[h, part, :], first + 2 * h + j, nbr)

    def to_core(acc, source, target, first, h):
        for j, side in enumerate((1, 0)):
            source[h, 128 * j : 128 * j + 128, :] = acc[ff_other(h, side), :].astype(BF)
            sum_copy(source, target, first, h, j).start()

    def to_side(acc, source, target, out, out_target, first, side_first, h):
        sum_copy(source, target, first, h, 0).wait_recv()
        out[h] = (acc[ff_own(h, 1), :] + target[h, 0:128, :].astype(F32)).astype(BF)
        return send(remote(out.at[h], out_target.at[h], side_first + h, y_nbr))

    @pl.loop(0, 8)
    def _(unit):
        @pl.when(unit == 1)
        def _():
            pair_pump(2)

        @pl.when(unit == 2)
        def _():
            pair_pump(3)
            pass_on(0)
            pair_pump(4)
            pair_wait(range(0, 4))

        @pl.when(unit == 3)
        def _():
            pair_pump(5)
            pass_on(1)
            for h in range(2):
                passed_on(h).wait_recv()

        @pl.when(unit == 4)
        def _():
            pair_pump(6)

        @pl.when(unit == 5)
        def _():
            pair_pump(7)

        @pl.when(unit == 6)
        def _():
            pair_wait(range(4, 8))

        @pl.when(unit == 7)
        def _():
            to_core(acc_b, gnt_s, gnt_r, 40, 1)

        flag = lambda value: jnp.where(value, 1, 0)
        slot = flag(jnp.logical_or(unit == 2, unit >= 5))
        part = flag(jnp.logical_or(unit >= 6, jnp.logical_or(unit == 1, unit == 4)))
        side = flag(unit >= 3)
        last_half = 7 - unit
        starts = [
            jnp.where(unit < 6, 512 * side + 256 * h, 512 * h + 256 * last_half) for h in range(2)
        ]
        tiles = [at(start, 256) for start in starts]
        lanes = at(256 * part, 256)
        pre = [mm(n2[rows, :], fcw[slot, :, lanes]) for rows in tiles]
        grad_act = [mm_nt(go[rows, :], pw[slot, lanes, :]) for rows in tiles]
        for rows, hidden, grad in zip(tiles, pre, grad_act):
            square = hidden * hidden
            tanh = jnp.tanh(GELU_SCALE * hidden * (1.0 + GELU_CUBE * square))
            half_up = 0.5 * (1.0 + tanh)
            slope = half_up + (0.5 * GELU_SCALE) * hidden * (1.0 - tanh * tanh) * (
                1.0 + 3.0 * GELU_CUBE * square
            )
            acc_b[rows, :] += mm_nt((grad * slope).astype(BF), fcw[slot, :, lanes])
            acc_a[rows, :] += mm((hidden * half_up).astype(BF), pw[slot, lanes, :])

    for pair in range(PAIRS):
        pending.append(pair_hop(1, pair, odd).wait_send)
    for h in range(2):
        pending.append(passed_on(h).wait_send)
        for j in range(2):
            pending.append(sum_copy(gnt_s, gnt_r, 40, h, j).wait_send)
            pending.append(sum_copy(mlp_s, mlp_r, 44, h, j).wait_send)

    gnt_side, mlp_side = [None, None], [None, None]
    to_core(acc_b, gnt_s, gnt_r, 40, 0)
    for h in (1, 0):
        gnt_side[h] = to_side(acc_b, gnt_s, gnt_r, gnt_xs, gnt_xr, 40, 17, h)
    for h in (1, 0):
        to_core(acc_a, mlp_s, mlp_r, 44, h)
    for h in (1, 0):
        mlp_side[h] = to_side(acc_a, mlp_s, mlp_r, mlp_xs, mlp_xr, 44, 21, h)
    for h in range(2):
        part = slice(128 * h, 128 * h + 128)
        sum_copy(mlp_s, mlp_r, 44, h, 1).wait_recv()
        bo_f[part, :] = res[part, :] + acc_a[ff_own(h, 0), :] + mlp_r[h, 128:256, :].astype(F32)

    gr = attn_own

    def residual_back(h):
        part = slice(128 * h, 128 * h + 128)
        unit, inverse = unit_of(res[part, :])
        sum_copy(gnt_s, gnt_r, 40, h, 1).wait_recv()
        total = acc_b[ff_own(h, 0), :] + gnt_r[h, 128:256, :].astype(F32)
        gnt_side[h].wait_recv()
        scaled = (total + gnt_xr[h].astype(F32)) * gain_two
        grad = go[ff_own(h, 0), :].astype(F32) + unit_back(scaled, unit, inverse)
        gr[part, :] = grad
        local = at(256 * h + 128 * c, 128)
        gr_b[local, :] = grad.astype(BF)
        return send(remote(gr_b.at[local, :], gr_b.at[local, :], 23 + h, nbr))

    def mixture_back(h):
        grad_mixture = mm_nt(gr_b[256 * h : 256 * h + 256, :], wo[...])
        dos[h] = (stacked(grad_mixture, first_head) * inv[h]).astype(BF)

    to_nbr = residual_back(1)
    to_nbr.wait_recv()
    mixture_back(1)

    def scores_back(h, first, count):
        size = 512 * (h + 1)
        group = [first + k for k in range(count)]
        lanes = [at(128 * s, 128) for s in group]
        k_lanes = [at(256 * s, 128) for s in group]
        v_lanes = [at(256 * s + 128, 128) for s in group]
        grads = [dos[h, :, lane] for lane in lanes]
        grad_prob = [mm_nt(grad, kv[0:size, lane]) for lane, grad in zip(v_lanes, grads)]
        dscores = []
        for s, lane, grad, block in zip(group, lanes, grads, grad_prob):
            mixture = mix[256 * h : 256 * h + 256, lane]
            delta = jnp.sum(
                grad.astype(F32) * jnp.concatenate((mixture, mixture), 0), -1, keepdims=True
            )
            dscores.append((p_refs[h][s].astype(F32) * (block - delta)).astype(BF))
        for k, (s, lane, grad, dscore) in enumerate(zip(group, lanes, grads, dscores)):
            both = 0.125 * mm(dscore, kv[0:size, k_lanes[k]])
            gq[:, lane] = jnp.where(first_lanes, both[0:256], both[256:512]).astype(BF)
            grad_keys = mm_tn(dscore, qs[h, :, lane])
            grad_values = mm_tn(p_refs[h][s], grad)
            if h:
                acc_a[:, k_lanes[k]] = grad_keys
                acc_a[:, v_lanes[k]] = grad_values
            else:
                acc_a[0:512, k_lanes[k]] += grad_keys
                acc_a[0:512, v_lanes[k]] += grad_values

    def factors_back(h):
        rows = slice(512 * h, 512 * h + 512)
        grads = acc_a[rows, :].astype(BF)
        query = gq[...]
        gd_scr[...] = ADAPTER_SCALING * mm_nt(grads, f3kv[...])
        gd_scr[at(256 * x, 256), :] += ADAPTER_SCALING * mm_nt(query, f1p[...])
        terms = (
            mm_tn(gd_scr[...].astype(BF), n1[rows, :])[0:8],
            mm_tn(down[rows_of(h, x), :], query)[0:8],
            mm_tn(down[rows, :], grads)[0:8],
        )
        for total, term in zip((fg_a, fg_q, fg_v), terms):
            total[...] = term if h else total[...] + term

    def rows_copy(h, j):
        part = pl.ds(128 * j, 128)
        return remote(gno_s.at[h, part, :], gno_r.at[h, part, :], 27 + 2 * h + j, nbr)

    def rows_back(h, j):
        side = x if j else 1 - x
        rows = rows_of(h, side)
        grad = mm_nt(acc_a[rows, :].astype(BF), wkv[...])
        grad += mm(gd_scr[at(256 * side, 256), :].astype(BF), f02[...])
        if j:
            grad += mm_nt(gq[...], wq[...])
        acc_b[rows, :] = grad
        gno_s[h, 128 * j : 128 * j + 128, :] = acc_b[other_rows(h, side), :].astype(BF)
        send(rows_copy(h, j))

    side_copies = {}

    def reduce_rows(h):
        rows_copy(h, 0).wait_recv()
        gno_xs[h] = (acc_b[own_rows(h, 1 - x), :] + gno_r[h, 0:128, :].astype(F32)).astype(BF)
        for k in range(2):
            part = pl.ds(64 * k, 64)
            side_copies[h, k] = send(
                remote(gno_xs.at[h, part, :], gno_xr.at[h, part, :], 48 + 2 * h + k, x_nbr)
            )

    def to_owner(src, dst, h, out_index, in_index):
        @pl.when(at_home[h])
        def _():
            pltpu.make_async_copy(src, dst, rsem.at[in_index + c]).start()

        @pl.when(jnp.logical_not(at_home[h]))
        def _():
            remote_to(src, dst, out_index, in_index + c, owners[h]).start()

        def sent():
            @pl.when(jnp.logical_not(at_home[h]))
            def _():
                remote_to(src, dst, out_index, in_index + c, owners[h]).wait_send()

        pending.append(sent)

    def input_rows(h, k):
        if k == 0:
            rows_copy(h, 1).wait_recv()
        start = 512 * h + 256 * x + 128 * c + 64 * k
        rows, part = at(start, 64), slice(64 * k, 64 * k + 64)
        unit, inverse = unit_of(tok[rows, :].astype(F32))
        total = acc_b[rows, :] + gno_r[h, 128 + 64 * k : 192 + 64 * k, :].astype(F32)
        side_copies[h, k].wait_recv()
        scaled = (total + gno_xr[h, part, :].astype(F32)) * gain_one
        out = slice(128 * h + 64 * k, 128 * h + 64 * k + 64)
        ig_s[out, :] = (gr[out, :] + unit_back(scaled, unit, inverse)).astype(BF)
        to_owner(ig_s.at[out, :], ig_r.at[at(128 * c + 64 * k, 64), :], h, 52 + 2 * h + k, 56 + 2 * k)

    @pl.loop(0, 2)
    def _(group):
        scores_back(1, 2 * group, 2)

    to_nbr = residual_back(0)
    factors_back(1)
    rows_back(1, 0)
    rows_back(1, 1)
    to_nbr.wait_recv()
    mixture_back(0)
    reduce_rows(1)
    scores_back(0, 0, 4)

    factors_back(0)

    ps[0:8, :] = fg_a[...]
    down_rows = lax.broadcasted_iota(jnp.int32, (8, 128), 0) < 4
    for s in range(4):
        ps[8:16, pl.ds(column[s], 128)] = ADAPTER_SCALING * jnp.where(
            down_rows, fg_q[:, 128 * s : 128 * s + 128], fg_v[:, 256 * s + 128 : 256 * s + 256]
        )
    core_sum = send(remote(ps, ps_r, 33, nbr))
    rows_back(0, 0)
    core_sum.wait_recv()
    eight = at(8 * c, 8)
    plane_buf[t] = ps[eight, :] + ps_r[eight, :]
    copies = [
        send(remote(plane_buf.at[t], plane_buf.at[t], 35 + k, device)) for k, device in enumerate(plane)
    ]
    reduce_rows(0)
    for h in (1, 0):
        part = slice(128 * h, 128 * h + 128)
        mlp_side[h].wait_recv()
        bo_s[part, :] = (bo_f[part, :] + mlp_xr[h].astype(F32)).astype(BF)
        to_owner(bo_s.at[part, :], bo_r.at[at(128 * c, 128), :], h, 60 + h, 62)
    rows_back(0, 1)
    for k in range(2):
        input_rows(1, k)
    for copy in copies:
        copy.wait_recv()
    z_buf[0] = plane_buf[0] + plane_buf[1] + plane_buf[2] + plane_buf[3]

    def z_copy(k):
        return remote(z_buf.at[2 * k], z_buf.at[2 * k + 1], 64 + k, zs[k])

    for k in range(len(zs)):
        send(z_copy(k))
        if k < 2:
            input_rows(0, k)
        z_copy(k).wait_recv()
        z_buf[2 * k + 2] = z_buf[2 * k] + z_buf[2 * k + 1]
    for k in range(len(zs), 2):
        input_rows(0, k)
    fin[eight, :] = z_buf[2 * len(zs)]
    send(remote(fin.at[eight, :], fin.at[eight, :], 34, nbr))
    theirs = at(8 - 8 * c, 8)
    remote(fin.at[theirs, :], fin.at[theirs, :], 34, nbr).wait_recv()
    result = pltpu.make_async_copy(fin, summed, load_sem.at[0])
    result.start()

    for core in range(2):
        part = pl.ds(128 * core, 128)
        remote_to(bo_s.at[pl.ds(0, 128), :], bo_r.at[part, :], 60, 62 + core, nbr).wait_recv()
        for k in range(2):
            part = pl.ds(128 * core + 64 * k, 64)
            remote_to(ig_s.at[pl.ds(0, 64), :], ig_r.at[part, :], 52, 56 + 2 * k + core, nbr).wait_recv()
    result.wait()
    drain()


def finish_kernel(
    factors, first_moment, second_moment, bo_in, ig_in, sum_in,
    block_out, input_grad, clipped, grad_norm, factors_new, first_new, second_new,
    bo, ig, summed, grads, sem, out_sem,
):
    pairs = [(sum_in, summed), (bo_in, bo), (ig_in, ig)]
    loads = [pltpu.make_async_copy(*pair, sem.at[k]) for k, pair in enumerate(pairs)]
    for load in loads:
        load.start()
    loads[0].wait()
    grad = summed[...]
    norm = jnp.sqrt(jnp.sum(grad * grad, (0, 1), keepdims=True))
    grad_norm[...] = norm
    grad = grad * (CLIP_NORM / jnp.maximum(norm, CLIP_NORM))
    for index, first in enumerate((0, 8, 4, 12)):
        value, weights = grad[first : first + 4], factors[index]
        first_value = BETA_ONE * first_moment[index] + (1.0 - BETA_ONE) * value
        second_value = BETA_TWO * second_moment[index] + (1.0 - BETA_TWO) * value * value
        first_hat = first_value / (1.0 - BETA_ONE**STEP)
        second_hat = second_value / (1.0 - BETA_TWO**STEP)
        clipped[index] = value
        first_new[index] = first_value
        second_new[index] = second_value
        factors_new[index] = weights - LEARN_RATE * (
            first_hat / (jnp.sqrt(second_hat) + ADAM_EPSILON) + WEIGHT_DECAY * weights
        )
    loads[1].wait()
    stores = [pltpu.make_async_copy(bo, block_out, out_sem.at[0])]
    stores[0].start()
    loads[2].wait()
    grads[...] = ig[...].astype(F32)
    stores.append(pltpu.make_async_copy(grads, input_grad, out_sem.at[1]))
    stores[1].start()
    for store in stores:
        store.wait()


def fused(planes, tokens, norm_params, wqkv, w_out, w_fc, w_proj, factors, first, second, grad_out):
    vmem = pl.BlockSpec(memory_space=pltpu.VMEM)
    hbm = pl.BlockSpec(memory_space=pl.ANY)

    def buf(*shape):
        return pltpu.VMEM(shape, BF)

    def acc(*shape):
        return pltpu.VMEM(shape, F32)

    def sems(*shape):
        return pltpu.SemaphoreType.DMA(shape)

    quarter = [buf(256, 1024)] * 2
    halves, eighths = [buf(2, 256, 1024)] * 2, [buf(2, 128, 1024)] * 2
    scratch = [
        buf(1024, 1024), buf(1024, 1024), buf(1024, 1024), buf(1024, 512), buf(1024, 1024), buf(512, 1024),
        buf(2, 1024, 512), buf(2, 512, 1024), buf(1024, 1024), buf(2, 512, 512), buf(4, 512, 512),
        buf(4, 512, 1024), acc(512, 512), acc(2, 512, 512), acc(256, 1024), *quarter,
        acc(256, 1024), buf(1024, 1024), acc(1024, 1024), acc(1024, 1024),
        *halves, *eighths, *halves, *eighths,
        buf(512, 1024), acc(256, 1024), buf(256, 1024), buf(256, 512), buf(2, 512, 512),
        *halves, *eighths, buf(256, 1024),
        buf(128, 1024), buf(128, 512), buf(128, 1024), buf(1024, 128), acc(512, 128),
        acc(8, 1024), acc(8, 512), acc(8, 1024), acc(16, 1024), acc(16, 1024), acc(4, 8, 1024),
        acc(2 * planes, 8, 1024), acc(16, 1024),
        sems(3, GROUPS), sems(3, GROUPS), sems(2, PAIRS), sems(2, PAIRS), sems(8), sems(64 + planes),
        sems(64 + planes),
    ]
    rows = jax.ShapeDtypeStruct((256, 1024), BF)
    passed = pl.pallas_call(
        functools.partial(fused_kernel, planes),
        name="block_step",
        out_shape=(rows, rows, jax.ShapeDtypeStruct((16, 1024), F32)),
        in_specs=[hbm, vmem, hbm, hbm, hbm, hbm, vmem, hbm],
        out_specs=(hbm,) * 3,
        scratch_shapes=scratch,
        compiler_params=pltpu.CompilerParams(
            collective_id=1, has_side_effects=True, vmem_limit_bytes=63 << 20
        ),
    )(tokens, norm_params, wqkv, w_out, w_fc, w_proj, factors, grad_out)
    small = jax.ShapeDtypeStruct((4, 4, 1024), F32)
    outs = pl.pallas_call(
        finish_kernel,
        name="finish_step",
        out_shape=(
            rows, jax.ShapeDtypeStruct((256, 1024), F32), small,
            jax.ShapeDtypeStruct((1, 1), F32), small, small, small,
        ),
        in_specs=[vmem] * 3 + [hbm] * 3,
        out_specs=(hbm, hbm) + (vmem,) * 5,
        scratch_shapes=[*quarter, acc(16, 1024), acc(256, 1024), sems(3), sems(2)],
        compiler_params=pltpu.CompilerParams(vmem_limit_bytes=62 << 20),
    )(factors, first, second, *passed)
    return outs[:3] + (outs[3].reshape(()),) + outs[4:]


def solution(mesh):
    placed = (
        P("dp", None),
        P(),
        P(None, None, "tensor"),
        P("tensor", None),
        P(None, "tensor"),
        P("tensor", None),
        P(),
        P(),
        P(),
        P("dp", None),
    )
    planes = mesh.shape["dp"] // 2

    def step(*args):
        rows, width = args[0].shape
        shapes = (rows, width, args[4].shape[1], args[2].shape[2], args[6].shape[1])
        fits = mesh.shape["tensor"] == 4 and mesh.shape["dp"] % 4 == 0
        if fits and shapes == (SEQ, 1024, 1024, 256, 4):
            return fused(planes, *args)
        return body(*args)

    return jax.shard_map(
        step,
        mesh=mesh,
        in_specs=placed,
        out_specs=(P(("dp", "tensor"), None), P(("dp", "tensor"), None), P(), P(), P(), P(), P()),
        check_vma=False,
    )
```

```python
import functools

import jax
import jax.numpy as jnp
from jax import lax
from jax.experimental import pallas as pl
from jax.experimental.pallas import tpu as pltpu
from jax.sharding import PartitionSpec as P

HD = 64
SEQ = 1024
STEP = 5


EPSILON = 1e-05
ADAPTER_SCALING = 8.0
CLIP_NORM = 16.0
LEARN_RATE = 0.03
BETA_ONE = 0.5
BETA_TWO = 0.5
WEIGHT_DECAY = 0.01
ADAM_EPSILON = 1e-08
NEG_LARGE = -1e30
GELU_SCALE = 0.7978845608028654
GELU_CUBE = 0.044715


def matrix_product(left, right):
    return jnp.dot(left, right, preferred_element_type=jnp.float32)


def product_with_transpose(left, right):
    return lax.dot_general(
        left, right, (((1,), (1,)), ((), ())), preferred_element_type=jnp.float32
    )


def transpose_then_product(left, right):
    return lax.dot_general(
        left, right, (((0,), (0,)), ((), ())), preferred_element_type=jnp.float32
    )


def normalize(value_rows_local, gain_vec, bias_vec):
    centered = value_rows_local - jnp.mean(value_rows_local, -1, keepdims=True)
    inverse = lax.rsqrt(jnp.mean(centered * centered, -1, keepdims=True) + EPSILON)
    unit_rows = centered * inverse
    return (unit_rows * gain_vec + bias_vec, unit_rows, inverse)


def normalize_back(incoming, unit_rows, inverse, gain_vec):
    scaled = incoming * gain_vec
    return inverse * (
        scaled
        - jnp.mean(scaled, -1, keepdims=True)
        - unit_rows * jnp.mean(scaled * unit_rows, -1, keepdims=True)
    )


def causal_scores(query_block, key_all, block_index, block_len):
    scores = (
        jnp.einsum("bqhd,bkhd->bhqk", query_block, key_all, preferred_element_type=jnp.float32)
        * 0.125
    )
    query_pos = block_index * block_len + jnp.arange(block_len)
    allowed = jnp.arange(SEQ)[None, :] <= query_pos[:, None]
    return jnp.where(allowed, scores, NEG_LARGE)


def attention_forward(query_rows_local, key_all, value_all):
    block_len = min(512, SEQ)
    outputs = []
    logsums = []
    for block_index in range(SEQ // block_len):
        query_block = query_rows_local[:, block_index * block_len : (block_index + 1) * block_len]
        scores = causal_scores(query_block, key_all, block_index, block_len)
        row_max = jnp.max(scores, -1, keepdims=True)
        exponent = jnp.exp(scores - row_max)
        row_total = jnp.sum(exponent, -1, keepdims=True)
        probability = (exponent / row_total).astype(jnp.bfloat16)
        mixture = jnp.einsum(
            "bhqk,bkhd->bqhd", probability, value_all, preferred_element_type=jnp.float32
        )
        outputs.append(mixture.astype(jnp.bfloat16))
        logsums.append(row_max[..., 0] + jnp.log(row_total[..., 0]))
    return (jnp.concatenate(outputs, 1), jnp.concatenate(logsums, 2))


def attention_backward(query_rows_local, key_all, value_all, grad_mixture, logsums):
    block_len = min(512, SEQ)
    grad_queries = []
    grad_keys = jnp.zeros(key_all.shape, jnp.float32)
    value_gradient_rows = jnp.zeros(value_all.shape, jnp.float32)
    for block_index in range(SEQ // block_len):
        lower = block_index * block_len
        query_block = query_rows_local[:, lower : lower + block_len]
        grad_block = grad_mixture[:, lower : lower + block_len]
        scores = causal_scores(query_block, key_all, block_index, block_len)
        probability = jnp.exp(scores - logsums[:, :, lower : lower + block_len, None])
        grad_prob = jnp.einsum(
            "bqhd,bkhd->bhqk", grad_block, value_all, preferred_element_type=jnp.float32
        )
        row_delta = jnp.sum(grad_prob * probability, -1, keepdims=True)
        dscore = (0.125 * (probability * (grad_prob - row_delta))).astype(jnp.bfloat16)
        grad_queries.append(
            jnp.einsum(
                "bhqk,bkhd->bqhd", dscore, key_all, preferred_element_type=jnp.float32
            ).astype(jnp.bfloat16)
        )
        grad_keys = grad_keys + jnp.einsum(
            "bhqk,bqhd->bkhd", dscore, query_block, preferred_element_type=jnp.float32
        )
        value_gradient_rows = value_gradient_rows + jnp.einsum(
            "bhqk,bqhd->bkhd",
            probability.astype(jnp.bfloat16),
            grad_block,
            preferred_element_type=jnp.float32,
        )
    return (
        jnp.concatenate(grad_queries, 1),
        grad_keys.astype(jnp.bfloat16),
        value_gradient_rows.astype(jnp.bfloat16),
    )


def adam_step(factor_grad, weights, first_old, second_old, grad_norm):
    clipped = factor_grad * (CLIP_NORM / jnp.maximum(grad_norm, CLIP_NORM))
    first_new = BETA_ONE * first_old + (1.0 - BETA_ONE) * clipped
    second_new = BETA_TWO * second_old + (1.0 - BETA_TWO) * clipped * clipped
    first_hat = first_new / (1.0 - BETA_ONE**STEP)
    second_hat = second_new / (1.0 - BETA_TWO**STEP)
    weights_new = weights - LEARN_RATE * (
        first_hat / (jnp.sqrt(second_hat) + ADAM_EPSILON) + WEIGHT_DECAY * weights
    )
    return (clipped, weights_new, first_new, second_new)


def body(
    tokens_in,
    norm_params,
    query_key_value_weight,
    out_weight,
    fc_weight,
    proj_weight,
    factors,
    first_moment,
    second_moment,
    grad_out,
):
    tensor_size = lax.axis_size("tensor")
    tensor_rank = lax.axis_index("tensor")
    token_count = tokens_in.shape[0]
    doc_count = token_count // SEQ
    local_width = query_key_value_weight.shape[2]
    heads_here = local_width // HD
    row_count = token_count // tensor_size
    row_start = tensor_rank * row_count
    rank_count = factors.shape[1]
    full_width = factors.shape[2]
    inputs = tokens_in.astype(jnp.float32)
    first_normalized, unit_one, inverse_one = normalize(inputs, norm_params[0], norm_params[1])
    first_normalized_reduced = first_normalized.astype(jnp.bfloat16)
    factor_reduced_precision = factors.astype(jnp.bfloat16)
    column_offset = tensor_rank * local_width
    query_adapter_output = lax.dynamic_slice_in_dim(
        factor_reduced_precision[1], column_offset, local_width, 1
    )
    value_adapter_output = lax.dynamic_slice_in_dim(
        factor_reduced_precision[3], column_offset, local_width, 1
    )
    query_down_factor = product_with_transpose(
        first_normalized_reduced, factor_reduced_precision[0]
    ).astype(jnp.bfloat16)
    value_down_factor = product_with_transpose(
        first_normalized_reduced, factor_reduced_precision[2]
    ).astype(jnp.bfloat16)
    query_rows_local = (
        matrix_product(first_normalized_reduced, query_key_value_weight[0])
        + ADAPTER_SCALING * matrix_product(query_down_factor, query_adapter_output)
    ).astype(jnp.bfloat16)
    keys_low = matrix_product(first_normalized_reduced, query_key_value_weight[1]).astype(
        jnp.bfloat16
    )
    values_low = (
        matrix_product(first_normalized_reduced, query_key_value_weight[2])
        + ADAPTER_SCALING * matrix_product(value_down_factor, value_adapter_output)
    ).astype(jnp.bfloat16)
    head_shape = (doc_count, SEQ, heads_here, HD)
    query_heads = query_rows_local.reshape(head_shape)
    keys_heads = keys_low.reshape(head_shape)
    values_heads = values_low.reshape(head_shape)
    mixture, logsums = attention_forward(query_heads, keys_heads, values_heads)
    attn_part = matrix_product(mixture.reshape(token_count, local_width), out_weight)
    grad_full = grad_out.astype(jnp.float32)
    attn_rows = lax.psum_scatter(
        attn_part.astype(jnp.bfloat16), "tensor", scatter_dimension=0, tiled=True
    ).astype(jnp.float32)
    resid_rows = lax.dynamic_slice_in_dim(inputs, row_start, row_count, 0) + attn_rows
    normed_two_rows, unit_two, inverse_two = normalize(resid_rows, norm_params[2], norm_params[3])
    normed_two_low = lax.all_gather(
        normed_two_rows.astype(jnp.bfloat16), "tensor", axis=0, tiled=True
    )
    hidden_pre = matrix_product(normed_two_low, fc_weight)
    hidden_act, gelu_pull = jax.vjp(
        lambda argument: jax.nn.gelu(argument, approximate=True), hidden_pre
    )
    mlp_part = matrix_product(hidden_act.astype(jnp.bfloat16), proj_weight)
    grad_hidden = product_with_transpose(grad_out, proj_weight)
    grad_pre = gelu_pull(grad_hidden)[0].astype(jnp.bfloat16)
    second_part = product_with_transpose(grad_pre, fc_weight)
    out_rows = resid_rows + lax.psum_scatter(
        mlp_part.astype(jnp.bfloat16), "tensor", scatter_dimension=0, tiled=True
    ).astype(jnp.float32)
    second_rows = lax.psum_scatter(
        second_part.astype(jnp.bfloat16), "tensor", scatter_dimension=0, tiled=True
    ).astype(jnp.float32)
    resid_grad_rows = lax.dynamic_slice_in_dim(grad_full, row_start, row_count, 0) + normalize_back(
        second_rows, unit_two, inverse_two, norm_params[2]
    )
    resid_grad_low = lax.all_gather(
        resid_grad_rows.astype(jnp.bfloat16), "tensor", axis=0, tiled=True
    )
    grad_mixture = product_with_transpose(resid_grad_low, out_weight).astype(jnp.bfloat16)
    query_gradient, grad_keys, value_gradient_rows = attention_backward(
        query_heads, keys_heads, values_heads, grad_mixture.reshape(head_shape), logsums
    )
    query_gradient = query_gradient.reshape(token_count, local_width)
    grad_keys = grad_keys.reshape(token_count, local_width)
    value_gradient_rows = value_gradient_rows.reshape(token_count, local_width)
    stacked = jnp.stack((query_gradient, grad_keys, value_gradient_rows))
    first_part = jnp.einsum(
        "stc,sdc->td", stacked, query_key_value_weight, preferred_element_type=jnp.float32
    )
    query_up_factor = ADAPTER_SCALING * product_with_transpose(query_gradient, query_adapter_output)
    value_up_factor = ADAPTER_SCALING * product_with_transpose(
        value_gradient_rows, value_adapter_output
    )
    first_part = first_part + jnp.dot(
        query_up_factor,
        factor_reduced_precision[0].astype(jnp.float32),
        precision=lax.Precision.HIGHEST,
    )
    first_part = first_part + jnp.dot(
        value_up_factor,
        factor_reduced_precision[2].astype(jnp.float32),
        precision=lax.Precision.HIGHEST,
    )
    first_rows = lax.psum_scatter(
        first_part.astype(jnp.bfloat16), "tensor", scatter_dimension=0, tiled=True
    ).astype(jnp.float32)
    unit_rows = lax.dynamic_slice_in_dim(unit_one, row_start, row_count, 0)
    inverse_rows = lax.dynamic_slice_in_dim(inverse_one, row_start, row_count, 0)
    input_rows = resid_grad_rows + normalize_back(
        first_rows, unit_rows, inverse_rows, norm_params[0]
    )
    query_cross_term = transpose_then_product(query_gradient, first_normalized_reduced)
    value_cross_term = transpose_then_product(value_gradient_rows, first_normalized_reduced)
    query_down_gradient = ADAPTER_SCALING * jnp.dot(
        query_adapter_output.astype(jnp.float32), query_cross_term, precision=lax.Precision.HIGHEST
    )
    value_down_gradient = ADAPTER_SCALING * jnp.dot(
        value_adapter_output.astype(jnp.float32), value_cross_term, precision=lax.Precision.HIGHEST
    )
    empty_slot = jnp.zeros((rank_count, full_width), jnp.float32)
    up_grad_query = lax.dynamic_update_slice_in_dim(
        empty_slot,
        ADAPTER_SCALING * transpose_then_product(query_down_factor, query_gradient),
        column_offset,
        1,
    )
    up_grad_value = lax.dynamic_update_slice_in_dim(
        empty_slot,
        ADAPTER_SCALING * transpose_then_product(value_down_factor, value_gradient_rows),
        column_offset,
        1,
    )
    partial_grad = jnp.stack(
        (query_down_gradient, up_grad_query, value_down_gradient, up_grad_value)
    )
    reduced = lax.psum(partial_grad, ("dp", "tensor"))
    grad_norm = jnp.sqrt(jnp.sum(reduced * reduced))
    clipped, weights_new, first_new, second_new = adam_step(
        reduced, factors, first_moment, second_moment, grad_norm
    )
    return (
        out_rows.astype(jnp.bfloat16),
        input_rows,
        clipped,
        grad_norm,
        weights_new,
        first_new,
        second_new,
    )


MESH = pl.DeviceIdType.MESH
BF = jnp.bfloat16
F32 = jnp.float32
GROUPS = 8
PAIRS = 8


def mm(left, right):
    return jnp.dot(left, right, preferred_element_type=F32)


def mm_nt(left, right):
    return lax.dot_general(left, right, (((1,), (1,)), ((), ())), preferred_element_type=F32)


def mm_tn(left, right):
    return lax.dot_general(left, right, (((0,), (0,)), ((), ())), preferred_element_type=F32)


def flip(value, bit):
    return value + bit - 2 * bit * ((value // bit) % 2)


def unit_of(rows):
    centered = rows - jnp.mean(rows, -1, keepdims=True)
    inverse = lax.rsqrt(jnp.mean(centered * centered, -1, keepdims=True) + EPSILON)
    return centered * inverse, inverse


def unit_back(scaled, unit, inverse):
    return inverse * (
        scaled - jnp.mean(scaled, -1, keepdims=True) - unit * jnp.mean(scaled * unit, -1, keepdims=True)
    )


def fused_kernel(
    planes,
    tokens, norm_params, wqkv, w_out, w_fc, w_proj, factors, grad_out,
    bo_r, ig_r, summed,
    tok, n1, go, wq, wkv, wo, fcw, pw, kv, qs, p0, p1, mix, inv, attn_own, attn_s, attn_r,
    res, n2, acc_a, acc_b, gnt_s, gnt_r, gnt_xs, gnt_xr, mlp_s, mlp_r, mlp_xs, mlp_xr,
    gr_b, bo_f, bo_s, gq, dos, gno_s, gno_r, gno_xs, gno_xr, ig_s,
    f02, f1p, f3kv, down, gd_scr, fg_a, fg_q, fg_v, ps, ps_r, plane_buf, z_buf, fin,
    chain_send, chain_recv, pair_send, pair_recv, load_sem, ssem, rsem,
):
    d = lax.axis_index("dp")
    t = lax.axis_index("tensor")
    z, c, x, y = d // 2, d % 2, t % 2, t // 2
    odd = z % 2
    nbr = (flip(d, 1), t)
    prim = (d, flip(t, 1 + odd))
    sec = (d, flip(t, 2 - odd))
    plane = [(d, flip(t, 1)), (d, flip(t, 2)), (d, 3 - t)]
    x_nbr, y_nbr = plane[0], plane[1]
    zs = [(flip(d, 2 << k), t) for k in range(planes.bit_length() - 1)]
    owners = [(2 * z + y, 2 * h + x) for h in range(2)]
    at_home = [jnp.logical_and(c == y, h == y) for h in range(2)]
    quarter = [t, flip(t, 1 + odd), flip(t, 2 - odd), 3 - t]
    column = [pl.multiple_of(q * 256 + c * 128, 128) for q in quarter]

    def at(start, size):
        return pl.ds(pl.multiple_of(start, size), size)

    def rows_of(half, side):
        return at(512 * half + 256 * side, 256)

    def own_rows(h, side):
        return at(512 * h + 256 * side + 128 * c, 128)

    def other_rows(h, side):
        return at(512 * h + 256 * side + 128 * (1 - c), 128)

    def ff_own(h, side):
        return at(512 * side + 256 * h + 128 * c, 128)

    def ff_other(h, side):
        return at(512 * side + 256 * h + 128 * (1 - c), 128)

    def remote_to(src, dst, out_index, in_index, device):
        return pltpu.make_async_remote_copy(
            src_ref=src, dst_ref=dst, send_sem=ssem.at[out_index], recv_sem=rsem.at[in_index],
            device_id=device, device_id_type=MESH,
        )

    def remote(src, dst, index, device):
        return remote_to(src, dst, index, index, device)

    pending = []

    def drain():
        for wait in pending:
            wait()

    def send(copy):
        copy.start()
        pending.append(copy.wait_send)
        return copy

    lane = at(c * 128, 128)
    loads = [
        pltpu.make_async_copy(wqkv.at[1, :, lane], wkv.at[:, pl.ds(0, 128)], load_sem.at[0]),
        pltpu.make_async_copy(wqkv.at[2, :, lane], wkv.at[:, pl.ds(128, 128)], load_sem.at[1]),
        pltpu.make_async_copy(wqkv.at[0, :, lane], wq.at[:, pl.ds(0, 128)], load_sem.at[2]),
        pltpu.make_async_copy(w_out.at[lane, :], wo.at[pl.ds(0, 128), :], load_sem.at[3]),
        pltpu.make_async_copy(w_fc.at[:, at(c * 512, 512)], fcw.at[0], load_sem.at[4]),
        pltpu.make_async_copy(w_proj.at[at(c * 512, 512), :], pw.at[0], load_sem.at[5]),
    ]
    for load in loads:
        load.start()

    barrier = pltpu.get_barrier_semaphore()
    partners = [nbr, x_nbr, y_nbr] + zs
    for device in partners:
        pl.semaphore_signal(barrier, inc=1, device_id=device, device_id_type=MESH)
    pl.semaphore_wait(barrier, len(partners))

    doc = []
    for r in range(4):
        part = pl.ds(256 * r, 256)
        doc.append((tokens.at[part, :], tok.at[part, :], r))
    place = jnp.where(c == y, 0, 512)
    grads = [
        (grad_out.at[rows_of(h, x), :], go.at[at(place + 256 * h, 256), :], 4 + h) for h in range(2)
    ]
    other_place = 512 - place
    grads_in = [
        (grad_out.at[rows_of(h, x), :], go.at[at(other_place + 256 * h, 256), :], 4 + h) for h in range(2)
    ]
    for h in range(2):
        pltpu.make_async_copy(*grads[h][:2], load_sem.at[6 + h]).start()

    @pl.when(c == y)
    def _():
        for src, dst, index in doc:
            remote(src, dst, index, nbr).start()
            pltpu.make_async_copy(src, dst, rsem.at[index]).start()

    def doc_sent():
        @pl.when(c == y)
        def _():
            for item in doc:
                remote(*item, nbr).wait_send()

    pending.append(doc_sent)
    for item in grads:
        send(remote(*item, nbr))

    def doc_wait(index):
        remote(*doc[index], nbr).wait_recv()

    def piece(slot, group):
        matrix, a = group // 2, group % 2
        if matrix < 2:
            return wkv.at[pl.ds(512 * a, 512), pl.ds(256 * slot + 128 * matrix, 128)]
        if matrix == 2:
            return wq.at[pl.ds(512 * a, 512), pl.ds(128 * slot, 128)]
        return wo.at[pl.ds(128 * slot + 64 * a, 64), :]

    def hop(slot, group):
        return pltpu.make_async_remote_copy(
            src_ref=piece(1 if slot > 1 else 0, group), dst_ref=piece(slot, group),
            send_sem=chain_send.at[slot - 1, group], recv_sem=chain_recv.at[slot - 1, group],
            device_id=(prim, zs[0], sec)[slot - 1], device_id_type=MESH,
        )

    def pump(group, later=True):
        hop(1, group).wait_recv()
        for slot in (2, 3):
            hop(slot, group).start()
            if later:
                pending.append(hop(slot, group).wait_send)

    def passed(groups):
        for group in groups:
            hop(2, group).wait_recv()
            hop(3, group).wait_recv()

    def pair_piece(slot, pair, parity):
        h, q = pair // 4, pair % 4
        if q < 2:
            return fcw.at[slot, at(512 * q + 256 * parity, 256), pl.ds(256 * h, 256)]
        return pw.at[slot, at(256 * h + 128 * (q - 2) + 64 * parity, 64), :]

    def pair_hop(step, pair, parity):
        return pltpu.make_async_remote_copy(
            src_ref=pair_piece(step, pair, parity), dst_ref=pair_piece(1, pair, parity),
            send_sem=pair_send.at[step, pair], recv_sem=pair_recv.at[step, pair],
            device_id=(x_nbr, zs[0])[step], device_id_type=MESH,
        )

    def pair_pump(pair):
        pair_hop(0, pair, odd).wait_recv()
        pair_hop(1, pair, odd).start()

    def pair_wait(pairs):
        for pair in pairs:
            pair_hop(1, pair, 1 - odd).wait_recv()

    for matrix in range(4):
        loads[matrix].wait()
        send(hop(1, 2 * matrix))
        send(hop(1, 2 * matrix + 1))
    loads[4].wait()
    loads[5].wait()
    for pair in range(2):
        pair_hop(0, pair, odd).start()

    fpad = acc_b.at[0:128, :]
    fpad[...] = jnp.zeros(fpad.shape, F32)
    fpad[0:4, :] = factors[0]
    fpad[4:8, :] = factors[2]
    f02[...] = fpad[...].astype(BF)
    fpad[...] = jnp.zeros(fpad.shape, F32)
    for s in range(4):
        fpad[0:4, 128 * s : 128 * s + 128] = factors[1, :, pl.ds(column[s], 128)]
    f1p[...] = fpad[:, :512].astype(BF)
    fpad[...] = jnp.zeros(fpad.shape, F32)
    for s in range(4):
        fpad[4:8, 256 * s + 128 : 256 * s + 256] = factors[3, :, pl.ds(column[s], 128)]
    f3kv[...] = fpad[...].astype(BF)
    ps[...] = jnp.zeros_like(ps)

    gain_one, bias_one = norm_params[0:1, :], norm_params[1:2, :]
    gain_two, bias_two = norm_params[2:3, :], norm_params[3:4, :]
    def first_norm(r):
        doc_wait(r)

        @pl.loop(0, 2)
        def _(q):
            rows = at(256 * r + 128 * q, 128)
            unit, _ = unit_of(tok[rows, :].astype(F32))
            n1[rows, :] = (unit * gain_one + bias_one).astype(BF)

    first_norm(0)
    first_norm(1)
    pump(0)
    first_norm(2)
    first_norm(3)

    @pl.loop(0, 2)
    def _(r):
        rows = at(512 * r, 512)
        down[rows, :] = mm_nt(n1[rows, :], f02[...]).astype(BF)

    pump(1)
    acc_a[...] = jnp.zeros_like(acc_a)
    acc_b[...] = jnp.zeros_like(acc_b)
    first_head = lax.broadcasted_iota(jnp.int32, (256, 512), 1) % 128 < 64
    first_lanes = first_head[:, 0:128]

    def stacked(rows, lanes):
        return jnp.concatenate((jnp.where(lanes, rows, 0.0), jnp.where(lanes, 0.0, rows)), 0)

    p_refs = (p0, p1)
    column_pos = lax.broadcasted_iota(jnp.int32, (512, 512), 1)
    row_pos = lax.broadcasted_iota(jnp.int32, (512, 512), 0) % 256 + 256 * x
    allowed = column_pos <= row_pos

    @pl.loop(0, 4)
    def _(s):
        @pl.when(s == 1)
        def _():
            for group in range(2, 6):
                pump(group, False)

        @pl.when(s == 2)
        def _():
            pump(6, False)
            passed(range(0, 6))

        @pl.when(s == 3)
        def _():
            pump(7, False)
            for pair in range(2, PAIRS):
                pair_hop(0, pair, odd).start()

        both_lanes, lanes = at(256 * s, 256), at(128 * s, 128)
        keys, values = at(256 * s, 128), at(256 * s + 128, 128)

        @pl.loop(0, 2)
        def _(r):
            rows = at(512 * r, 512)
            kv[rows, both_lanes] = (
                mm(n1[rows, :], wkv[:, both_lanes]) + ADAPTER_SCALING * mm(down[rows, :], f3kv[:, both_lanes])
            ).astype(BF)

        for h in range(2):
            rows = rows_of(h, x)
            query = mm(n1[rows, :], wq[:, lanes]) + ADAPTER_SCALING * mm(down[rows, :], f1p[:, lanes])
            qs[h, :, lanes] = stacked(query.astype(BF).astype(F32) * 0.125, first_lanes).astype(BF)
        scores = [mm_nt(qs[h, :, lanes], kv[0 : 512 * (h + 1), keys]) for h in range(2)]
        kept = []
        for h in range(2):
            last = jnp.where(allowed, scores[h][:, 512 * h :], NEG_LARGE)
            block = jnp.concatenate((scores[h][:, :512], last), 1) if h else last
            exponent = jnp.exp(block - jnp.max(block, -1, keepdims=True))
            inverse = 1.0 / jnp.sum(exponent, -1, keepdims=True)
            p_refs[h][s] = exponent.astype(BF)
            inv[h, :, lanes] = jnp.broadcast_to(inverse, (512, 128))
            kept.append((exponent.astype(BF), inverse))
        for h in range(2):
            both = mm(kept[h][0], kv[0 : 512 * (h + 1), values]) * kept[h][1]
            mix[256 * h : 256 * h + 256, lanes] = jnp.where(first_lanes, both[0:256], both[256:512])

    for group in range(2, GROUPS):
        pending.append(hop(2, group).wait_send)
        pending.append(hop(3, group).wait_send)
    for pair in range(PAIRS):
        pending.append(pair_hop(0, pair, odd).wait_send)
    pair_pump(0)
    passed(range(6, 8))

    def heads_out(sub):
        rows = [mix[at(256 * h + 128 * sub, 128), :].astype(BF) for h in range(2)]
        return mm(jnp.concatenate(rows, 0), wo[...])

    attn_s[...] = heads_out(1 - c).astype(BF)
    to_nbr = send(remote(attn_s, attn_r, 8, nbr))
    pair_pump(1)
    attn_own[...] = heads_out(c)
    pair_pump(2)
    to_nbr.wait_recv()

    gathered = []
    for h in range(2):
        part = slice(128 * h, 128 * h + 128)
        rows = own_rows(h, x)
        residual = tok[rows, :].astype(F32) + attn_own[part, :] + attn_r[part, :].astype(F32)
        res[part, :] = residual
        unit, _ = unit_of(residual)
        rows = ff_own(h, 0)
        n2[rows, :] = (unit * gain_two + bias_two).astype(BF)
        gathered.append(send(remote(n2.at[rows, :], n2.at[ff_own(h, 1), :], 11 + h, y_nbr)))
        gathered.append(send(remote(n2.at[rows, :], n2.at[rows, :], 9 + h, nbr)))
    pair_pump(3)
    for h in range(2):
        pltpu.make_async_copy(*grads[h][:2], load_sem.at[6 + h]).wait()
        remote(*grads_in[h], nbr).wait_recv()
    gathered[1].wait_recv()
    gathered[3].wait_recv()

    def pass_on(h):
        gathered[2 * h].wait_recv()
        rows = ff_own(h, 1)
        remote(n2.at[rows, :], n2.at[rows, :], 13 + h, nbr).start()

    def passed_on(h):
        rows = ff_own(h, 1)
        return remote(n2.at[rows, :], n2.at[rows, :], 13 + h, nbr)

    def sum_copy(source, target, first, h, j):
        part = pl.ds(128 * j, 128)
        return remote(source.at[h, part, :], target.at[h, part, :], first + 2 * h + j, nbr)

    def to_core(acc, source, target, first, h):
        for j, side in enumerate((1, 0)):
            source[h, 128 * j : 128 * j + 128, :] = acc[ff_other(h, side), :].astype(BF)
            sum_copy(source, target, first, h, j).start()

    def to_side(acc, source, target, out, out_target, first, side_first, h):
        sum_copy(source, target, first, h, 0).wait_recv()
        out[h] = (acc[ff_own(h, 1), :] + target[h, 0:128, :].astype(F32)).astype(BF)
        return send(remote(out.at[h], out_target.at[h], side_first + h, y_nbr))

    @pl.loop(0, 8)
    def _(unit):
        @pl.when(unit == 1)
        def _():
            pair_pump(4)

        @pl.when(unit == 2)
        def _():
            pair_wait(range(0, 4))
            pass_on(0)
            pair_pump(5)

        @pl.when(unit == 3)
        def _():
            pair_pump(6)
            pass_on(1)
            pair_pump(7)
            for h in range(2):
                passed_on(h).wait_recv()

        @pl.when(unit == 6)
        def _():
            pair_wait(range(4, 8))

        @pl.when(unit == 7)
        def _():
            to_core(acc_b, gnt_s, gnt_r, 40, 1)

        flag = lambda value: jnp.where(value, 1, 0)
        slot = flag(jnp.logical_or(unit == 2, unit >= 5))
        part = flag(jnp.logical_or(unit >= 6, jnp.logical_or(unit == 1, unit == 4)))
        side = flag(unit >= 3)
        last_half = 7 - unit
        starts = [
            jnp.where(unit < 6, 512 * side + 256 * h, 512 * h + 256 * last_half) for h in range(2)
        ]
        tiles = [at(start, 256) for start in starts]
        lanes = at(256 * part, 256)
        pre = [mm(n2[rows, :], fcw[slot, :, lanes]) for rows in tiles]
        grad_act = [mm_nt(go[rows, :], pw[slot, lanes, :]) for rows in tiles]
        for rows, hidden, grad in zip(tiles, pre, grad_act):
            square = hidden * hidden
            tanh = jnp.tanh(GELU_SCALE * hidden * (1.0 + GELU_CUBE * square))
            half_up = 0.5 * (1.0 + tanh)
            slope = half_up + (0.5 * GELU_SCALE) * hidden * (1.0 - tanh * tanh) * (
                1.0 + 3.0 * GELU_CUBE * square
            )
            acc_b[rows, :] += mm_nt((grad * slope).astype(BF), fcw[slot, :, lanes])
            acc_a[rows, :] += mm((hidden * half_up).astype(BF), pw[slot, lanes, :])

    for pair in range(PAIRS):
        pending.append(pair_hop(1, pair, odd).wait_send)
    for h in range(2):
        pending.append(passed_on(h).wait_send)
        for j in range(2):
            pending.append(sum_copy(gnt_s, gnt_r, 40, h, j).wait_send)
            pending.append(sum_copy(mlp_s, mlp_r, 44, h, j).wait_send)

    gnt_side, mlp_side = [None, None], [None, None]
    to_core(acc_b, gnt_s, gnt_r, 40, 0)
    for h in (1, 0):
        gnt_side[h] = to_side(acc_b, gnt_s, gnt_r, gnt_xs, gnt_xr, 40, 17, h)
    for h in (1, 0):
        to_core(acc_a, mlp_s, mlp_r, 44, h)
    for h in (1, 0):
        mlp_side[h] = to_side(acc_a, mlp_s, mlp_r, mlp_xs, mlp_xr, 44, 21, h)
    for h in range(2):
        part = slice(128 * h, 128 * h + 128)
        sum_copy(mlp_s, mlp_r, 44, h, 1).wait_recv()
        bo_f[part, :] = res[part, :] + acc_a[ff_own(h, 0), :] + mlp_r[h, 128:256, :].astype(F32)

    gr = attn_own

    def residual_back(h):
        part = slice(128 * h, 128 * h + 128)
        unit, inverse = unit_of(res[part, :])
        sum_copy(gnt_s, gnt_r, 40, h, 1).wait_recv()
        total = acc_b[ff_own(h, 0), :] + gnt_r[h, 128:256, :].astype(F32)
        gnt_side[h].wait_recv()
        scaled = (total + gnt_xr[h].astype(F32)) * gain_two
        grad = go[ff_own(h, 0), :].astype(F32) + unit_back(scaled, unit, inverse)
        gr[part, :] = grad
        local = at(256 * h + 128 * c, 128)
        gr_b[local, :] = grad.astype(BF)
        return send(remote(gr_b.at[local, :], gr_b.at[local, :], 23 + h, nbr))

    def mixture_back(h):
        grad_mixture = mm_nt(gr_b[256 * h : 256 * h + 256, :], wo[...])
        dos[h] = (stacked(grad_mixture, first_head) * inv[h]).astype(BF)

    to_nbr = residual_back(1)
    to_nbr.wait_recv()
    mixture_back(1)

    def scores_back(h, first, count):
        size = 512 * (h + 1)
        group = [first + k for k in range(count)]
        lanes = [at(128 * s, 128) for s in group]
        k_lanes = [at(256 * s, 128) for s in group]
        v_lanes = [at(256 * s + 128, 128) for s in group]
        grads = [dos[h, :, lane] for lane in lanes]
        grad_prob = [mm_nt(grad, kv[0:size, lane]) for lane, grad in zip(v_lanes, grads)]
        dscores = []
        for s, lane, grad, block in zip(group, lanes, grads, grad_prob):
            mixture = mix[256 * h : 256 * h + 256, lane]
            delta = jnp.sum(
                grad.astype(F32) * jnp.concatenate((mixture, mixture), 0), -1, keepdims=True
            )
            dscores.append((p_refs[h][s].astype(F32) * (block - delta)).astype(BF))
        for k, (s, lane, grad, dscore) in enumerate(zip(group, lanes, grads, dscores)):
            both = 0.125 * mm(dscore, kv[0:size, k_lanes[k]])
            gq[:, lane] = jnp.where(first_lanes, both[0:256], both[256:512]).astype(BF)
            grad_keys = mm_tn(dscore, qs[h, :, lane])
            grad_values = mm_tn(p_refs[h][s], grad)
            if h:
                acc_a[:, k_lanes[k]] = grad_keys
                acc_a[:, v_lanes[k]] = grad_values
            else:
                acc_a[0:512, k_lanes[k]] += grad_keys
                acc_a[0:512, v_lanes[k]] += grad_values

    def factors_back(h):
        rows = slice(512 * h, 512 * h + 512)
        grads = acc_a[rows, :].astype(BF)
        query = gq[...]
        gd_scr[...] = ADAPTER_SCALING * mm_nt(grads, f3kv[...])
        gd_scr[at(256 * x, 256), :] += ADAPTER_SCALING * mm_nt(query, f1p[...])
        terms = (
            mm_tn(gd_scr[...].astype(BF), n1[rows, :])[0:8],
            mm_tn(down[rows_of(h, x), :], query)[0:8],
            mm_tn(down[rows, :], grads)[0:8],
        )
        for total, term in zip((fg_a, fg_q, fg_v), terms):
            total[...] = term if h else total[...] + term

    def rows_copy(h, j):
        part = pl.ds(128 * j, 128)
        return remote(gno_s.at[h, part, :], gno_r.at[h, part, :], 27 + 2 * h + j, nbr)

    def rows_back(h, j):
        side = x if j else 1 - x
        rows = rows_of(h, side)
        grad = mm_nt(acc_a[rows, :].astype(BF), wkv[...])
        grad += mm(gd_scr[at(256 * side, 256), :].astype(BF), f02[...])
        if j:
            grad += mm_nt(gq[...], wq[...])
        acc_b[rows, :] = grad
        gno_s[h, 128 * j : 128 * j + 128, :] = acc_b[other_rows(h, side), :].astype(BF)
        send(rows_copy(h, j))

    side_copies = {}

    def reduce_rows(h):
        rows_copy(h, 0).wait_recv()
        gno_xs[h] = (acc_b[own_rows(h, 1 - x), :] + gno_r[h, 0:128, :].astype(F32)).astype(BF)
        for k in range(2):
            part = pl.ds(64 * k, 64)
            side_copies[h, k] = send(
                remote(gno_xs.at[h, part, :], gno_xr.at[h, part, :], 48 + 2 * h + k, x_nbr)
            )

    def to_owner(src, dst, h, out_index, in_index):
        @pl.when(at_home[h])
        def _():
            pltpu.make_async_copy(src, dst, rsem.at[in_index + c]).start()

        @pl.when(jnp.logical_not(at_home[h]))
        def _():
            remote_to(src, dst, out_index, in_index + c, owners[h]).start()

        def sent():
            @pl.when(jnp.logical_not(at_home[h]))
            def _():
                remote_to(src, dst, out_index, in_index + c, owners[h]).wait_send()

        pending.append(sent)

    def input_rows(h, k):
        if k == 0:
            rows_copy(h, 1).wait_recv()
        start = 512 * h + 256 * x + 128 * c + 64 * k
        rows, part = at(start, 64), slice(64 * k, 64 * k + 64)
        unit, inverse = unit_of(tok[rows, :].astype(F32))
        total = acc_b[rows, :] + gno_r[h, 128 + 64 * k : 192 + 64 * k, :].astype(F32)
        side_copies[h, k].wait_recv()
        scaled = (total + gno_xr[h, part, :].astype(F32)) * gain_one
        out = slice(128 * h + 64 * k, 128 * h + 64 * k + 64)
        ig_s[out, :] = (gr[out, :] + unit_back(scaled, unit, inverse)).astype(BF)
        to_owner(ig_s.at[out, :], ig_r.at[at(128 * c + 64 * k, 64), :], h, 52 + 2 * h + k, 56 + 2 * k)

    @pl.loop(0, 2)
    def _(group):
        scores_back(1, 2 * group, 2)

    to_nbr = residual_back(0)
    factors_back(1)
    rows_back(1, 0)
    rows_back(1, 1)
    to_nbr.wait_recv()
    mixture_back(0)
    reduce_rows(1)
    scores_back(0, 0, 4)

    factors_back(0)

    ps[0:8, :] = fg_a[...]
    down_rows = lax.broadcasted_iota(jnp.int32, (8, 128), 0) < 4
    for s in range(4):
        ps[8:16, pl.ds(column[s], 128)] = ADAPTER_SCALING * jnp.where(
            down_rows, fg_q[:, 128 * s : 128 * s + 128], fg_v[:, 256 * s + 128 : 256 * s + 256]
        )
    core_sum = send(remote(ps, ps_r, 33, nbr))
    rows_back(0, 0)
    core_sum.wait_recv()
    eight = at(8 * c, 8)
    plane_buf[t] = ps[eight, :] + ps_r[eight, :]
    copies = [
        send(remote(plane_buf.at[t], plane_buf.at[t], 35 + k, device)) for k, device in enumerate(plane)
    ]
    reduce_rows(0)
    for h in (1, 0):
        part = slice(128 * h, 128 * h + 128)
        mlp_side[h].wait_recv()
        bo_s[part, :] = (bo_f[part, :] + mlp_xr[h].astype(F32)).astype(BF)
        to_owner(bo_s.at[part, :], bo_r.at[at(128 * c, 128), :], h, 60 + h, 62)
    rows_back(0, 1)
    for k in range(2):
        input_rows(1, k)
    for copy in copies:
        copy.wait_recv()
    z_buf[0] = plane_buf[0] + plane_buf[1] + plane_buf[2] + plane_buf[3]

    def z_copy(k):
        return remote(z_buf.at[2 * k], z_buf.at[2 * k + 1], 64 + k, zs[k])

    for k in range(len(zs)):
        send(z_copy(k))
        if k < 2:
            input_rows(0, k)
        z_copy(k).wait_recv()
        z_buf[2 * k + 2] = z_buf[2 * k] + z_buf[2 * k + 1]
    for k in range(len(zs), 2):
        input_rows(0, k)
    fin[eight, :] = z_buf[2 * len(zs)]
    send(remote(fin.at[eight, :], fin.at[eight, :], 34, nbr))
    theirs = at(8 - 8 * c, 8)
    remote(fin.at[theirs, :], fin.at[theirs, :], 34, nbr).wait_recv()
    result = pltpu.make_async_copy(fin, summed, load_sem.at[0])
    result.start()

    for core in range(2):
        part = pl.ds(128 * core, 128)
        remote_to(bo_s.at[pl.ds(0, 128), :], bo_r.at[part, :], 60, 62 + core, nbr).wait_recv()
        for k in range(2):
            part = pl.ds(128 * core + 64 * k, 64)
            remote_to(ig_s.at[pl.ds(0, 64), :], ig_r.at[part, :], 52, 56 + 2 * k + core, nbr).wait_recv()
    result.wait()
    drain()


def finish_kernel(
    factors, first_moment, second_moment, bo_in, ig_in, sum_in,
    block_out, input_grad, clipped, grad_norm, factors_new, first_new, second_new,
    bo, ig, summed, grads, sem, out_sem,
):
    pairs = [(sum_in, summed), (bo_in, bo), (ig_in, ig)]
    loads = [pltpu.make_async_copy(*pair, sem.at[k]) for k, pair in enumerate(pairs)]
    for load in loads:
        load.start()
    loads[0].wait()
    grad = summed[...]
    norm = jnp.sqrt(jnp.sum(grad * grad, (0, 1), keepdims=True))
    grad_norm[...] = norm
    grad = grad * (CLIP_NORM / jnp.maximum(norm, CLIP_NORM))
    for index, first in enumerate((0, 8, 4, 12)):
        value, weights = grad[first : first + 4], factors[index]
        first_value = BETA_ONE * first_moment[index] + (1.0 - BETA_ONE) * value
        second_value = BETA_TWO * second_moment[index] + (1.0 - BETA_TWO) * value * value
        first_hat = first_value / (1.0 - BETA_ONE**STEP)
        second_hat = second_value / (1.0 - BETA_TWO**STEP)
        clipped[index] = value
        first_new[index] = first_value
        second_new[index] = second_value
        factors_new[index] = weights - LEARN_RATE * (
            first_hat / (jnp.sqrt(second_hat) + ADAM_EPSILON) + WEIGHT_DECAY * weights
        )
    loads[1].wait()
    stores = [pltpu.make_async_copy(bo, block_out, out_sem.at[0])]
    stores[0].start()
    loads[2].wait()
    grads[...] = ig[...].astype(F32)
    stores.append(pltpu.make_async_copy(grads, input_grad, out_sem.at[1]))
    stores[1].start()
    for store in stores:
        store.wait()


def fused(planes, tokens, norm_params, wqkv, w_out, w_fc, w_proj, factors, first, second, grad_out):
    vmem = pl.BlockSpec(memory_space=pltpu.VMEM)
    hbm = pl.BlockSpec(memory_space=pl.ANY)

    def buf(*shape):
        return pltpu.VMEM(shape, BF)

    def acc(*shape):
        return pltpu.VMEM(shape, F32)

    def sems(*shape):
        return pltpu.SemaphoreType.DMA(shape)

    quarter = [buf(256, 1024)] * 2
    halves, eighths = [buf(2, 256, 1024)] * 2, [buf(2, 128, 1024)] * 2
    scratch = [
        buf(1024, 1024), buf(1024, 1024), buf(1024, 1024), buf(1024, 512), buf(1024, 1024), buf(512, 1024),
        buf(2, 1024, 512), buf(2, 512, 1024), buf(1024, 1024), buf(2, 512, 512), buf(4, 512, 512),
        buf(4, 512, 1024), acc(512, 512), acc(2, 512, 512), acc(256, 1024), *quarter,
        acc(256, 1024), buf(1024, 1024), acc(1024, 1024), acc(1024, 1024),
        *halves, *eighths, *halves, *eighths,
        buf(512, 1024), acc(256, 1024), buf(256, 1024), buf(256, 512), buf(2, 512, 512),
        *halves, *eighths, buf(256, 1024),
        buf(128, 1024), buf(128, 512), buf(128, 1024), buf(1024, 128), acc(512, 128),
        acc(8, 1024), acc(8, 512), acc(8, 1024), acc(16, 1024), acc(16, 1024), acc(4, 8, 1024),
        acc(2 * planes, 8, 1024), acc(16, 1024),
        sems(3, GROUPS), sems(3, GROUPS), sems(2, PAIRS), sems(2, PAIRS), sems(8), sems(64 + planes),
        sems(64 + planes),
    ]
    rows = jax.ShapeDtypeStruct((256, 1024), BF)
    passed = pl.pallas_call(
        functools.partial(fused_kernel, planes),
        name="block_step",
        out_shape=(rows, rows, jax.ShapeDtypeStruct((16, 1024), F32)),
        in_specs=[hbm, vmem, hbm, hbm, hbm, hbm, vmem, hbm],
        out_specs=(hbm,) * 3,
        scratch_shapes=scratch,
        compiler_params=pltpu.CompilerParams(
            collective_id=1, has_side_effects=True, vmem_limit_bytes=63 << 20
        ),
    )(tokens, norm_params, wqkv, w_out, w_fc, w_proj, factors, grad_out)
    small = jax.ShapeDtypeStruct((4, 4, 1024), F32)
    outs = pl.pallas_call(
        finish_kernel,
        name="finish_step",
        out_shape=(
            rows, jax.ShapeDtypeStruct((256, 1024), F32), small,
            jax.ShapeDtypeStruct((1, 1), F32), small, small, small,
        ),
        in_specs=[vmem] * 3 + [hbm] * 3,
        out_specs=(hbm, hbm) + (vmem,) * 5,
        scratch_shapes=[*quarter, acc(16, 1024), acc(256, 1024), sems(3), sems(2)],
        compiler_params=pltpu.CompilerParams(vmem_limit_bytes=62 << 20),
    )(factors, first, second, *passed)
    return outs[:3] + (outs[3].reshape(()),) + outs[4:]


def solution(mesh):
    placed = (
        P("dp", None),
        P(),
        P(None, None, "tensor"),
        P("tensor", None),
        P(None, "tensor"),
        P("tensor", None),
        P(),
        P(),
        P(),
        P("dp", None),
    )
    planes = mesh.shape["dp"] // 2

    def step(*args):
        rows, width = args[0].shape
        shapes = (rows, width, args[4].shape[1], args[2].shape[2], args[6].shape[1])
        fits = mesh.shape["tensor"] == 4 and mesh.shape["dp"] % 4 == 0
        if fits and shapes == (SEQ, 1024, 1024, 256, 4):
            return fused(planes, *args)
        return body(*args)

    return jax.shard_map(
        step,
        mesh=mesh,
        in_specs=placed,
        out_specs=(P(("dp", "tensor"), None), P(("dp", "tensor"), None), P(), P(), P(), P(), P()),
        check_vma=False,
    )
```

```python
import functools

import jax
import jax.numpy as jnp
from jax import lax
from jax.experimental import pallas as pl
from jax.experimental.pallas import tpu as pltpu
from jax.sharding import PartitionSpec as P

HD = 64
SEQ = 1024
STEP = 5


EPSILON = 1e-05
ADAPTER_SCALING = 8.0
CLIP_NORM = 16.0
LEARN_RATE = 0.03
BETA_ONE = 0.5
BETA_TWO = 0.5
WEIGHT_DECAY = 0.01
ADAM_EPSILON = 1e-08
NEG_LARGE = -1e30
GELU_SCALE = 0.7978845608028654
GELU_CUBE = 0.044715


def matrix_product(left, right):
    return jnp.dot(left, right, preferred_element_type=jnp.float32)


def product_with_transpose(left, right):
    return lax.dot_general(
        left, right, (((1,), (1,)), ((), ())), preferred_element_type=jnp.float32
    )


def transpose_then_product(left, right):
    return lax.dot_general(
        left, right, (((0,), (0,)), ((), ())), preferred_element_type=jnp.float32
    )


def normalize(value_rows_local, gain_vec, bias_vec):
    centered = value_rows_local - jnp.mean(value_rows_local, -1, keepdims=True)
    inverse = lax.rsqrt(jnp.mean(centered * centered, -1, keepdims=True) + EPSILON)
    unit_rows = centered * inverse
    return (unit_rows * gain_vec + bias_vec, unit_rows, inverse)


def normalize_back(incoming, unit_rows, inverse, gain_vec):
    scaled = incoming * gain_vec
    return inverse * (
        scaled
        - jnp.mean(scaled, -1, keepdims=True)
        - unit_rows * jnp.mean(scaled * unit_rows, -1, keepdims=True)
    )


def causal_scores(query_block, key_all, block_index, block_len):
    scores = (
        jnp.einsum("bqhd,bkhd->bhqk", query_block, key_all, preferred_element_type=jnp.float32)
        * 0.125
    )
    query_pos = block_index * block_len + jnp.arange(block_len)
    allowed = jnp.arange(SEQ)[None, :] <= query_pos[:, None]
    return jnp.where(allowed, scores, NEG_LARGE)


def attention_forward(query_rows_local, key_all, value_all):
    block_len = min(512, SEQ)
    outputs = []
    logsums = []
    for block_index in range(SEQ // block_len):
        query_block = query_rows_local[:, block_index * block_len : (block_index + 1) * block_len]
        scores = causal_scores(query_block, key_all, block_index, block_len)
        row_max = jnp.max(scores, -1, keepdims=True)
        exponent = jnp.exp(scores - row_max)
        row_total = jnp.sum(exponent, -1, keepdims=True)
        probability = (exponent / row_total).astype(jnp.bfloat16)
        mixture = jnp.einsum(
            "bhqk,bkhd->bqhd", probability, value_all, preferred_element_type=jnp.float32
        )
        outputs.append(mixture.astype(jnp.bfloat16))
        logsums.append(row_max[..., 0] + jnp.log(row_total[..., 0]))
    return (jnp.concatenate(outputs, 1), jnp.concatenate(logsums, 2))


def attention_backward(query_rows_local, key_all, value_all, grad_mixture, logsums):
    block_len = min(512, SEQ)
    grad_queries = []
    grad_keys = jnp.zeros(key_all.shape, jnp.float32)
    value_gradient_rows = jnp.zeros(value_all.shape, jnp.float32)
    for block_index in range(SEQ // block_len):
        lower = block_index * block_len
        query_block = query_rows_local[:, lower : lower + block_len]
        grad_block = grad_mixture[:, lower : lower + block_len]
        scores = causal_scores(query_block, key_all, block_index, block_len)
        probability = jnp.exp(scores - logsums[:, :, lower : lower + block_len, None])
        grad_prob = jnp.einsum(
            "bqhd,bkhd->bhqk", grad_block, value_all, preferred_element_type=jnp.float32
        )
        row_delta = jnp.sum(grad_prob * probability, -1, keepdims=True)
        dscore = (0.125 * (probability * (grad_prob - row_delta))).astype(jnp.bfloat16)
        grad_queries.append(
            jnp.einsum(
                "bhqk,bkhd->bqhd", dscore, key_all, preferred_element_type=jnp.float32
            ).astype(jnp.bfloat16)
        )
        grad_keys = grad_keys + jnp.einsum(
            "bhqk,bqhd->bkhd", dscore, query_block, preferred_element_type=jnp.float32
        )
        value_gradient_rows = value_gradient_rows + jnp.einsum(
            "bhqk,bqhd->bkhd",
            probability.astype(jnp.bfloat16),
            grad_block,
            preferred_element_type=jnp.float32,
        )
    return (
        jnp.concatenate(grad_queries, 1),
        grad_keys.astype(jnp.bfloat16),
        value_gradient_rows.astype(jnp.bfloat16),
    )


def adam_step(factor_grad, weights, first_old, second_old, grad_norm):
    clipped = factor_grad * (CLIP_NORM / jnp.maximum(grad_norm, CLIP_NORM))
    first_new = BETA_ONE * first_old + (1.0 - BETA_ONE) * clipped
    second_new = BETA_TWO * second_old + (1.0 - BETA_TWO) * clipped * clipped
    first_hat = first_new / (1.0 - BETA_ONE**STEP)
    second_hat = second_new / (1.0 - BETA_TWO**STEP)
    weights_new = weights - LEARN_RATE * (
        first_hat / (jnp.sqrt(second_hat) + ADAM_EPSILON) + WEIGHT_DECAY * weights
    )
    return (clipped, weights_new, first_new, second_new)


def body(
    tokens_in,
    norm_params,
    query_key_value_weight,
    out_weight,
    fc_weight,
    proj_weight,
    factors,
    first_moment,
    second_moment,
    grad_out,
):
    tensor_size = lax.axis_size("tensor")
    tensor_rank = lax.axis_index("tensor")
    token_count = tokens_in.shape[0]
    doc_count = token_count // SEQ
    local_width = query_key_value_weight.shape[2]
    heads_here = local_width // HD
    row_count = token_count // tensor_size
    row_start = tensor_rank * row_count
    rank_count = factors.shape[1]
    full_width = factors.shape[2]
    inputs = tokens_in.astype(jnp.float32)
    first_normalized, unit_one, inverse_one = normalize(inputs, norm_params[0], norm_params[1])
    first_normalized_reduced = first_normalized.astype(jnp.bfloat16)
    factor_reduced_precision = factors.astype(jnp.bfloat16)
    column_offset = tensor_rank * local_width
    query_adapter_output = lax.dynamic_slice_in_dim(
        factor_reduced_precision[1], column_offset, local_width, 1
    )
    value_adapter_output = lax.dynamic_slice_in_dim(
        factor_reduced_precision[3], column_offset, local_width, 1
    )
    query_down_factor = product_with_transpose(
        first_normalized_reduced, factor_reduced_precision[0]
    ).astype(jnp.bfloat16)
    value_down_factor = product_with_transpose(
        first_normalized_reduced, factor_reduced_precision[2]
    ).astype(jnp.bfloat16)
    query_rows_local = (
        matrix_product(first_normalized_reduced, query_key_value_weight[0])
        + ADAPTER_SCALING * matrix_product(query_down_factor, query_adapter_output)
    ).astype(jnp.bfloat16)
    keys_low = matrix_product(first_normalized_reduced, query_key_value_weight[1]).astype(
        jnp.bfloat16
    )
    values_low = (
        matrix_product(first_normalized_reduced, query_key_value_weight[2])
        + ADAPTER_SCALING * matrix_product(value_down_factor, value_adapter_output)
    ).astype(jnp.bfloat16)
    head_shape = (doc_count, SEQ, heads_here, HD)
    query_heads = query_rows_local.reshape(head_shape)
    keys_heads = keys_low.reshape(head_shape)
    values_heads = values_low.reshape(head_shape)
    mixture, logsums = attention_forward(query_heads, keys_heads, values_heads)
    attn_part = matrix_product(mixture.reshape(token_count, local_width), out_weight)
    grad_full = grad_out.astype(jnp.float32)
    attn_rows = lax.psum_scatter(
        attn_part.astype(jnp.bfloat16), "tensor", scatter_dimension=0, tiled=True
    ).astype(jnp.float32)
    resid_rows = lax.dynamic_slice_in_dim(inputs, row_start, row_count, 0) + attn_rows
    normed_two_rows, unit_two, inverse_two = normalize(resid_rows, norm_params[2], norm_params[3])
    normed_two_low = lax.all_gather(
        normed_two_rows.astype(jnp.bfloat16), "tensor", axis=0, tiled=True
    )
    hidden_pre = matrix_product(normed_two_low, fc_weight)
    hidden_act, gelu_pull = jax.vjp(
        lambda argument: jax.nn.gelu(argument, approximate=True), hidden_pre
    )
    mlp_part = matrix_product(hidden_act.astype(jnp.bfloat16), proj_weight)
    grad_hidden = product_with_transpose(grad_out, proj_weight)
    grad_pre = gelu_pull(grad_hidden)[0].astype(jnp.bfloat16)
    second_part = product_with_transpose(grad_pre, fc_weight)
    out_rows = resid_rows + lax.psum_scatter(
        mlp_part.astype(jnp.bfloat16), "tensor", scatter_dimension=0, tiled=True
    ).astype(jnp.float32)
    second_rows = lax.psum_scatter(
        second_part.astype(jnp.bfloat16), "tensor", scatter_dimension=0, tiled=True
    ).astype(jnp.float32)
    resid_grad_rows = lax.dynamic_slice_in_dim(grad_full, row_start, row_count, 0) + normalize_back(
        second_rows, unit_two, inverse_two, norm_params[2]
    )
    resid_grad_low = lax.all_gather(
        resid_grad_rows.astype(jnp.bfloat16), "tensor", axis=0, tiled=True
    )
    grad_mixture = product_with_transpose(resid_grad_low, out_weight).astype(jnp.bfloat16)
    query_gradient, grad_keys, value_gradient_rows = attention_backward(
        query_heads, keys_heads, values_heads, grad_mixture.reshape(head_shape), logsums
    )
    query_gradient = query_gradient.reshape(token_count, local_width)
    grad_keys = grad_keys.reshape(token_count, local_width)
    value_gradient_rows = value_gradient_rows.reshape(token_count, local_width)
    stacked = jnp.stack((query_gradient, grad_keys, value_gradient_rows))
    first_part = jnp.einsum(
        "stc,sdc->td", stacked, query_key_value_weight, preferred_element_type=jnp.float32
    )
    query_up_factor = ADAPTER_SCALING * product_with_transpose(query_gradient, query_adapter_output)
    value_up_factor = ADAPTER_SCALING * product_with_transpose(
        value_gradient_rows, value_adapter_output
    )
    first_part = first_part + jnp.dot(
        query_up_factor,
        factor_reduced_precision[0].astype(jnp.float32),
        precision=lax.Precision.HIGHEST,
    )
    first_part = first_part + jnp.dot(
        value_up_factor,
        factor_reduced_precision[2].astype(jnp.float32),
        precision=lax.Precision.HIGHEST,
    )
    first_rows = lax.psum_scatter(
        first_part.astype(jnp.bfloat16), "tensor", scatter_dimension=0, tiled=True
    ).astype(jnp.float32)
    unit_rows = lax.dynamic_slice_in_dim(unit_one, row_start, row_count, 0)
    inverse_rows = lax.dynamic_slice_in_dim(inverse_one, row_start, row_count, 0)
    input_rows = resid_grad_rows + normalize_back(
        first_rows, unit_rows, inverse_rows, norm_params[0]
    )
    query_cross_term = transpose_then_product(query_gradient, first_normalized_reduced)
    value_cross_term = transpose_then_product(value_gradient_rows, first_normalized_reduced)
    query_down_gradient = ADAPTER_SCALING * jnp.dot(
        query_adapter_output.astype(jnp.float32), query_cross_term, precision=lax.Precision.HIGHEST
    )
    value_down_gradient = ADAPTER_SCALING * jnp.dot(
        value_adapter_output.astype(jnp.float32), value_cross_term, precision=lax.Precision.HIGHEST
    )
    empty_slot = jnp.zeros((rank_count, full_width), jnp.float32)
    up_grad_query = lax.dynamic_update_slice_in_dim(
        empty_slot,
        ADAPTER_SCALING * transpose_then_product(query_down_factor, query_gradient),
        column_offset,
        1,
    )
    up_grad_value = lax.dynamic_update_slice_in_dim(
        empty_slot,
        ADAPTER_SCALING * transpose_then_product(value_down_factor, value_gradient_rows),
        column_offset,
        1,
    )
    partial_grad = jnp.stack(
        (query_down_gradient, up_grad_query, value_down_gradient, up_grad_value)
    )
    reduced = lax.psum(partial_grad, ("dp", "tensor"))
    grad_norm = jnp.sqrt(jnp.sum(reduced * reduced))
    clipped, weights_new, first_new, second_new = adam_step(
        reduced, factors, first_moment, second_moment, grad_norm
    )
    return (
        out_rows.astype(jnp.bfloat16),
        input_rows,
        clipped,
        grad_norm,
        weights_new,
        first_new,
        second_new,
    )


MESH = pl.DeviceIdType.MESH
BF = jnp.bfloat16
F32 = jnp.float32
GROUPS = 8
PAIRS = 8


def mm(left, right):
    return jnp.dot(left, right, preferred_element_type=F32)


def mm_nt(left, right):
    return lax.dot_general(left, right, (((1,), (1,)), ((), ())), preferred_element_type=F32)


def mm_tn(left, right):
    return lax.dot_general(left, right, (((0,), (0,)), ((), ())), preferred_element_type=F32)


def flip(value, bit):
    return value + bit - 2 * bit * ((value // bit) % 2)


def unit_of(rows):
    centered = rows - jnp.mean(rows, -1, keepdims=True)
    inverse = lax.rsqrt(jnp.mean(centered * centered, -1, keepdims=True) + EPSILON)
    return centered * inverse, inverse


def unit_back(scaled, unit, inverse):
    return inverse * (
        scaled - jnp.mean(scaled, -1, keepdims=True) - unit * jnp.mean(scaled * unit, -1, keepdims=True)
    )


def fused_kernel(
    planes,
    tokens, norm_params, wqkv, w_out, w_fc, w_proj, factors, grad_out,
    bo_r, ig_r, summed,
    tok, n1, go, wq, wkv, wo, fcw, pw, kv, qs, p0, p1, mix, inv, attn_own, attn_s, attn_r,
    res, n2, acc_a, acc_b, gnt_s, gnt_r, gnt_xs, gnt_xr, mlp_s, mlp_r, mlp_xs, mlp_xr,
    gr_b, bo_f, bo_s, gq, dos, gno_s, gno_r, gno_xs, gno_xr, ig_s,
    f02, f1p, f3kv, down, gd_scr, fg_a, fg_q, fg_v, ps, ps_r, plane_buf, z_buf, fin,
    chain_send, chain_recv, pair_send, pair_recv, load_sem, ssem, rsem,
):
    d = lax.axis_index("dp")
    t = lax.axis_index("tensor")
    z, c, x, y = d // 2, d % 2, t % 2, t // 2
    odd = z % 2
    nbr = (flip(d, 1), t)
    prim = (d, flip(t, 1 + odd))
    sec = (d, flip(t, 2 - odd))
    plane = [(d, flip(t, 1)), (d, flip(t, 2)), (d, 3 - t)]
    x_nbr, y_nbr = plane[0], plane[1]
    zs = [(flip(d, 2 << k), t) for k in range(planes.bit_length() - 1)]
    owners = [(2 * z + y, 2 * h + x) for h in range(2)]
    at_home = [jnp.logical_and(c == y, h == y) for h in range(2)]
    quarter = [t, flip(t, 1 + odd), flip(t, 2 - odd), 3 - t]
    column = [pl.multiple_of(q * 256 + c * 128, 128) for q in quarter]

    def at(start, size):
        return pl.ds(pl.multiple_of(start, size), size)

    def rows_of(half, side):
        return at(512 * half + 256 * side, 256)

    def own_rows(h, side):
        return at(512 * h + 256 * side + 128 * c, 128)

    def other_rows(h, side):
        return at(512 * h + 256 * side + 128 * (1 - c), 128)

    def ff_own(h, side):
        return at(512 * side + 256 * h + 128 * c, 128)

    def ff_other(h, side):
        return at(512 * side + 256 * h + 128 * (1 - c), 128)

    def remote_to(src, dst, out_index, in_index, device):
        return pltpu.make_async_remote_copy(
            src_ref=src, dst_ref=dst, send_sem=ssem.at[out_index], recv_sem=rsem.at[in_index],
            device_id=device, device_id_type=MESH,
        )

    def remote(src, dst, index, device):
        return remote_to(src, dst, index, index, device)

    pending = []

    def drain():
        for wait in pending:
            wait()

    def send(copy):
        copy.start()
        pending.append(copy.wait_send)
        return copy

    lane = at(c * 128, 128)
    loads = [
        pltpu.make_async_copy(wqkv.at[1, :, lane], wkv.at[:, pl.ds(0, 128)], load_sem.at[0]),
        pltpu.make_async_copy(wqkv.at[2, :, lane], wkv.at[:, pl.ds(128, 128)], load_sem.at[1]),
        pltpu.make_async_copy(wqkv.at[0, :, lane], wq.at[:, pl.ds(0, 128)], load_sem.at[2]),
        pltpu.make_async_copy(w_out.at[lane, :], wo.at[pl.ds(0, 128), :], load_sem.at[3]),
        pltpu.make_async_copy(w_fc.at[:, at(c * 512, 512)], fcw.at[0], load_sem.at[4]),
        pltpu.make_async_copy(w_proj.at[at(c * 512, 512), :], pw.at[0], load_sem.at[5]),
    ]
    for load in loads:
        load.start()

    barrier = pltpu.get_barrier_semaphore()
    partners = [nbr, x_nbr, y_nbr] + zs
    for device in partners:
        pl.semaphore_signal(barrier, inc=1, device_id=device, device_id_type=MESH)
    fpad = acc_b.at[0:128, :]
    fpad[...] = jnp.zeros(fpad.shape, F32)
    fpad[0:4, :] = factors[0]
    fpad[4:8, :] = factors[2]
    f02[...] = fpad[...].astype(BF)
    fpad[...] = jnp.zeros(fpad.shape, F32)
    for s in range(4):
        fpad[0:4, 128 * s : 128 * s + 128] = factors[1, :, pl.ds(column[s], 128)]
    f1p[...] = fpad[:, :512].astype(BF)
    fpad[...] = jnp.zeros(fpad.shape, F32)
    for s in range(4):
        fpad[4:8, 256 * s + 128 : 256 * s + 256] = factors[3, :, pl.ds(column[s], 128)]
    f3kv[...] = fpad[...].astype(BF)
    ps[...] = jnp.zeros_like(ps)
    acc_a[...] = jnp.zeros_like(acc_a)
    acc_b[...] = jnp.zeros_like(acc_b)
    pl.semaphore_wait(barrier, len(partners))

    doc = []
    for r in range(4):
        part = pl.ds(256 * r, 256)
        doc.append((tokens.at[part, :], tok.at[part, :], r))
    place = jnp.where(c == y, 0, 512)
    grads = [
        (grad_out.at[rows_of(h, x), :], go.at[at(place + 256 * h, 256), :], 4 + h) for h in range(2)
    ]
    other_place = 512 - place
    grads_in = [
        (grad_out.at[rows_of(h, x), :], go.at[at(other_place + 256 * h, 256), :], 4 + h) for h in range(2)
    ]
    for h in range(2):
        pltpu.make_async_copy(*grads[h][:2], load_sem.at[6 + h]).start()

    @pl.when(c == y)
    def _():
        for src, dst, index in doc:
            remote(src, dst, index, nbr).start()
            pltpu.make_async_copy(src, dst, rsem.at[index]).start()

    def doc_sent():
        @pl.when(c == y)
        def _():
            for item in doc:
                remote(*item, nbr).wait_send()

    pending.append(doc_sent)
    for item in grads:
        send(remote(*item, nbr))

    def doc_wait(index):
        remote(*doc[index], nbr).wait_recv()

    def piece(slot, group):
        matrix, a = group // 2, group % 2
        if matrix < 2:
            return wkv.at[pl.ds(512 * a, 512), pl.ds(256 * slot + 128 * matrix, 128)]
        if matrix == 2:
            return wq.at[pl.ds(512 * a, 512), pl.ds(128 * slot, 128)]
        return wo.at[pl.ds(128 * slot + 64 * a, 64), :]

    def hop(slot, group):
        return pltpu.make_async_remote_copy(
            src_ref=piece(1 if slot > 1 else 0, group), dst_ref=piece(slot, group),
            send_sem=chain_send.at[slot - 1, group], recv_sem=chain_recv.at[slot - 1, group],
            device_id=(prim, zs[0], sec)[slot - 1], device_id_type=MESH,
        )

    def pump(group, later=True):
        hop(1, group).wait_recv()
        for slot in (2, 3):
            hop(slot, group).start()
            if later:
                pending.append(hop(slot, group).wait_send)

    def passed(groups):
        for group in groups:
            hop(2, group).wait_recv()
            hop(3, group).wait_recv()

    def pair_piece(slot, pair, parity):
        h, q = pair // 4, pair % 4
        if q < 2:
            return fcw.at[slot, at(512 * q + 256 * parity, 256), pl.ds(256 * h, 256)]
        return pw.at[slot, at(256 * h + 128 * (q - 2) + 64 * parity, 64), :]

    def pair_hop(step, pair, parity):
        return pltpu.make_async_remote_copy(
            src_ref=pair_piece(step, pair, parity), dst_ref=pair_piece(1, pair, parity),
            send_sem=pair_send.at[step, pair], recv_sem=pair_recv.at[step, pair],
            device_id=(x_nbr, zs[0])[step], device_id_type=MESH,
        )

    def pair_pump(pair):
        pair_hop(0, pair, odd).wait_recv()
        pair_hop(1, pair, odd).start()

    def pair_wait(pairs):
        for pair in pairs:
            pair_hop(1, pair, 1 - odd).wait_recv()

    for matrix in range(4):
        loads[matrix].wait()
        send(hop(1, 2 * matrix))
        send(hop(1, 2 * matrix + 1))
    loads[4].wait()
    loads[5].wait()
    for pair in range(2):
        pair_hop(0, pair, odd).start()

    gain_one, bias_one = norm_params[0:1, :], norm_params[1:2, :]
    gain_two, bias_two = norm_params[2:3, :], norm_params[3:4, :]
    def first_norm(r):
        doc_wait(r)

        @pl.loop(0, 2)
        def _(q):
            rows = at(256 * r + 128 * q, 128)
            unit, _ = unit_of(tok[rows, :].astype(F32))
            n1[rows, :] = (unit * gain_one + bias_one).astype(BF)

    first_norm(0)
    first_norm(1)
    pump(0)
    first_norm(2)
    first_norm(3)

    @pl.loop(0, 2)
    def _(r):
        rows = at(512 * r, 512)
        down[rows, :] = mm_nt(n1[rows, :], f02[...]).astype(BF)

    pump(1)
    first_head = lax.broadcasted_iota(jnp.int32, (256, 512), 1) % 128 < 64
    first_lanes = first_head[:, 0:128]

    def stacked(rows, lanes):
        return jnp.concatenate((jnp.where(lanes, rows, 0.0), jnp.where(lanes, 0.0, rows)), 0)

    p_refs = (p0, p1)
    column_pos = lax.broadcasted_iota(jnp.int32, (512, 512), 1)
    row_pos = lax.broadcasted_iota(jnp.int32, (512, 512), 0) % 256 + 256 * x
    allowed = column_pos <= row_pos

    @pl.loop(0, 4)
    def _(s):
        @pl.when(s == 1)
        def _():
            for group in range(2, 6):
                pump(group, False)

        @pl.when(s == 2)
        def _():
            pump(6, False)
            passed(range(0, 6))

        @pl.when(s == 3)
        def _():
            pump(7, False)
            for pair in range(2, PAIRS):
                pair_hop(0, pair, odd).start()

        both_lanes, lanes = at(256 * s, 256), at(128 * s, 128)
        keys, values = at(256 * s, 128), at(256 * s + 128, 128)

        @pl.loop(0, 2)
        def _(r):
            rows = at(512 * r, 512)
            kv[rows, both_lanes] = (
                mm(n1[rows, :], wkv[:, both_lanes]) + ADAPTER_SCALING * mm(down[rows, :], f3kv[:, both_lanes])
            ).astype(BF)

        for h in range(2):
            rows = rows_of(h, x)
            query = mm(n1[rows, :], wq[:, lanes]) + ADAPTER_SCALING * mm(down[rows, :], f1p[:, lanes])
            qs[h, :, lanes] = stacked(query.astype(BF).astype(F32) * 0.125, first_lanes).astype(BF)
        scores = [mm_nt(qs[h, :, lanes], kv[0 : 512 * (h + 1), keys]) for h in range(2)]
        kept = []
        for h in range(2):
            last = jnp.where(allowed, scores[h][:, 512 * h :], NEG_LARGE)
            block = jnp.concatenate((scores[h][:, :512], last), 1) if h else last
            exponent = jnp.exp(block - jnp.max(block, -1, keepdims=True))
            inverse = 1.0 / jnp.sum(exponent, -1, keepdims=True)
            p_refs[h][s] = exponent.astype(BF)
            inv[h, :, lanes] = jnp.broadcast_to(inverse, (512, 128))
            kept.append((exponent.astype(BF), inverse))
        for h in range(2):
            both = mm(kept[h][0], kv[0 : 512 * (h + 1), values]) * kept[h][1]
            mix[256 * h : 256 * h + 256, lanes] = jnp.where(first_lanes, both[0:256], both[256:512])

    for group in range(2, GROUPS):
        pending.append(hop(2, group).wait_send)
        pending.append(hop(3, group).wait_send)
    for pair in range(PAIRS):
        pending.append(pair_hop(0, pair, odd).wait_send)
    pair_pump(0)
    passed(range(6, 8))

    def heads_out(sub):
        rows = [mix[at(256 * h + 128 * sub, 128), :].astype(BF) for h in range(2)]
        return mm(jnp.concatenate(rows, 0), wo[...])

    attn_s[...] = heads_out(1 - c).astype(BF)
    to_nbr = send(remote(attn_s, attn_r, 8, nbr))
    pair_pump(1)
    attn_own[...] = heads_out(c)
    pair_pump(2)
    to_nbr.wait_recv()

    gathered = []
    for h in range(2):
        part = slice(128 * h, 128 * h + 128)
        rows = own_rows(h, x)
        residual = tok[rows, :].astype(F32) + attn_own[part, :] + attn_r[part, :].astype(F32)
        res[part, :] = residual
        unit, _ = unit_of(residual)
        rows = ff_own(h, 0)
        n2[rows, :] = (unit * gain_two + bias_two).astype(BF)
        gathered.append(send(remote(n2.at[rows, :], n2.at[ff_own(h, 1), :], 11 + h, y_nbr)))
        gathered.append(send(remote(n2.at[rows, :], n2.at[rows, :], 9 + h, nbr)))
    pair_pump(3)
    for h in range(2):
        pltpu.make_async_copy(*grads[h][:2], load_sem.at[6 + h]).wait()
        remote(*grads_in[h], nbr).wait_recv()
    gathered[1].wait_recv()
    gathered[3].wait_recv()

    def pass_on(h):
        gathered[2 * h].wait_recv()
        rows = ff_own(h, 1)
        remote(n2.at[rows, :], n2.at[rows, :], 13 + h, nbr).start()

    def passed_on(h):
        rows = ff_own(h, 1)
        return remote(n2.at[rows, :], n2.at[rows, :], 13 + h, nbr)

    def sum_copy(source, target, first, h, j):
        part = pl.ds(128 * j, 128)
        return remote(source.at[h, part, :], target.at[h, part, :], first + 2 * h + j, nbr)

    def to_core(acc, source, target, first, h):
        for j, side in enumerate((1, 0)):
            source[h, 128 * j : 128 * j + 128, :] = acc[ff_other(h, side), :].astype(BF)
            sum_copy(source, target, first, h, j).start()

    def to_side(acc, source, target, out, out_target, first, side_first, h):
        sum_copy(source, target, first, h, 0).wait_recv()
        out[h] = (acc[ff_own(h, 1), :] + target[h, 0:128, :].astype(F32)).astype(BF)
        return send(remote(out.at[h], out_target.at[h], side_first + h, y_nbr))

    @pl.loop(0, 8)
    def _(unit):
        @pl.when(unit == 1)
        def _():
            pair_pump(4)

        @pl.when(unit == 2)
        def _():
            pair_wait(range(0, 4))
            pass_on(0)
            pair_pump(5)

        @pl.when(unit == 3)
        def _():
            pair_pump(6)
            pass_on(1)
            pair_pump(7)
            for h in range(2):
                passed_on(h).wait_recv()

        @pl.when(unit == 6)
        def _():
            pair_wait(range(4, 8))

        @pl.when(unit == 7)
        def _():
            to_core(acc_b, gnt_s, gnt_r, 40, 1)

        flag = lambda value: jnp.where(value, 1, 0)
        slot = flag(jnp.logical_or(unit == 2, unit >= 5))
        part = flag(jnp.logical_or(unit >= 6, jnp.logical_or(unit == 1, unit == 4)))
        side = flag(unit >= 3)
        last_half = 7 - unit
        starts = [
            jnp.where(unit < 6, 512 * side + 256 * h, 512 * h + 256 * last_half) for h in range(2)
        ]
        tiles = [at(start, 256) for start in starts]
        lanes = at(256 * part, 256)
        pre = [mm(n2[rows, :], fcw[slot, :, lanes]) for rows in tiles]
        grad_act = [mm_nt(go[rows, :], pw[slot, lanes, :]) for rows in tiles]
        for rows, hidden, grad in zip(tiles, pre, grad_act):
            square = hidden * hidden
            tanh = jnp.tanh(GELU_SCALE * hidden * (1.0 + GELU_CUBE * square))
            half_up = 0.5 * (1.0 + tanh)
            slope = half_up + (0.5 * GELU_SCALE) * hidden * (1.0 - tanh * tanh) * (
                1.0 + 3.0 * GELU_CUBE * square
            )
            acc_b[rows, :] += mm_nt((grad * slope).astype(BF), fcw[slot, :, lanes])
            acc_a[rows, :] += mm((hidden * half_up).astype(BF), pw[slot, lanes, :])

    for pair in range(PAIRS):
        pending.append(pair_hop(1, pair, odd).wait_send)
    for h in range(2):
        pending.append(passed_on(h).wait_send)
        for j in range(2):
            pending.append(sum_copy(gnt_s, gnt_r, 40, h, j).wait_send)
            pending.append(sum_copy(mlp_s, mlp_r, 44, h, j).wait_send)

    gnt_side = [None, None]
    gnt_side[1] = to_side(acc_b, gnt_s, gnt_r, gnt_xs, gnt_xr, 40, 17, 1)
    to_core(acc_b, gnt_s, gnt_r, 40, 0)
    gnt_side[0] = to_side(acc_b, gnt_s, gnt_r, gnt_xs, gnt_xr, 40, 17, 0)
    for h in (1, 0):
        to_core(acc_a, mlp_s, mlp_r, 44, h)
    near, far = y, 1 - y
    for h in (1, 0):
        for j in range(2):
            sum_copy(mlp_s, mlp_r, 44, h, j).wait_recv()

    def chip_sum(h, side):
        return acc_a[ff_own(h, side), :] + mlp_r[h, 128 * (1 - side) : 128 * (1 - side) + 128, :].astype(F32)

    mlp_xs[0] = chip_sum(far, 1).astype(BF)
    mlp_xs[1] = (res[at(128 * far, 128), :] + chip_sum(far, 0)).astype(BF)
    mlp_side = [send(remote(mlp_xs.at[k], mlp_xr.at[k], 21 + k, y_nbr)) for k in range(2)]
    bo_f[0] = res[at(128 * near, 128), :] + chip_sum(near, 0)
    bo_f[1] = chip_sum(near, 1)

    gr = attn_own

    def residual_back(h):
        part = slice(128 * h, 128 * h + 128)
        unit, inverse = unit_of(res[part, :])
        sum_copy(gnt_s, gnt_r, 40, h, 1).wait_recv()
        total = acc_b[ff_own(h, 0), :] + gnt_r[h, 128:256, :].astype(F32)
        gnt_side[h].wait_recv()
        scaled = (total + gnt_xr[h].astype(F32)) * gain_two
        grad = go[ff_own(h, 0), :].astype(F32) + unit_back(scaled, unit, inverse)
        gr[part, :] = grad
        local = at(256 * h + 128 * c, 128)
        gr_b[local, :] = grad.astype(BF)
        return send(remote(gr_b.at[local, :], gr_b.at[local, :], 23 + h, nbr))

    def mixture_back(h):
        grad_mixture = mm_nt(gr_b[256 * h : 256 * h + 256, :], wo[...])
        dos[h] = (stacked(grad_mixture, first_head) * inv[h]).astype(BF)

    to_nbr = residual_back(1)
    to_nbr.wait_recv()
    mixture_back(1)

    def scores_back(h, first, count):
        size = 512 * (h + 1)
        group = [first + k for k in range(count)]
        lanes = [at(128 * s, 128) for s in group]
        k_lanes = [at(256 * s, 128) for s in group]
        v_lanes = [at(256 * s + 128, 128) for s in group]
        grads = [dos[h, :, lane] for lane in lanes]
        grad_prob = [mm_nt(grad, kv[0:size, lane]) for lane, grad in zip(v_lanes, grads)]
        dscores = []
        for s, lane, grad, block in zip(group, lanes, grads, grad_prob):
            mixture = mix[256 * h : 256 * h + 256, lane]
            delta = jnp.sum(
                grad.astype(F32) * jnp.concatenate((mixture, mixture), 0), -1, keepdims=True
            )
            dscores.append((p_refs[h][s].astype(F32) * (block - delta)).astype(BF))
        for k, (s, lane, grad, dscore) in enumerate(zip(group, lanes, grads, dscores)):
            both = 0.125 * mm(dscore, kv[0:size, k_lanes[k]])
            gq[:, lane] = jnp.where(first_lanes, both[0:256], both[256:512]).astype(BF)
            grad_keys = mm_tn(dscore, qs[h, :, lane])
            grad_values = mm_tn(p_refs[h][s], grad)
            if h:
                acc_a[:, k_lanes[k]] = grad_keys
                acc_a[:, v_lanes[k]] = grad_values
            else:
                acc_a[0:512, k_lanes[k]] += grad_keys
                acc_a[0:512, v_lanes[k]] += grad_values

    def factors_back(h):
        rows = slice(512 * h, 512 * h + 512)
        grads = acc_a[rows, :].astype(BF)
        query = gq[...]
        gd_scr[...] = ADAPTER_SCALING * mm_nt(grads, f3kv[...])
        gd_scr[at(256 * x, 256), :] += ADAPTER_SCALING * mm_nt(query, f1p[...])
        terms = (
            mm_tn(gd_scr[...].astype(BF), n1[rows, :])[0:8],
            mm_tn(down[rows_of(h, x), :], query)[0:8],
            mm_tn(down[rows, :], grads)[0:8],
        )
        for total, term in zip((fg_a, fg_q, fg_v), terms):
            total[...] = term if h else total[...] + term

    def rows_copy(h, j):
        part = pl.ds(128 * j, 128)
        return remote(gno_s.at[h, part, :], gno_r.at[h, part, :], 27 + 2 * h + j, nbr)

    def rows_back(h, j):
        side = x if j else 1 - x
        rows = rows_of(h, side)
        grad = mm_nt(acc_a[rows, :].astype(BF), wkv[...])
        grad += mm(gd_scr[at(256 * side, 256), :].astype(BF), f02[...])
        if j:
            grad += mm_nt(gq[...], wq[...])
        acc_b[rows, :] = grad
        gno_s[h, 128 * j : 128 * j + 128, :] = acc_b[other_rows(h, side), :].astype(BF)
        send(rows_copy(h, j))

    side_copies = {}

    def reduce_rows(h):
        rows_copy(h, 0).wait_recv()
        gno_xs[h] = (acc_b[own_rows(h, 1 - x), :] + gno_r[h, 0:128, :].astype(F32)).astype(BF)
        for k in range(2):
            part = pl.ds(64 * k, 64)
            side_copies[h, k] = send(
                remote(gno_xs.at[h, part, :], gno_xr.at[h, part, :], 48 + 2 * h + k, x_nbr)
            )

    def to_owner(src, dst, h, out_index, in_index):
        @pl.when(at_home[h])
        def _():
            pltpu.make_async_copy(src, dst, rsem.at[in_index + c]).start()

        @pl.when(jnp.logical_not(at_home[h]))
        def _():
            remote_to(src, dst, out_index, in_index + c, owners[h]).start()

        def sent():
            @pl.when(jnp.logical_not(at_home[h]))
            def _():
                remote_to(src, dst, out_index, in_index + c, owners[h]).wait_send()

        pending.append(sent)

    def input_rows(h, k):
        if k == 0:
            rows_copy(h, 1).wait_recv()
        start = 512 * h + 256 * x + 128 * c + 64 * k
        rows, part = at(start, 64), slice(64 * k, 64 * k + 64)
        unit, inverse = unit_of(tok[rows, :].astype(F32))
        total = acc_b[rows, :] + gno_r[h, 128 + 64 * k : 192 + 64 * k, :].astype(F32)
        side_copies[h, k].wait_recv()
        scaled = (total + gno_xr[h, part, :].astype(F32)) * gain_one
        out = slice(128 * h + 64 * k, 128 * h + 64 * k + 64)
        ig_s[out, :] = (gr[out, :] + unit_back(scaled, unit, inverse)).astype(BF)
        to_owner(ig_s.at[out, :], ig_r.at[at(128 * c + 64 * k, 64), :], h, 52 + 2 * h + k, 56 + 2 * k)

    scores_back(1, 0, 2)
    scores_back(1, 2, 2)

    to_nbr = residual_back(0)
    factors_back(1)
    rows_back(1, 0)
    rows_back(1, 1)
    to_nbr.wait_recv()
    mixture_back(0)
    reduce_rows(1)
    scores_back(0, 0, 4)

    factors_back(0)

    ps[0:8, :] = fg_a[...]
    down_rows = lax.broadcasted_iota(jnp.int32, (8, 128), 0) < 4
    for s in range(4):
        ps[8:16, pl.ds(column[s], 128)] = ADAPTER_SCALING * jnp.where(
            down_rows, fg_q[:, 128 * s : 128 * s + 128], fg_v[:, 256 * s + 128 : 256 * s + 256]
        )
    core_sum = send(remote(ps, ps_r, 33, nbr))
    rows_back(0, 0)
    core_sum.wait_recv()
    eight = at(8 * c, 8)
    plane_buf[t] = ps[eight, :] + ps_r[eight, :]
    copies = [
        send(remote(plane_buf.at[t], plane_buf.at[t], 35 + k, device)) for k, device in enumerate(plane)
    ]
    reduce_rows(0)
    for k in range(2):
        mlp_side[k].wait_recv()
        bo_s[k] = (bo_f[k] + mlp_xr[k].astype(F32)).astype(BF)
    kept = jnp.where(c == y, 0, 1)
    home = pl.ds(pl.multiple_of(128 * c, 128), 128)
    bo_home = pltpu.make_async_copy(bo_s.at[kept], bo_r.at[home, :], load_sem.at[1])
    bo_home.start()
    bo_away = send(remote(bo_s.at[1 - kept], bo_r.at[home, :], 60, nbr))
    rows_back(0, 1)
    for k in range(2):
        input_rows(1, k)
    for copy in copies:
        copy.wait_recv()
    z_buf[0] = plane_buf[0] + plane_buf[1] + plane_buf[2] + plane_buf[3]

    def z_copy(k):
        return remote(z_buf.at[2 * k], z_buf.at[2 * k + 1], 64 + k, zs[k])

    for k in range(len(zs)):
        send(z_copy(k))
        if k < 2:
            input_rows(0, k)
        z_copy(k).wait_recv()
        z_buf[2 * k + 2] = z_buf[2 * k] + z_buf[2 * k + 1]
    for k in range(len(zs), 2):
        input_rows(0, k)
    fin[eight, :] = z_buf[2 * len(zs)]
    send(remote(fin.at[eight, :], fin.at[eight, :], 34, nbr))
    theirs = at(8 - 8 * c, 8)
    remote(fin.at[theirs, :], fin.at[theirs, :], 34, nbr).wait_recv()
    result = pltpu.make_async_copy(fin, summed, load_sem.at[0])
    result.start()

    bo_home.wait()
    bo_away.wait_recv()
    for core in range(2):
        for k in range(2):
            part = pl.ds(128 * core + 64 * k, 64)
            remote_to(ig_s.at[pl.ds(0, 64), :], ig_r.at[part, :], 52, 56 + 2 * k + core, nbr).wait_recv()
    result.wait()
    drain()


def finish_kernel(
    factors, first_moment, second_moment, bo_in, ig_in, sum_in,
    block_out, input_grad, clipped, grad_norm, factors_new, first_new, second_new,
    bo, ig, summed, grads, sem, out_sem,
):
    pairs = [(sum_in, summed), (bo_in, bo), (ig_in, ig)]
    loads = [pltpu.make_async_copy(*pair, sem.at[k]) for k, pair in enumerate(pairs)]
    for load in loads:
        load.start()
    loads[0].wait()
    grad = summed[...]
    norm = jnp.sqrt(jnp.sum(grad * grad, (0, 1), keepdims=True))
    grad_norm[...] = norm
    grad = grad * (CLIP_NORM / jnp.maximum(norm, CLIP_NORM))
    for index, first in enumerate((0, 8, 4, 12)):
        value, weights = grad[first : first + 4], factors[index]
        first_value = BETA_ONE * first_moment[index] + (1.0 - BETA_ONE) * value
        second_value = BETA_TWO * second_moment[index] + (1.0 - BETA_TWO) * value * value
        first_hat = first_value / (1.0 - BETA_ONE**STEP)
        second_hat = second_value / (1.0 - BETA_TWO**STEP)
        clipped[index] = value
        first_new[index] = first_value
        second_new[index] = second_value
        factors_new[index] = weights - LEARN_RATE * (
            first_hat / (jnp.sqrt(second_hat) + ADAM_EPSILON) + WEIGHT_DECAY * weights
        )
    loads[1].wait()
    stores = [pltpu.make_async_copy(bo, block_out, out_sem.at[0])]
    stores[0].start()
    loads[2].wait()
    grads[...] = ig[...].astype(F32)
    stores.append(pltpu.make_async_copy(grads, input_grad, out_sem.at[1]))
    stores[1].start()
    for store in stores:
        store.wait()


def fused(planes, tokens, norm_params, wqkv, w_out, w_fc, w_proj, factors, first, second, grad_out):
    vmem = pl.BlockSpec(memory_space=pltpu.VMEM)
    hbm = pl.BlockSpec(memory_space=pl.ANY)

    def buf(*shape):
        return pltpu.VMEM(shape, BF)

    def acc(*shape):
        return pltpu.VMEM(shape, F32)

    def sems(*shape):
        return pltpu.SemaphoreType.DMA(shape)

    quarter = [buf(256, 1024)] * 2
    halves, eighths = [buf(2, 256, 1024)] * 2, [buf(2, 128, 1024)] * 2
    scratch = [
        buf(1024, 1024), buf(1024, 1024), buf(1024, 1024), buf(1024, 512), buf(1024, 1024), buf(512, 1024),
        buf(2, 1024, 512), buf(2, 512, 1024), buf(1024, 1024), buf(2, 512, 512), buf(4, 512, 512),
        buf(4, 512, 1024), acc(512, 512), acc(2, 512, 512), acc(256, 1024), *quarter,
        acc(256, 1024), buf(1024, 1024), acc(1024, 1024), acc(1024, 1024),
        *halves, *eighths, *halves, *eighths,
        buf(512, 1024), acc(2, 128, 1024), buf(2, 128, 1024), buf(256, 512), buf(2, 512, 512),
        *halves, *eighths, buf(256, 1024),
        buf(128, 1024), buf(128, 512), buf(128, 1024), buf(1024, 128), acc(512, 128),
        acc(8, 1024), acc(8, 512), acc(8, 1024), acc(16, 1024), acc(16, 1024), acc(4, 8, 1024),
        acc(2 * planes, 8, 1024), acc(16, 1024),
        sems(3, GROUPS), sems(3, GROUPS), sems(2, PAIRS), sems(2, PAIRS), sems(8), sems(64 + planes),
        sems(64 + planes),
    ]
    rows = jax.ShapeDtypeStruct((256, 1024), BF)
    passed = pl.pallas_call(
        functools.partial(fused_kernel, planes),
        name="block_step",
        out_shape=(rows, rows, jax.ShapeDtypeStruct((16, 1024), F32)),
        in_specs=[hbm, vmem, hbm, hbm, hbm, hbm, vmem, hbm],
        out_specs=(hbm,) * 3,
        scratch_shapes=scratch,
        compiler_params=pltpu.CompilerParams(
            collective_id=1, has_side_effects=True, vmem_limit_bytes=63 << 20
        ),
    )(tokens, norm_params, wqkv, w_out, w_fc, w_proj, factors, grad_out)
    small = jax.ShapeDtypeStruct((4, 4, 1024), F32)
    outs = pl.pallas_call(
        finish_kernel,
        name="finish_step",
        out_shape=(
            rows, jax.ShapeDtypeStruct((256, 1024), F32), small,
            jax.ShapeDtypeStruct((1, 1), F32), small, small, small,
        ),
        in_specs=[vmem] * 3 + [hbm] * 3,
        out_specs=(hbm, hbm) + (vmem,) * 5,
        scratch_shapes=[*quarter, acc(16, 1024), acc(256, 1024), sems(3), sems(2)],
        compiler_params=pltpu.CompilerParams(vmem_limit_bytes=62 << 20),
    )(factors, first, second, *passed)
    return outs[:3] + (outs[3].reshape(()),) + outs[4:]


def solution(mesh):
    placed = (
        P("dp", None),
        P(),
        P(None, None, "tensor"),
        P("tensor", None),
        P(None, "tensor"),
        P("tensor", None),
        P(),
        P(),
        P(),
        P("dp", None),
    )
    planes = mesh.shape["dp"] // 2

    def step(*args):
        rows, width = args[0].shape
        shapes = (rows, width, args[4].shape[1], args[2].shape[2], args[6].shape[1])
        fits = mesh.shape["tensor"] == 4 and mesh.shape["dp"] % 4 == 0
        if fits and shapes == (SEQ, 1024, 1024, 256, 4):
            return fused(planes, *args)
        return body(*args)

    return jax.shard_map(
        step,
        mesh=mesh,
        in_specs=placed,
        out_specs=(P(("dp", "tensor"), None), P(("dp", "tensor"), None), P(), P(), P(), P(), P()),
        check_vma=False,
    )
```

```python
import functools

import jax
import jax.numpy as jnp
from jax import lax
from jax.experimental import pallas as pl
from jax.experimental.pallas import tpu as pltpu
from jax.sharding import PartitionSpec as P

HD = 64
SEQ = 1024
STEP = 5


EPSILON = 1e-05
ADAPTER_SCALING = 8.0
CLIP_NORM = 16.0
LEARN_RATE = 0.03
BETA_ONE = 0.5
BETA_TWO = 0.5
WEIGHT_DECAY = 0.01
ADAM_EPSILON = 1e-08
NEG_LARGE = -1e30
GELU_SCALE = 0.7978845608028654
GELU_CUBE = 0.044715


def matrix_product(left, right):
    return jnp.dot(left, right, preferred_element_type=jnp.float32)


def product_with_transpose(left, right):
    return lax.dot_general(
        left, right, (((1,), (1,)), ((), ())), preferred_element_type=jnp.float32
    )


def transpose_then_product(left, right):
    return lax.dot_general(
        left, right, (((0,), (0,)), ((), ())), preferred_element_type=jnp.float32
    )


def normalize(value_rows_local, gain_vec, bias_vec):
    centered = value_rows_local - jnp.mean(value_rows_local, -1, keepdims=True)
    inverse = lax.rsqrt(jnp.mean(centered * centered, -1, keepdims=True) + EPSILON)
    unit_rows = centered * inverse
    return (unit_rows * gain_vec + bias_vec, unit_rows, inverse)


def normalize_back(incoming, unit_rows, inverse, gain_vec):
    scaled = incoming * gain_vec
    return inverse * (
        scaled
        - jnp.mean(scaled, -1, keepdims=True)
        - unit_rows * jnp.mean(scaled * unit_rows, -1, keepdims=True)
    )


def causal_scores(query_block, key_all, block_index, block_len):
    scores = (
        jnp.einsum("bqhd,bkhd->bhqk", query_block, key_all, preferred_element_type=jnp.float32)
        * 0.125
    )
    query_pos = block_index * block_len + jnp.arange(block_len)
    allowed = jnp.arange(SEQ)[None, :] <= query_pos[:, None]
    return jnp.where(allowed, scores, NEG_LARGE)


def attention_forward(query_rows_local, key_all, value_all):
    block_len = min(512, SEQ)
    outputs = []
    logsums = []
    for block_index in range(SEQ // block_len):
        query_block = query_rows_local[:, block_index * block_len : (block_index + 1) * block_len]
        scores = causal_scores(query_block, key_all, block_index, block_len)
        row_max = jnp.max(scores, -1, keepdims=True)
        exponent = jnp.exp(scores - row_max)
        row_total = jnp.sum(exponent, -1, keepdims=True)
        probability = (exponent / row_total).astype(jnp.bfloat16)
        mixture = jnp.einsum(
            "bhqk,bkhd->bqhd", probability, value_all, preferred_element_type=jnp.float32
        )
        outputs.append(mixture.astype(jnp.bfloat16))
        logsums.append(row_max[..., 0] + jnp.log(row_total[..., 0]))
    return (jnp.concatenate(outputs, 1), jnp.concatenate(logsums, 2))


def attention_backward(query_rows_local, key_all, value_all, grad_mixture, logsums):
    block_len = min(512, SEQ)
    grad_queries = []
    grad_keys = jnp.zeros(key_all.shape, jnp.float32)
    value_gradient_rows = jnp.zeros(value_all.shape, jnp.float32)
    for block_index in range(SEQ // block_len):
        lower = block_index * block_len
        query_block = query_rows_local[:, lower : lower + block_len]
        grad_block = grad_mixture[:, lower : lower + block_len]
        scores = causal_scores(query_block, key_all, block_index, block_len)
        probability = jnp.exp(scores - logsums[:, :, lower : lower + block_len, None])
        grad_prob = jnp.einsum(
            "bqhd,bkhd->bhqk", grad_block, value_all, preferred_element_type=jnp.float32
        )
        row_delta = jnp.sum(grad_prob * probability, -1, keepdims=True)
        dscore = (0.125 * (probability * (grad_prob - row_delta))).astype(jnp.bfloat16)
        grad_queries.append(
            jnp.einsum(
                "bhqk,bkhd->bqhd", dscore, key_all, preferred_element_type=jnp.float32
            ).astype(jnp.bfloat16)
        )
        grad_keys = grad_keys + jnp.einsum(
            "bhqk,bqhd->bkhd", dscore, query_block, preferred_element_type=jnp.float32
        )
        value_gradient_rows = value_gradient_rows + jnp.einsum(
            "bhqk,bqhd->bkhd",
            probability.astype(jnp.bfloat16),
            grad_block,
            preferred_element_type=jnp.float32,
        )
    return (
        jnp.concatenate(grad_queries, 1),
        grad_keys.astype(jnp.bfloat16),
        value_gradient_rows.astype(jnp.bfloat16),
    )


def adam_step(factor_grad, weights, first_old, second_old, grad_norm):
    clipped = factor_grad * (CLIP_NORM / jnp.maximum(grad_norm, CLIP_NORM))
    first_new = BETA_ONE * first_old + (1.0 - BETA_ONE) * clipped
    second_new = BETA_TWO * second_old + (1.0 - BETA_TWO) * clipped * clipped
    first_hat = first_new / (1.0 - BETA_ONE**STEP)
    second_hat = second_new / (1.0 - BETA_TWO**STEP)
    weights_new = weights - LEARN_RATE * (
        first_hat / (jnp.sqrt(second_hat) + ADAM_EPSILON) + WEIGHT_DECAY * weights
    )
    return (clipped, weights_new, first_new, second_new)


def body(
    tokens_in,
    norm_params,
    query_key_value_weight,
    out_weight,
    fc_weight,
    proj_weight,
    factors,
    first_moment,
    second_moment,
    grad_out,
):
    tensor_size = lax.axis_size("tensor")
    tensor_rank = lax.axis_index("tensor")
    token_count = tokens_in.shape[0]
    doc_count = token_count // SEQ
    local_width = query_key_value_weight.shape[2]
    heads_here = local_width // HD
    row_count = token_count // tensor_size
    row_start = tensor_rank * row_count
    rank_count = factors.shape[1]
    full_width = factors.shape[2]
    inputs = tokens_in.astype(jnp.float32)
    first_normalized, unit_one, inverse_one = normalize(inputs, norm_params[0], norm_params[1])
    first_normalized_reduced = first_normalized.astype(jnp.bfloat16)
    factor_reduced_precision = factors.astype(jnp.bfloat16)
    column_offset = tensor_rank * local_width
    query_adapter_output = lax.dynamic_slice_in_dim(
        factor_reduced_precision[1], column_offset, local_width, 1
    )
    value_adapter_output = lax.dynamic_slice_in_dim(
        factor_reduced_precision[3], column_offset, local_width, 1
    )
    query_down_factor = product_with_transpose(
        first_normalized_reduced, factor_reduced_precision[0]
    ).astype(jnp.bfloat16)
    value_down_factor = product_with_transpose(
        first_normalized_reduced, factor_reduced_precision[2]
    ).astype(jnp.bfloat16)
    query_rows_local = (
        matrix_product(first_normalized_reduced, query_key_value_weight[0])
        + ADAPTER_SCALING * matrix_product(query_down_factor, query_adapter_output)
    ).astype(jnp.bfloat16)
    keys_low = matrix_product(first_normalized_reduced, query_key_value_weight[1]).astype(
        jnp.bfloat16
    )
    values_low = (
        matrix_product(first_normalized_reduced, query_key_value_weight[2])
        + ADAPTER_SCALING * matrix_product(value_down_factor, value_adapter_output)
    ).astype(jnp.bfloat16)
    head_shape = (doc_count, SEQ, heads_here, HD)
    query_heads = query_rows_local.reshape(head_shape)
    keys_heads = keys_low.reshape(head_shape)
    values_heads = values_low.reshape(head_shape)
    mixture, logsums = attention_forward(query_heads, keys_heads, values_heads)
    attn_part = matrix_product(mixture.reshape(token_count, local_width), out_weight)
    grad_full = grad_out.astype(jnp.float32)
    attn_rows = lax.psum_scatter(
        attn_part.astype(jnp.bfloat16), "tensor", scatter_dimension=0, tiled=True
    ).astype(jnp.float32)
    resid_rows = lax.dynamic_slice_in_dim(inputs, row_start, row_count, 0) + attn_rows
    normed_two_rows, unit_two, inverse_two = normalize(resid_rows, norm_params[2], norm_params[3])
    normed_two_low = lax.all_gather(
        normed_two_rows.astype(jnp.bfloat16), "tensor", axis=0, tiled=True
    )
    hidden_pre = matrix_product(normed_two_low, fc_weight)
    hidden_act, gelu_pull = jax.vjp(
        lambda argument: jax.nn.gelu(argument, approximate=True), hidden_pre
    )
    mlp_part = matrix_product(hidden_act.astype(jnp.bfloat16), proj_weight)
    grad_hidden = product_with_transpose(grad_out, proj_weight)
    grad_pre = gelu_pull(grad_hidden)[0].astype(jnp.bfloat16)
    second_part = product_with_transpose(grad_pre, fc_weight)
    out_rows = resid_rows + lax.psum_scatter(
        mlp_part.astype(jnp.bfloat16), "tensor", scatter_dimension=0, tiled=True
    ).astype(jnp.float32)
    second_rows = lax.psum_scatter(
        second_part.astype(jnp.bfloat16), "tensor", scatter_dimension=0, tiled=True
    ).astype(jnp.float32)
    resid_grad_rows = lax.dynamic_slice_in_dim(grad_full, row_start, row_count, 0) + normalize_back(
        second_rows, unit_two, inverse_two, norm_params[2]
    )
    resid_grad_low = lax.all_gather(
        resid_grad_rows.astype(jnp.bfloat16), "tensor", axis=0, tiled=True
    )
    grad_mixture = product_with_transpose(resid_grad_low, out_weight).astype(jnp.bfloat16)
    query_gradient, grad_keys, value_gradient_rows = attention_backward(
        query_heads, keys_heads, values_heads, grad_mixture.reshape(head_shape), logsums
    )
    query_gradient = query_gradient.reshape(token_count, local_width)
    grad_keys = grad_keys.reshape(token_count, local_width)
    value_gradient_rows = value_gradient_rows.reshape(token_count, local_width)
    stacked = jnp.stack((query_gradient, grad_keys, value_gradient_rows))
    first_part = jnp.einsum(
        "stc,sdc->td", stacked, query_key_value_weight, preferred_element_type=jnp.float32
    )
    query_up_factor = ADAPTER_SCALING * product_with_transpose(query_gradient, query_adapter_output)
    value_up_factor = ADAPTER_SCALING * product_with_transpose(
        value_gradient_rows, value_adapter_output
    )
    first_part = first_part + jnp.dot(
        query_up_factor,
        factor_reduced_precision[0].astype(jnp.float32),
        precision=lax.Precision.HIGHEST,
    )
    first_part = first_part + jnp.dot(
        value_up_factor,
        factor_reduced_precision[2].astype(jnp.float32),
        precision=lax.Precision.HIGHEST,
    )
    first_rows = lax.psum_scatter(
        first_part.astype(jnp.bfloat16), "tensor", scatter_dimension=0, tiled=True
    ).astype(jnp.float32)
    unit_rows = lax.dynamic_slice_in_dim(unit_one, row_start, row_count, 0)
    inverse_rows = lax.dynamic_slice_in_dim(inverse_one, row_start, row_count, 0)
    input_rows = resid_grad_rows + normalize_back(
        first_rows, unit_rows, inverse_rows, norm_params[0]
    )
    query_cross_term = transpose_then_product(query_gradient, first_normalized_reduced)
    value_cross_term = transpose_then_product(value_gradient_rows, first_normalized_reduced)
    query_down_gradient = ADAPTER_SCALING * jnp.dot(
        query_adapter_output.astype(jnp.float32), query_cross_term, precision=lax.Precision.HIGHEST
    )
    value_down_gradient = ADAPTER_SCALING * jnp.dot(
        value_adapter_output.astype(jnp.float32), value_cross_term, precision=lax.Precision.HIGHEST
    )
    empty_slot = jnp.zeros((rank_count, full_width), jnp.float32)
    up_grad_query = lax.dynamic_update_slice_in_dim(
        empty_slot,
        ADAPTER_SCALING * transpose_then_product(query_down_factor, query_gradient),
        column_offset,
        1,
    )
    up_grad_value = lax.dynamic_update_slice_in_dim(
        empty_slot,
        ADAPTER_SCALING * transpose_then_product(value_down_factor, value_gradient_rows),
        column_offset,
        1,
    )
    partial_grad = jnp.stack(
        (query_down_gradient, up_grad_query, value_down_gradient, up_grad_value)
    )
    reduced = lax.psum(partial_grad, ("dp", "tensor"))
    grad_norm = jnp.sqrt(jnp.sum(reduced * reduced))
    clipped, weights_new, first_new, second_new = adam_step(
        reduced, factors, first_moment, second_moment, grad_norm
    )
    return (
        out_rows.astype(jnp.bfloat16),
        input_rows,
        clipped,
        grad_norm,
        weights_new,
        first_new,
        second_new,
    )


MESH = pl.DeviceIdType.MESH
BF = jnp.bfloat16
F32 = jnp.float32
GROUPS = 8
PAIRS = 8


def mm(left, right):
    return jnp.dot(left, right, preferred_element_type=F32)


def mm_nt(left, right):
    return lax.dot_general(left, right, (((1,), (1,)), ((), ())), preferred_element_type=F32)


def mm_tn(left, right):
    return lax.dot_general(left, right, (((0,), (0,)), ((), ())), preferred_element_type=F32)


def flip(value, bit):
    return value + bit - 2 * bit * ((value // bit) % 2)


def unit_of(rows):
    centered = rows - jnp.mean(rows, -1, keepdims=True)
    inverse = lax.rsqrt(jnp.mean(centered * centered, -1, keepdims=True) + EPSILON)
    return centered * inverse, inverse


def unit_back(scaled, unit, inverse):
    return inverse * (
        scaled - jnp.mean(scaled, -1, keepdims=True) - unit * jnp.mean(scaled * unit, -1, keepdims=True)
    )


def fused_kernel(
    planes,
    tokens, norm_params, wqkv, w_out, w_fc, w_proj, factors, grad_out,
    bo_r, ig_r, summed,
    tok, n1, go, wq, wkv, wo, fcw, pw, kv, qs, p0, p1, mix, inv, attn_own, attn_s, attn_r,
    res, n2, acc_a, acc_b, gnt_s, gnt_r, gnt_xs, gnt_xr, mlp_s, mlp_r, mlp_xs, mlp_xr,
    gr_b, bo_f, bo_s, gq, dos, gno_s, gno_r, gno_xs, gno_xr, ig_s,
    f02, f1p, f3kv, down, gd_scr, fg_a, fg_q, fg_v, ps, ps_r, plane_buf, z_buf, fin,
    chain_send, chain_recv, pair_send, pair_recv, load_sem, ssem, rsem,
):
    d = lax.axis_index("dp")
    t = lax.axis_index("tensor")
    z, c, x, y = d // 2, d % 2, t % 2, t // 2
    odd = z % 2
    nbr = (flip(d, 1), t)
    prim = (d, flip(t, 1 + odd))
    sec = (d, flip(t, 2 - odd))
    plane = [(d, flip(t, 1)), (d, flip(t, 2)), (d, 3 - t)]
    x_nbr, y_nbr = plane[0], plane[1]
    zs = [(flip(d, 2 << k), t) for k in range(planes.bit_length() - 1)]
    owners = [(2 * z + y, 2 * h + x) for h in range(2)]
    at_home = [jnp.logical_and(c == y, h == y) for h in range(2)]
    quarter = [t, flip(t, 1 + odd), flip(t, 2 - odd), 3 - t]
    column = [pl.multiple_of(q * 256 + c * 128, 128) for q in quarter]

    def at(start, size):
        return pl.ds(pl.multiple_of(start, size), size)

    def rows_of(half, side):
        return at(512 * half + 256 * side, 256)

    def own_rows(h, side):
        return at(512 * h + 256 * side + 128 * c, 128)

    def other_rows(h, side):
        return at(512 * h + 256 * side + 128 * (1 - c), 128)

    def ff_own(h, side):
        return at(512 * side + 256 * h + 128 * c, 128)

    def ff_other(h, side):
        return at(512 * side + 256 * h + 128 * (1 - c), 128)

    def remote_to(src, dst, out_index, in_index, device):
        return pltpu.make_async_remote_copy(
            src_ref=src, dst_ref=dst, send_sem=ssem.at[out_index], recv_sem=rsem.at[in_index],
            device_id=device, device_id_type=MESH,
        )

    def remote(src, dst, index, device):
        return remote_to(src, dst, index, index, device)

    pending = []

    def drain():
        for wait in pending:
            wait()

    def send(copy):
        copy.start()
        pending.append(copy.wait_send)
        return copy

    lane = at(c * 128, 128)
    loads = [
        pltpu.make_async_copy(wqkv.at[1, :, lane], wkv.at[:, pl.ds(0, 128)], load_sem.at[0]),
        pltpu.make_async_copy(wqkv.at[2, :, lane], wkv.at[:, pl.ds(128, 128)], load_sem.at[1]),
        pltpu.make_async_copy(wqkv.at[0, :, lane], wq.at[:, pl.ds(0, 128)], load_sem.at[2]),
        pltpu.make_async_copy(w_out.at[lane, :], wo.at[pl.ds(0, 128), :], load_sem.at[3]),
        pltpu.make_async_copy(w_fc.at[:, at(c * 512, 512)], fcw.at[0], load_sem.at[4]),
        pltpu.make_async_copy(w_proj.at[at(c * 512, 512), :], pw.at[0], load_sem.at[5]),
    ]
    for load in loads:
        load.start()

    barrier = pltpu.get_barrier_semaphore()
    partners = [nbr, x_nbr, y_nbr] + zs
    for device in partners:
        pl.semaphore_signal(barrier, inc=1, device_id=device, device_id_type=MESH)
    fpad = acc_b.at[0:128, :]
    fpad[...] = jnp.zeros(fpad.shape, F32)
    fpad[0:4, :] = factors[0]
    fpad[4:8, :] = factors[2]
    f02[...] = fpad[...].astype(BF)
    fpad[...] = jnp.zeros(fpad.shape, F32)
    for s in range(4):
        fpad[0:4, 128 * s : 128 * s + 128] = factors[1, :, pl.ds(column[s], 128)]
    f1p[...] = fpad[:, :512].astype(BF)
    fpad[...] = jnp.zeros(fpad.shape, F32)
    for s in range(4):
        fpad[4:8, 256 * s + 128 : 256 * s + 256] = factors[3, :, pl.ds(column[s], 128)]
    f3kv[...] = fpad[...].astype(BF)
    ps[...] = jnp.zeros_like(ps)
    acc_a[...] = jnp.zeros_like(acc_a)
    acc_b[...] = jnp.zeros_like(acc_b)
    pl.semaphore_wait(barrier, len(partners))

    doc = []
    for r in range(4):
        part = pl.ds(256 * r, 256)
        doc.append((tokens.at[part, :], tok.at[part, :], r))
    place = jnp.where(c == y, 0, 512)
    grads = [
        (grad_out.at[rows_of(h, x), :], go.at[at(place + 256 * h, 256), :], 4 + h) for h in range(2)
    ]
    other_place = 512 - place
    grads_in = [
        (grad_out.at[rows_of(h, x), :], go.at[at(other_place + 256 * h, 256), :], 4 + h) for h in range(2)
    ]
    for h in range(2):
        pltpu.make_async_copy(*grads[h][:2], load_sem.at[6 + h]).start()

    @pl.when(c == y)
    def _():
        for src, dst, index in doc:
            remote(src, dst, index, nbr).start()
            pltpu.make_async_copy(src, dst, rsem.at[index]).start()

    def doc_sent():
        @pl.when(c == y)
        def _():
            for item in doc:
                remote(*item, nbr).wait_send()

    pending.append(doc_sent)
    for item in grads:
        send(remote(*item, nbr))

    def doc_wait(index):
        remote(*doc[index], nbr).wait_recv()

    def piece(slot, group):
        matrix, a = group // 2, group % 2
        if matrix < 2:
            return wkv.at[pl.ds(512 * a, 512), pl.ds(256 * slot + 128 * matrix, 128)]
        if matrix == 2:
            return wq.at[pl.ds(512 * a, 512), pl.ds(128 * slot, 128)]
        return wo.at[pl.ds(128 * slot + 64 * a, 64), :]

    def hop(slot, group):
        return pltpu.make_async_remote_copy(
            src_ref=piece(1 if slot > 1 else 0, group), dst_ref=piece(slot, group),
            send_sem=chain_send.at[slot - 1, group], recv_sem=chain_recv.at[slot - 1, group],
            device_id=(prim, zs[0], sec)[slot - 1], device_id_type=MESH,
        )

    def pump(group, later=True):
        hop(1, group).wait_recv()
        for slot in (2, 3):
            hop(slot, group).start()
            if later:
                pending.append(hop(slot, group).wait_send)

    def passed(groups):
        for group in groups:
            hop(2, group).wait_recv()
            hop(3, group).wait_recv()

    def pair_piece(slot, pair, parity):
        h, q = pair // 4, pair % 4
        if q < 2:
            return fcw.at[slot, at(512 * q + 256 * parity, 256), pl.ds(256 * h, 256)]
        return pw.at[slot, at(256 * h + 128 * (q - 2) + 64 * parity, 64), :]

    def pair_hop(step, pair, parity):
        return pltpu.make_async_remote_copy(
            src_ref=pair_piece(step, pair, parity), dst_ref=pair_piece(1, pair, parity),
            send_sem=pair_send.at[step, pair], recv_sem=pair_recv.at[step, pair],
            device_id=(x_nbr, zs[0])[step], device_id_type=MESH,
        )

    def pair_pump(pair):
        pair_hop(0, pair, odd).wait_recv()
        pair_hop(1, pair, odd).start()

    def pair_wait(pairs):
        for pair in pairs:
            pair_hop(1, pair, 1 - odd).wait_recv()

    for matrix in range(4):
        loads[matrix].wait()
        send(hop(1, 2 * matrix))
        send(hop(1, 2 * matrix + 1))
    loads[4].wait()
    loads[5].wait()
    for pair in range(2):
        pair_hop(0, pair, odd).start()

    gain_one, bias_one = norm_params[0:1, :], norm_params[1:2, :]
    gain_two, bias_two = norm_params[2:3, :], norm_params[3:4, :]
    def first_norm(r):
        doc_wait(r)

        @pl.loop(0, 2)
        def _(q):
            rows = at(256 * r + 128 * q, 128)
            unit, _ = unit_of(tok[rows, :].astype(F32))
            n1[rows, :] = (unit * gain_one + bias_one).astype(BF)

    first_norm(0)
    first_norm(1)
    pump(0)
    first_norm(2)
    first_norm(3)

    @pl.loop(0, 2)
    def _(r):
        rows = at(512 * r, 512)
        down[rows, :] = mm_nt(n1[rows, :], f02[...]).astype(BF)

    pump(1)
    first_head = lax.broadcasted_iota(jnp.int32, (256, 512), 1) % 128 < 64
    first_lanes = first_head[:, 0:128]

    def stacked(rows, lanes):
        return jnp.concatenate((jnp.where(lanes, rows, 0.0), jnp.where(lanes, 0.0, rows)), 0)

    p_refs = (p0, p1)
    column_pos = lax.broadcasted_iota(jnp.int32, (512, 512), 1)
    row_pos = lax.broadcasted_iota(jnp.int32, (512, 512), 0) % 256 + 256 * x
    allowed = column_pos <= row_pos

    @pl.loop(0, 4)
    def _(s):
        @pl.when(s == 1)
        def _():
            for group in range(2, 6):
                pump(group, False)

        @pl.when(s == 2)
        def _():
            pump(6, False)
            passed(range(0, 6))

        @pl.when(s == 3)
        def _():
            pump(7, False)
            for pair in range(2, PAIRS):
                pair_hop(0, pair, odd).start()

        both_lanes, lanes = at(256 * s, 256), at(128 * s, 128)
        keys, values = at(256 * s, 128), at(256 * s + 128, 128)

        @pl.loop(0, 2)
        def _(r):
            rows = at(512 * r, 512)
            kv[rows, both_lanes] = (
                mm(n1[rows, :], wkv[:, both_lanes]) + ADAPTER_SCALING * mm(down[rows, :], f3kv[:, both_lanes])
            ).astype(BF)

        for h in range(2):
            rows = rows_of(h, x)
            query = mm(n1[rows, :], wq[:, lanes]) + ADAPTER_SCALING * mm(down[rows, :], f1p[:, lanes])
            qs[h, :, lanes] = stacked(query.astype(BF).astype(F32) * 0.125, first_lanes).astype(BF)
        scores = [mm_nt(qs[h, :, lanes], kv[0 : 512 * (h + 1), keys]) for h in range(2)]
        kept = []
        for h in range(2):
            last = jnp.where(allowed, scores[h][:, 512 * h :], NEG_LARGE)
            block = jnp.concatenate((scores[h][:, :512], last), 1) if h else last
            exponent = jnp.exp(block - jnp.max(block, -1, keepdims=True))
            inverse = 1.0 / jnp.sum(exponent, -1, keepdims=True)
            p_refs[h][s] = exponent.astype(BF)
            inv[h, :, lanes] = jnp.broadcast_to(inverse, (512, 128))
            kept.append((exponent.astype(BF), inverse))
        for h in range(2):
            both = mm(kept[h][0], kv[0 : 512 * (h + 1), values]) * kept[h][1]
            mix[256 * h : 256 * h + 256, lanes] = jnp.where(first_lanes, both[0:256], both[256:512])

    for group in range(2, GROUPS):
        pending.append(hop(2, group).wait_send)
        pending.append(hop(3, group).wait_send)
    for pair in range(PAIRS):
        pending.append(pair_hop(0, pair, odd).wait_send)
    pair_pump(0)
    passed(range(6, 8))

    def heads_out(sub):
        rows = [mix[at(256 * h + 128 * sub, 128), :].astype(BF) for h in range(2)]
        return mm(jnp.concatenate(rows, 0), wo[...])

    attn_s[...] = heads_out(1 - c).astype(BF)
    to_nbr = send(remote(attn_s, attn_r, 8, nbr))
    pair_pump(1)
    attn_own[...] = heads_out(c)
    pair_pump(2)
    to_nbr.wait_recv()

    gathered = []
    for h in range(2):
        part = slice(128 * h, 128 * h + 128)
        rows = own_rows(h, x)
        residual = tok[rows, :].astype(F32) + attn_own[part, :] + attn_r[part, :].astype(F32)
        res[part, :] = residual
        unit, _ = unit_of(residual)
        rows = ff_own(h, 0)
        n2[rows, :] = (unit * gain_two + bias_two).astype(BF)
        gathered.append(send(remote(n2.at[rows, :], n2.at[ff_own(h, 1), :], 11 + h, y_nbr)))
        gathered.append(send(remote(n2.at[rows, :], n2.at[rows, :], 9 + h, nbr)))
    pair_pump(3)
    for h in range(2):
        pltpu.make_async_copy(*grads[h][:2], load_sem.at[6 + h]).wait()
        remote(*grads_in[h], nbr).wait_recv()
    gathered[1].wait_recv()
    gathered[3].wait_recv()

    def pass_on(h):
        gathered[2 * h].wait_recv()
        rows = ff_own(h, 1)
        remote(n2.at[rows, :], n2.at[rows, :], 13 + h, nbr).start()

    def passed_on(h):
        rows = ff_own(h, 1)
        return remote(n2.at[rows, :], n2.at[rows, :], 13 + h, nbr)

    def sum_copy(source, target, first, h, j):
        part = pl.ds(128 * j, 128)
        return remote(source.at[h, part, :], target.at[h, part, :], first + 2 * h + j, nbr)

    def to_core(acc, source, target, first, h):
        for j, side in enumerate((1, 0)):
            source[h, 128 * j : 128 * j + 128, :] = acc[ff_other(h, side), :].astype(BF)
            sum_copy(source, target, first, h, j).start()

    def to_side(acc, source, target, out, out_target, first, side_first, h):
        sum_copy(source, target, first, h, 0).wait_recv()
        out[h] = (acc[ff_own(h, 1), :] + target[h, 0:128, :].astype(F32)).astype(BF)
        return send(remote(out.at[h], out_target.at[h], side_first + h, y_nbr))

    @pl.loop(0, 8)
    def _(unit):
        @pl.when(unit == 1)
        def _():
            pair_pump(4)

        @pl.when(unit == 2)
        def _():
            pair_wait(range(0, 4))
            pair_pump(5)

        @pl.when(unit == 3)
        def _():
            pass_on(0)
            pair_pump(6)
            passed_on(0).wait_recv()

        @pl.when(unit == 4)
        def _():
            pair_pump(7)
            pass_on(1)
            passed_on(1).wait_recv()

        @pl.when(unit == 6)
        def _():
            pair_wait(range(4, 8))

        @pl.when(unit == 7)
        def _():
            to_core(acc_b, gnt_s, gnt_r, 40, 1)

        flag = lambda value: jnp.where(value, 1, 0)
        single = jnp.logical_or(unit == 3, unit == 4)
        slot = flag(jnp.logical_or(unit == 2, unit >= 5))
        tiles, lanes = [], []
        for k in range(2):
            half = jnp.where(single, unit - 3, jnp.where(unit >= 6, 7 - unit, k))
            side = jnp.where(unit >= 6, 1 - k, flag(unit >= 3))
            part = jnp.where(single, k, flag(jnp.logical_or(unit >= 6, unit == 1)))
            tiles.append(at(512 * side + 256 * half, 256))
            lanes.append(at(256 * part, 256))
        pre = [mm(n2[rows, :], fcw[slot, :, lane]) for rows, lane in zip(tiles, lanes)]
        grad_act = [mm_nt(go[rows, :], pw[slot, lane, :]) for rows, lane in zip(tiles, lanes)]
        for rows, lane, hidden, grad in zip(tiles, lanes, pre, grad_act):
            square = hidden * hidden
            tanh = jnp.tanh(GELU_SCALE * hidden * (1.0 + GELU_CUBE * square))
            half_up = 0.5 * (1.0 + tanh)
            slope = half_up + (0.5 * GELU_SCALE) * hidden * (1.0 - tanh * tanh) * (
                1.0 + 3.0 * GELU_CUBE * square
            )
            acc_b[rows, :] += mm_nt((grad * slope).astype(BF), fcw[slot, :, lane])
            acc_a[rows, :] += mm((hidden * half_up).astype(BF), pw[slot, lane, :])

    for pair in range(PAIRS):
        pending.append(pair_hop(1, pair, odd).wait_send)
    for h in range(2):
        pending.append(passed_on(h).wait_send)
        for j in range(2):
            pending.append(sum_copy(gnt_s, gnt_r, 40, h, j).wait_send)
            pending.append(sum_copy(mlp_s, mlp_r, 44, h, j).wait_send)

    gnt_side = [None, None]
    gnt_side[1] = to_side(acc_b, gnt_s, gnt_r, gnt_xs, gnt_xr, 40, 17, 1)
    to_core(acc_b, gnt_s, gnt_r, 40, 0)
    gnt_side[0] = to_side(acc_b, gnt_s, gnt_r, gnt_xs, gnt_xr, 40, 17, 0)
    for h in (1, 0):
        to_core(acc_a, mlp_s, mlp_r, 44, h)
    near, far = y, 1 - y
    for h in (1, 0):
        for j in range(2):
            sum_copy(mlp_s, mlp_r, 44, h, j).wait_recv()

    def chip_sum(h, side):
        return acc_a[ff_own(h, side), :] + mlp_r[h, 128 * (1 - side) : 128 * (1 - side) + 128, :].astype(F32)

    mlp_xs[0] = chip_sum(far, 1).astype(BF)
    mlp_xs[1] = (res[at(128 * far, 128), :] + chip_sum(far, 0)).astype(BF)
    mlp_side = [send(remote(mlp_xs.at[k], mlp_xr.at[k], 21 + k, y_nbr)) for k in range(2)]
    bo_f[0] = res[at(128 * near, 128), :] + chip_sum(near, 0)
    bo_f[1] = chip_sum(near, 1)

    gr = attn_own

    def residual_back(h):
        part = slice(128 * h, 128 * h + 128)
        unit, inverse = unit_of(res[part, :])
        sum_copy(gnt_s, gnt_r, 40, h, 1).wait_recv()
        total = acc_b[ff_own(h, 0), :] + gnt_r[h, 128:256, :].astype(F32)
        gnt_side[h].wait_recv()
        scaled = (total + gnt_xr[h].astype(F32)) * gain_two
        grad = go[ff_own(h, 0), :].astype(F32) + unit_back(scaled, unit, inverse)
        gr[part, :] = grad
        local = at(256 * h + 128 * c, 128)
        gr_b[local, :] = grad.astype(BF)
        return send(remote(gr_b.at[local, :], gr_b.at[local, :], 23 + h, nbr))

    def mixture_back(h):
        grad_mixture = mm_nt(gr_b[256 * h : 256 * h + 256, :], wo[...])
        dos[h] = (stacked(grad_mixture, first_head) * inv[h]).astype(BF)

    to_nbr = residual_back(1)
    to_nbr.wait_recv()
    mixture_back(1)

    def scores_back(h, first, count):
        size = 512 * (h + 1)
        group = [first + k for k in range(count)]
        lanes = [at(128 * s, 128) for s in group]
        k_lanes = [at(256 * s, 128) for s in group]
        v_lanes = [at(256 * s + 128, 128) for s in group]
        grads = [dos[h, :, lane] for lane in lanes]
        grad_prob = [mm_nt(grad, kv[0:size, lane]) for lane, grad in zip(v_lanes, grads)]
        dscores = []
        for s, lane, grad, block in zip(group, lanes, grads, grad_prob):
            mixture = mix[256 * h : 256 * h + 256, lane]
            delta = jnp.sum(
                grad.astype(F32) * jnp.concatenate((mixture, mixture), 0), -1, keepdims=True
            )
            dscores.append((p_refs[h][s].astype(F32) * (block - delta)).astype(BF))
        for k, (s, lane, grad, dscore) in enumerate(zip(group, lanes, grads, dscores)):
            both = 0.125 * mm(dscore, kv[0:size, k_lanes[k]])
            gq[:, lane] = jnp.where(first_lanes, both[0:256], both[256:512]).astype(BF)
            grad_keys = mm_tn(dscore, qs[h, :, lane])
            grad_values = mm_tn(p_refs[h][s], grad)
            if h:
                acc_a[:, k_lanes[k]] = grad_keys
                acc_a[:, v_lanes[k]] = grad_values
            else:
                acc_a[0:512, k_lanes[k]] += grad_keys
                acc_a[0:512, v_lanes[k]] += grad_values

    def factors_back(h):
        rows = slice(512 * h, 512 * h + 512)
        grads = acc_a[rows, :].astype(BF)
        query = gq[...]
        gd_scr[...] = ADAPTER_SCALING * mm_nt(grads, f3kv[...])
        gd_scr[at(256 * x, 256), :] += ADAPTER_SCALING * mm_nt(query, f1p[...])
        terms = (
            mm_tn(gd_scr[...].astype(BF), n1[rows, :])[0:8],
            mm_tn(down[rows_of(h, x), :], query)[0:8],
            mm_tn(down[rows, :], grads)[0:8],
        )
        for total, term in zip((fg_a, fg_q, fg_v), terms):
            total[...] = term if h else total[...] + term

    def rows_copy(h, j):
        part = pl.ds(128 * j, 128)
        return remote(gno_s.at[h, part, :], gno_r.at[h, part, :], 27 + 2 * h + j, nbr)

    def rows_back(h, j):
        side = x if j else 1 - x
        rows = rows_of(h, side)
        grad = mm_nt(acc_a[rows, :].astype(BF), wkv[...])
        grad += mm(gd_scr[at(256 * side, 256), :].astype(BF), f02[...])
        if j:
            grad += mm_nt(gq[...], wq[...])
        acc_b[rows, :] = grad
        gno_s[h, 128 * j : 128 * j + 128, :] = acc_b[other_rows(h, side), :].astype(BF)
        send(rows_copy(h, j))

    side_copies = {}

    def reduce_rows(h):
        rows_copy(h, 0).wait_recv()
        gno_xs[h] = (acc_b[own_rows(h, 1 - x), :] + gno_r[h, 0:128, :].astype(F32)).astype(BF)
        for k in range(2):
            part = pl.ds(64 * k, 64)
            side_copies[h, k] = send(
                remote(gno_xs.at[h, part, :], gno_xr.at[h, part, :], 48 + 2 * h + k, x_nbr)
            )

    def to_owner(src, dst, h, out_index, in_index):
        @pl.when(at_home[h])
        def _():
            pltpu.make_async_copy(src, dst, rsem.at[in_index + c]).start()

        @pl.when(jnp.logical_not(at_home[h]))
        def _():
            remote_to(src, dst, out_index, in_index + c, owners[h]).start()

        def sent():
            @pl.when(jnp.logical_not(at_home[h]))
            def _():
                remote_to(src, dst, out_index, in_index + c, owners[h]).wait_send()

        pending.append(sent)

    def input_rows(h, k):
        if k == 0:
            rows_copy(h, 1).wait_recv()
        start = 512 * h + 256 * x + 128 * c + 64 * k
        rows, part = at(start, 64), slice(64 * k, 64 * k + 64)
        unit, inverse = unit_of(tok[rows, :].astype(F32))
        total = acc_b[rows, :] + gno_r[h, 128 + 64 * k : 192 + 64 * k, :].astype(F32)
        side_copies[h, k].wait_recv()
        scaled = (total + gno_xr[h, part, :].astype(F32)) * gain_one
        out = slice(128 * h + 64 * k, 128 * h + 64 * k + 64)
        ig_s[out, :] = (gr[out, :] + unit_back(scaled, unit, inverse)).astype(BF)
        to_owner(ig_s.at[out, :], ig_r.at[at(128 * c + 64 * k, 64), :], h, 52 + 2 * h + k, 56 + 2 * k)

    scores_back(1, 0, 2)
    scores_back(1, 2, 2)

    to_nbr = residual_back(0)
    factors_back(1)
    rows_back(1, 0)
    rows_back(1, 1)
    to_nbr.wait_recv()
    mixture_back(0)
    reduce_rows(1)
    scores_back(0, 0, 4)

    factors_back(0)

    ps[0:8, :] = fg_a[...]
    down_rows = lax.broadcasted_iota(jnp.int32, (8, 128), 0) < 4
    for s in range(4):
        ps[8:16, pl.ds(column[s], 128)] = ADAPTER_SCALING * jnp.where(
            down_rows, fg_q[:, 128 * s : 128 * s + 128], fg_v[:, 256 * s + 128 : 256 * s + 256]
        )
    core_sum = send(remote(ps, ps_r, 33, nbr))
    rows_back(0, 0)
    core_sum.wait_recv()
    eight = at(8 * c, 8)
    plane_buf[t] = ps[eight, :] + ps_r[eight, :]
    copies = [
        send(remote(plane_buf.at[t], plane_buf.at[t], 35 + k, device)) for k, device in enumerate(plane)
    ]
    reduce_rows(0)
    for k in range(2):
        mlp_side[k].wait_recv()
        bo_s[k] = (bo_f[k] + mlp_xr[k].astype(F32)).astype(BF)
    kept = jnp.where(c == y, 0, 1)
    home = pl.ds(pl.multiple_of(128 * c, 128), 128)
    bo_home = pltpu.make_async_copy(bo_s.at[kept], bo_r.at[home, :], load_sem.at[1])
    bo_home.start()
    bo_away = send(remote(bo_s.at[1 - kept], bo_r.at[home, :], 60, nbr))
    rows_back(0, 1)
    for copy in copies:
        copy.wait_recv()
    z_buf[0] = plane_buf[0] + plane_buf[1] + plane_buf[2] + plane_buf[3]

    def z_copy(k):
        return remote(z_buf.at[2 * k], z_buf.at[2 * k + 1], 64 + k, zs[k])

    for k in range(len(zs)):
        send(z_copy(k))
        if k == 0:
            input_rows(1, 0)
            input_rows(1, 1)
        if k < 2:
            input_rows(0, k)
        z_copy(k).wait_recv()
        z_buf[2 * k + 2] = z_buf[2 * k] + z_buf[2 * k + 1]
    for k in range(len(zs), 2):
        input_rows(0, k)
    fin[eight, :] = z_buf[2 * len(zs)]
    send(remote(fin.at[eight, :], fin.at[eight, :], 34, nbr))
    theirs = at(8 - 8 * c, 8)
    remote(fin.at[theirs, :], fin.at[theirs, :], 34, nbr).wait_recv()
    result = pltpu.make_async_copy(fin, summed, load_sem.at[0])
    result.start()

    bo_home.wait()
    bo_away.wait_recv()
    for core in range(2):
        for k in range(2):
            part = pl.ds(128 * core + 64 * k, 64)
            remote_to(ig_s.at[pl.ds(0, 64), :], ig_r.at[part, :], 52, 56 + 2 * k + core, nbr).wait_recv()
    result.wait()
    drain()


def finish_kernel(
    factors, first_moment, second_moment, bo_in, ig_in, sum_in,
    block_out, input_grad, clipped, grad_norm, factors_new, first_new, second_new,
    bo, ig, summed, grads, sem, out_sem,
):
    pairs = [(sum_in, summed), (bo_in, bo), (ig_in, ig)]
    loads = [pltpu.make_async_copy(*pair, sem.at[k]) for k, pair in enumerate(pairs)]
    for load in loads:
        load.start()
    loads[0].wait()
    grad = summed[...]
    norm = jnp.sqrt(jnp.sum(grad * grad, (0, 1), keepdims=True))
    grad_norm[...] = norm
    grad = grad * (CLIP_NORM / jnp.maximum(norm, CLIP_NORM))
    for index, first in enumerate((0, 8, 4, 12)):
        value, weights = grad[first : first + 4], factors[index]
        first_value = BETA_ONE * first_moment[index] + (1.0 - BETA_ONE) * value
        second_value = BETA_TWO * second_moment[index] + (1.0 - BETA_TWO) * value * value
        first_hat = first_value / (1.0 - BETA_ONE**STEP)
        second_hat = second_value / (1.0 - BETA_TWO**STEP)
        clipped[index] = value
        first_new[index] = first_value
        second_new[index] = second_value
        factors_new[index] = weights - LEARN_RATE * (
            first_hat / (jnp.sqrt(second_hat) + ADAM_EPSILON) + WEIGHT_DECAY * weights
        )
    loads[1].wait()
    stores = [pltpu.make_async_copy(bo, block_out, out_sem.at[0])]
    stores[0].start()
    loads[2].wait()
    grads[...] = ig[...].astype(F32)
    stores.append(pltpu.make_async_copy(grads, input_grad, out_sem.at[1]))
    stores[1].start()
    for store in stores:
        store.wait()


def fused(planes, tokens, norm_params, wqkv, w_out, w_fc, w_proj, factors, first, second, grad_out):
    vmem = pl.BlockSpec(memory_space=pltpu.VMEM)
    hbm = pl.BlockSpec(memory_space=pl.ANY)

    def buf(*shape):
        return pltpu.VMEM(shape, BF)

    def acc(*shape):
        return pltpu.VMEM(shape, F32)

    def sems(*shape):
        return pltpu.SemaphoreType.DMA(shape)

    quarter = [buf(256, 1024)] * 2
    halves, eighths = [buf(2, 256, 1024)] * 2, [buf(2, 128, 1024)] * 2
    scratch = [
        buf(1024, 1024), buf(1024, 1024), buf(1024, 1024), buf(1024, 512), buf(1024, 1024), buf(512, 1024),
        buf(2, 1024, 512), buf(2, 512, 1024), buf(1024, 1024), buf(2, 512, 512), buf(4, 512, 512),
        buf(4, 512, 1024), acc(512, 512), acc(2, 512, 512), acc(256, 1024), *quarter,
        acc(256, 1024), buf(1024, 1024), acc(1024, 1024), acc(1024, 1024),
        *halves, *eighths, *halves, *eighths,
        buf(512, 1024), acc(2, 128, 1024), buf(2, 128, 1024), buf(256, 512), buf(2, 512, 512),
        *halves, *eighths, buf(256, 1024),
        buf(128, 1024), buf(128, 512), buf(128, 1024), buf(1024, 128), acc(512, 128),
        acc(8, 1024), acc(8, 512), acc(8, 1024), acc(16, 1024), acc(16, 1024), acc(4, 8, 1024),
        acc(2 * planes, 8, 1024), acc(16, 1024),
        sems(3, GROUPS), sems(3, GROUPS), sems(2, PAIRS), sems(2, PAIRS), sems(8), sems(64 + planes),
        sems(64 + planes),
    ]
    rows = jax.ShapeDtypeStruct((256, 1024), BF)
    passed = pl.pallas_call(
        functools.partial(fused_kernel, planes),
        name="block_step",
        out_shape=(rows, rows, jax.ShapeDtypeStruct((16, 1024), F32)),
        in_specs=[hbm, vmem, hbm, hbm, hbm, hbm, vmem, hbm],
        out_specs=(hbm,) * 3,
        scratch_shapes=scratch,
        compiler_params=pltpu.CompilerParams(
            collective_id=1, has_side_effects=True, vmem_limit_bytes=63 << 20
        ),
    )(tokens, norm_params, wqkv, w_out, w_fc, w_proj, factors, grad_out)
    small = jax.ShapeDtypeStruct((4, 4, 1024), F32)
    outs = pl.pallas_call(
        finish_kernel,
        name="finish_step",
        out_shape=(
            rows, jax.ShapeDtypeStruct((256, 1024), F32), small,
            jax.ShapeDtypeStruct((1, 1), F32), small, small, small,
        ),
        in_specs=[vmem] * 3 + [hbm] * 3,
        out_specs=(hbm, hbm) + (vmem,) * 5,
        scratch_shapes=[*quarter, acc(16, 1024), acc(256, 1024), sems(3), sems(2)],
        compiler_params=pltpu.CompilerParams(vmem_limit_bytes=62 << 20),
    )(factors, first, second, *passed)
    return outs[:3] + (outs[3].reshape(()),) + outs[4:]


def solution(mesh):
    placed = (
        P("dp", None),
        P(),
        P(None, None, "tensor"),
        P("tensor", None),
        P(None, "tensor"),
        P("tensor", None),
        P(),
        P(),
        P(),
        P("dp", None),
    )
    planes = mesh.shape["dp"] // 2

    def step(*args):
        rows, width = args[0].shape
        shapes = (rows, width, args[4].shape[1], args[2].shape[2], args[6].shape[1])
        fits = mesh.shape["tensor"] == 4 and mesh.shape["dp"] % 4 == 0
        if fits and shapes == (SEQ, 1024, 1024, 256, 4):
            return fused(planes, *args)
        return body(*args)

    return jax.shard_map(
        step,
        mesh=mesh,
        in_specs=placed,
        out_specs=(P(("dp", "tensor"), None), P(("dp", "tensor"), None), P(), P(), P(), P(), P()),
        check_vma=False,
    )
```
